32 devices in a mesh: parts: 2 (over x), expert: 16 (over z, y, core).
Axes of the slice: x: 2, y: 2, z: 4, core: 2. Of those that a mesh axis runs over, the one named last changes fastest.
Arguments:
- activations: bfloat16 [768, 6144], P(('parts', 'expert')), parts along dimension 0, may hold values from -6 to 6
- expert_ids: int32 [768, 2], P(('parts', 'expert')), parts along dimension 0, may hold values from 0 to 3, all different within a row; in each aligned block of 24 rows (0 to 23, 24 to 47, ...) at most 16 rows name the same one
- route_logits: float32 [768, 2], P(('parts', 'expert')), parts along dimension 0, may hold values from -6 to 6
- norm_gain: float32 [6144], replicated, may hold values from 0.25 to 1.75
- w_gate: bfloat16 [18432, 6144], P('expert'), may hold values from -0.078125 to 0.078125
- w_up: bfloat16 [18432, 6144], P('expert'), may hold values from -0.078125 to 0.078125
- w_down: bfloat16 [18432, 6144], P('expert'), may hold values from -0.09375 to 0.09375
Outputs:
- mixed: bfloat16 [768, 6144], P(('parts', 'expert')), parts along dimension 0
The draws below stay inside these ranges and needn't reach their ends.
There are 2 independent parts, one for each index of `parts`. The reference program is written for one: setup_inputs(seed, part) draws one part's arguments, and reference() takes and returns one part's arrays. A program takes and returns all parts, laid end to end along the dimension named above; an argument that names none is the same for every part. Nothing has to cross between parts.
Inputs may be any that keep to these rules, and one draw needn't show every extreme that they name: `expert_ids`: each row names two different experts; among the rows of one device no expert is named more than 16 times, a bound that some block reaches.
All inputs are finite; a program needn't handle non-finite values.
Results may differ from the reference program's by a relative error of at most 0.0054.
Values may be sent and summed in bfloat16 or wider, within the bound.
No kernel may reach another device: no remote copies, remote signals or barrier semaphores. Data moves between devices by JAX's collectives and lax.ppermute only.
A program may use at most 128 MiB of HBM per device.

```python
import math
import jax
import jax.numpy as jnp
import numpy as np
from jax import lax

D = 6144
FF_EXP = 4608
EXPERTS = 4
TOK_DEV = 24
GROUP = 4
FF_DEV = 1152
CAP = 16
TOKENS = 384
N_EXPERT = 16


def steps_of(key, shape, cuts, smallest, largest):
    gain = 1.0
    for position, parts in cuts:
        steps = jax.random.uniform(jax.random.fold_in(jax.random.fold_in(key, 6), position), (parts,), jnp.float32, smallest / len(cuts), largest / len(cuts))
        gain = gain * jnp.repeat(jnp.exp(steps), shape[position] // parts).reshape((-1,) + (1,) * (len(shape) - 1 - position))
    return gain


def assign_block(key, own, number, rows, number_of, top, reach, lean):
    order = jax.random.permutation(key, number_of)
    packed, ordinary = portions_of(number_of, rows * top, reach, lean, True), portions_of(number_of, rows * top, reach, lean, False)
    places = jnp.arange(number_of)

    def named(lengths, offset_by):
        used = int((lengths > 0).sum())
        fixed = max(1, used // 4)
        moved = fixed + (places - fixed + offset_by * (used - fixed)) % max(1, number_of - fixed)
        return jnp.zeros((number_of,), jnp.int32).at[order[jnp.where(places < fixed, places, moved)]].set(jnp.asarray(lengths, jnp.int32))

    lengths = jnp.where(number % 4 == 0, named(packed, number // 4), named(ordinary, number - number // 4 - 1))
    mixed = jax.random.permutation(jax.random.fold_in(own, 3), number_of)
    giver, receiver = mixed[0:number_of // 2 * 2:2], mixed[1:number_of // 2 * 2:2]
    margin = jnp.minimum(lengths[giver] - 1, reach - lengths[receiver]) // 2
    margin = jnp.where((giver == order[0]) | (receiver == order[0]) | (lengths[receiver] == 0), 0, jnp.maximum(margin, 0))
    moved = jax.random.randint(jax.random.fold_in(own, 4), (number_of // 2,), 0, 1 << 20) % (margin + 1)
    lengths = lengths.at[giver].add(-moved).at[receiver].add(moved)
    members = jnp.searchsorted(jnp.cumsum(lengths), jnp.arange(rows * top), side="right").astype(jnp.int32)
    grid = members.reshape(top, rows).T
    grid = grid[jax.random.permutation(jax.random.fold_in(own, 1), rows)]
    offset_by = jax.random.randint(jax.random.fold_in(own, 2), (rows, 1), 0, top)
    return jnp.take_along_axis(grid, (jnp.arange(top)[None, :] + offset_by) % top, axis=1)


def portions_of(count, total, reach, skew, full):
    portions = [(1 << 20) // math.isqrt(rank ** skew) + 1 for rank in range(1, count + 1)]
    largest = reach if full else min(reach, max(-(-total // count), total * portions[0] // sum(portions)))
    least = 1 if total - largest >= count - 1 else 0
    given, spare = [largest] + [least] * (count - 1), total - largest - least * (count - 1)
    while spare > 0:
        candidates = [i for i in range(1, count) if given[i] < largest] or [i for i in range(1, count) if given[i] < reach]
        mass, budget = sum([portions[i] for i in candidates]), spare
        for i in candidates:
            more = min(reach - given[i], max(1, budget * portions[i] // mass), spare)
            given[i] = given[i] + more
            spare = spare - more
    return np.array(given)


def bell_draw(key, shape, deviation, most, cuts=(), held_as=jnp.bfloat16):
    entries = deviation * jax.random.normal(key, shape, jnp.float32)
    if cuts:
        entries = entries * steps_of(key, shape, cuts, -0.22, 0.18)
    return jnp.clip(entries, -most, most).astype(held_as)


def setup_inputs(seed: int = 0, part: int = 0) -> dict:
    seeds = jax.random.split(jax.random.key(seed), 8)
    own_keys = jax.random.split(jax.random.fold_in(seeds[7], part), 8)
    activations = bell_draw(own_keys[0], (TOKENS, D), 1.0, 6.0, ((0, 16),))
    expert_ids_keys = jax.random.split(jax.random.fold_in(own_keys[1], 1), TOKENS // TOK_DEV)
    expert_ids_turns = jax.random.permutation(jax.random.fold_in(own_keys[1], 3), TOKENS // TOK_DEV)
    expert_ids = jax.vmap(lambda own, number: assign_block(jax.random.fold_in(own_keys[1], 2), own, number, TOK_DEV, EXPERTS, 2, CAP, 2))(expert_ids_keys, expert_ids_turns).reshape((TOKENS, 2))
    route_logits = bell_draw(own_keys[2], (TOKENS, 2), 1.5, 6.0, ((0, 16),), jnp.float32)
    norm_gain = jnp.clip(1.0 + 0.15 * jax.random.normal(seeds[3], (D,), jnp.float32), 0.25, 1.75)
    w_gate = bell_draw(seeds[4], (EXPERTS * FF_EXP, D), D ** -0.5, 0.078125, ((0, 16),))
    w_up = bell_draw(seeds[5], (EXPERTS * FF_EXP, D), D ** -0.5, 0.078125, ((0, 16),))
    w_down = bell_draw(seeds[6], (EXPERTS * FF_EXP, D), FF_EXP ** -0.5, 0.09375, ((0, 16),))
    return {"activations": activations, "expert_ids": expert_ids, "route_logits": route_logits, "norm_gain": norm_gain, "w_gate": w_gate, "w_up": w_up, "w_down": w_down}


def reference(activations, expert_ids, route_logits, norm_gain, w_gate, w_up, w_down):
    values = activations.astype(jnp.float32)
    mean_sq = lax.optimization_barrier(jnp.mean(values * values, axis=-1, keepdims=True))
    normed = (values * lax.rsqrt(mean_sq + 1e-06) * norm_gain).astype(jnp.bfloat16)
    routes = expert_ids.reshape(N_EXPERT, 2 * TOK_DEV)
    one_hot = (routes[:, :, None] == jnp.arange(EXPERTS, dtype=jnp.int32)[None, None, :]).astype(jnp.int32)
    ranking = jnp.cumsum(one_hot, axis=1) - one_hot
    slot_index = lax.optimization_barrier(jnp.sum(ranking * one_hot, axis=-1)).astype(jnp.int32)
    source = jnp.arange(N_EXPERT, dtype=jnp.int32)[:, None]
    column = (source * CAP + slot_index).astype(jnp.int32)
    token_index = (source * TOK_DEV + jnp.arange(2 * TOK_DEV, dtype=jnp.int32)[None, :] // 2).astype(jnp.int32)
    pair_weight = jax.nn.sigmoid(route_logits - route_logits[:, ::-1]).reshape(N_EXPERT, 2 * TOK_DEV)
    slot_tokens = jnp.zeros((EXPERTS, N_EXPERT * CAP), jnp.int32).at[routes, column].set(token_index + 1)
    slot_weights = jnp.zeros((EXPERTS, N_EXPERT * CAP), jnp.float32).at[routes, column].set(pair_weight)
    gate_all = w_gate.reshape(EXPERTS, GROUP, FF_DEV, D)
    up_all = w_up.reshape(EXPERTS, GROUP, FF_DEV, D)
    down_all = w_down.reshape(EXPERTS, GROUP, FF_DEV, D)

    def expert_step(total, inputs):
        tokens_here, weights_here, gate_e, up_e, down_e = inputs
        live = tokens_here > 0
        safe = jnp.maximum(tokens_here - 1, 0).astype(jnp.int32)
        rows = jnp.where(live[:, None], normed[safe], jnp.zeros((), jnp.bfloat16))

        def member(accum, pieces):
            gate_part, up_part, down_part = pieces
            gate = lax.dot_general(rows, gate_part, (((1,), (1,)), ((), ())), preferred_element_type=jnp.float32)
            upper = lax.dot_general(rows, up_part, (((1,), (1,)), ((), ())), preferred_element_type=jnp.float32)
            hidden = (jax.nn.silu(gate) * upper).astype(jnp.bfloat16)
            part = jnp.dot(hidden, down_part, preferred_element_type=jnp.float32).astype(jnp.bfloat16)
            return (accum + part.astype(jnp.float32), None)
        accum, unused = lax.scan(member, jnp.zeros((N_EXPERT * CAP, D), jnp.float32), (gate_e, up_e, down_e))
        expert_out = accum.astype(jnp.bfloat16)
        update = jnp.where(live[:, None], weights_here[:, None] * expert_out.astype(jnp.float32), 0.0)
        return (total.at[safe].add(update), None)
    start = jnp.zeros((TOKENS, D), jnp.float32)
    total, unused = lax.scan(expert_step, start, (slot_tokens, slot_weights, gate_all, up_all, down_all))
    return (values + total).astype(jnp.bfloat16)
```

```python
import functools

import jax
import jax.numpy as jnp
from jax import lax
from jax.experimental import pallas as pl
from jax.experimental.pallas import tpu as pltpu
from jax.sharding import PartitionSpec as P

EXPERTS = 4
CAP = 16
CHUNKS = 4
MIB = 1 << 20


def choices(ids, plane):
    tokens = ids.shape[0]
    shape = (tokens, EXPERTS * CAP)
    lane = lax.broadcasted_iota(jnp.int32, shape, 1)
    expert = lax.rem(lane // CAP + plane, EXPERTS)
    slot = (lane % CAP).astype(jnp.float32)
    first = ids[:, 0:1] == expert
    second = ids[:, 1:2] == expert
    named = (first | second).astype(jnp.float32)
    earlier = lax.broadcasted_iota(jnp.int32, (tokens, tokens), 0) > lax.broadcasted_iota(
        jnp.int32, (tokens, tokens), 1
    )
    rank = jnp.dot(earlier.astype(jnp.float32), named, preferred_element_type=jnp.float32)
    here = rank == slot
    return first & here, second & here


def pack_kernel(group, ids_ref, act_ref, gain_ref, *out_refs):
    plane = lax.axis_index("expert") // group
    values = act_ref[...].astype(jnp.float32)
    mean_sq = jnp.mean(values * values, axis=-1, keepdims=True)
    normed = (values * lax.rsqrt(mean_sq + 1e-06) * gain_ref[...]).astype(jnp.bfloat16)
    first, second = choices(ids_ref[...], plane)
    pick = (first | second).astype(jnp.float32).astype(jnp.bfloat16)
    width = out_refs[0].shape[1]
    for k in range(len(out_refs) // EXPERTS):
        rows = lax.dot_general(
            pick,
            normed[:, k * width : (k + 1) * width],
            (((0,), (0,)), ((), ())),
            preferred_element_type=jnp.float32,
        ).astype(jnp.bfloat16)
        for s in range(EXPERTS):
            out_refs[k * EXPERTS + s][...] = rows[s * CAP : (s + 1) * CAP]


def pack(group, ids, activations, gain):
    width = activations.shape[1]
    part = width // CHUNKS
    return pl.pallas_call(
        functools.partial(pack_kernel, group),
        out_shape=[jax.ShapeDtypeStruct((CAP, part), jnp.bfloat16)] * (CHUNKS * EXPERTS),
        compiler_params=pltpu.CompilerParams(vmem_limit_bytes=16 * MIB),
        name="norm_and_pack",
    )(ids, activations, gain.reshape(1, width))


def gate_up_kernel(count, begin, end, *refs):
    pieces, refs = refs[:count], refs[count:]
    gate_w, up_w, refs = refs[0], refs[1], refs[2:]
    held, refs = refs[-1], refs[:-1]

    @pl.when(pl.program_id(0) == 0)
    def _():
        at = 0
        for piece in pieces:
            held[at : at + piece.shape[0], :] = piece[...]
            at += piece.shape[0]

    dims = (((1,), (1,)), ((), ()))
    gate = lax.dot_general(held[...], gate_w[...], dims, preferred_element_type=jnp.float32)
    upper = lax.dot_general(held[...], up_w[...], dims, preferred_element_type=jnp.float32)
    if not begin:
        gate = gate + refs[0][...]
        upper = upper + refs[1][...]
        refs = refs[2:]
    if end:
        refs[0][...] = (jax.nn.silu(gate) * upper).astype(jnp.bfloat16)
    else:
        refs[0][...] = gate
        refs[1][...] = upper


def gate_up(k, pieces, w_gate, w_up, totals):
    begin, end = k == 0, k == CHUNKS - 1
    hidden = w_gate.shape[0]
    part = pieces[0].shape[1]
    rows = sum(p.shape[0] for p in pieces)
    block = 384 if hidden % 384 == 0 else hidden
    total_spec = pl.BlockSpec((rows, block), lambda h: (0, h))
    weight_spec = pl.BlockSpec((block, part), lambda h: (h, k))
    in_specs = [pl.BlockSpec(p.shape, lambda h: (0, 0)) for p in pieces] + [weight_spec] * 2
    in_specs += [total_spec] * len(totals)
    total = jax.ShapeDtypeStruct((rows, hidden), jnp.float32)
    if end:
        out_shape = [jax.ShapeDtypeStruct((rows, hidden), jnp.bfloat16)]
        aliases = {}
    else:
        out_shape = [total, total]
        aliases = {} if begin else {len(pieces) + 2: 0, len(pieces) + 3: 1}
    return pl.pallas_call(
        functools.partial(gate_up_kernel, len(pieces), begin, end),
        grid=(hidden // block,),
        in_specs=in_specs,
        out_specs=[total_spec] * len(out_shape),
        out_shape=out_shape,
        scratch_shapes=[pltpu.VMEM((rows, part), jnp.bfloat16)],
        input_output_aliases=aliases,
        compiler_params=pltpu.CompilerParams(vmem_limit_bytes=24 * MIB),
        cost_estimate=pl.CostEstimate(
            flops=4 * rows * hidden * part,
            bytes_accessed=4 * hidden * part + 16 * rows * hidden,
            transcendentals=0,
        ),
        name="gate_up",
    )(*pieces, w_gate, w_up, *totals)


def down_kernel(hidden_ref, w_ref, keep_ref, send_ref):
    out = jnp.dot(hidden_ref[...], w_ref[...], preferred_element_type=jnp.float32)
    out = out.astype(jnp.bfloat16)
    half = keep_ref.shape[0]
    keep_ref[...] = out[:half]
    send_ref[...] = out[half:]


def down(k, hidden, w_down):
    rows, depth = hidden.shape
    part = w_down.shape[1] // CHUNKS
    block = 512
    steps = part // block
    half = pl.BlockSpec((rows // 2, block), lambda c: (0, c))
    return pl.pallas_call(
        down_kernel,
        grid=(steps,),
        in_specs=[
            pl.BlockSpec((rows, depth), lambda c: (0, 0)),
            pl.BlockSpec((depth, block), lambda c: (0, k * steps + c)),
        ],
        out_specs=[half, half],
        out_shape=[jax.ShapeDtypeStruct((rows // 2, part), jnp.bfloat16)] * 2,
        compiler_params=pltpu.CompilerParams(vmem_limit_bytes=24 * MIB),
        cost_estimate=pl.CostEstimate(
            flops=2 * rows * depth * part,
            bytes_accessed=2 * (depth * part + rows * depth + rows * part),
            transcendentals=0,
        ),
        name="down",
    )(hidden, w_down)


def mix_kernel(group, ids_ref, logits_ref, act_ref, *refs):
    pieces, out_ref = refs[:-1], refs[-1]
    plane = lax.axis_index("expert") // group
    first, second = choices(ids_ref[...], plane)
    first = first.astype(jnp.float32).astype(jnp.bfloat16)
    second = second.astype(jnp.float32).astype(jnp.bfloat16)
    logits = logits_ref[...]
    lead = logits[:, 0:1] - logits[:, 1:2]
    weight_first = jax.nn.sigmoid(lead)
    weight_second = jax.nn.sigmoid(-lead)
    part = pieces[0].shape[1]
    for k in range(len(pieces) // EXPERTS):
        rows = jnp.concatenate([p[...] for p in pieces[k * EXPERTS : (k + 1) * EXPERTS]], axis=0)
        out_first = jnp.dot(first, rows, preferred_element_type=jnp.float32)
        out_second = jnp.dot(second, rows, preferred_element_type=jnp.float32)
        columns = slice(k * part, (k + 1) * part)
        values = act_ref[:, columns].astype(jnp.float32)
        out_ref[:, columns] = (
            values + weight_first * out_first + weight_second * out_second
        ).astype(jnp.bfloat16)


def mix(group, ids, logits, activations, pieces):
    return pl.pallas_call(
        functools.partial(mix_kernel, group),
        out_shape=jax.ShapeDtypeStruct(activations.shape, jnp.bfloat16),
        compiler_params=pltpu.CompilerParams(vmem_limit_bytes=16 * MIB),
        name="mix",
    )(ids, logits, activations, *pieces)


def on_device(activations, expert_ids, route_logits, norm_gain, w_gate, w_up, w_down):
    devices = lax.axis_size("expert")
    group = devices // EXPERTS

    def shift(x, s):
        return lax.ppermute(
            x, "expert", [(i, (i + s * group) % devices) for i in range(devices)]
        )

    def swap(x, bit):
        return lax.ppermute(x, "expert", [(i, i ^ bit) for i in range(devices)])

    packed = pack(group, expert_ids, activations, norm_gain)
    totals = []
    for k in range(CHUNKS):
        own = packed[k * EXPERTS : (k + 1) * EXPERTS]
        gathered = [own[0]] + [shift(own[s], s) for s in range(1, EXPERTS)]
        pieces = [jnp.concatenate(gathered, axis=0)]
        bit = group // 2
        while bit:
            block = pieces[0] if len(pieces) == 1 else jnp.concatenate(pieces, axis=0)
            pieces.append(swap(block, bit))
            bit //= 2
        totals = gate_up(k, pieces, w_gate, w_up, totals)
    hidden = totals[0]
    returned = []
    for k in range(CHUNKS):
        keep, send = down(k, hidden, w_down)
        bit = 1
        while bit < group:
            arrived = swap(send, bit)
            total = keep.astype(jnp.float32) + arrived.astype(jnp.float32)
            total = total.astype(jnp.bfloat16)
            half = total.shape[0] // 2
            keep, send = total[:half], total[half:]
            bit *= 2
        blocks = [total[s * CAP : (s + 1) * CAP] for s in range(EXPERTS)]
        returned.append(blocks[0])
        returned += [shift(blocks[s], -s) for s in range(1, EXPERTS)]
    return mix(group, expert_ids, route_logits, activations, returned)


def solution(mesh):
    in_specs = (
        P(("parts", "expert"), None),
        P(("parts", "expert"), None),
        P(("parts", "expert"), None),
        P(),
        P("expert", None),
        P("expert", None),
        P("expert", None),
    )
    out_specs = P(("parts", "expert"), None)
    return jax.shard_map(
        on_device, mesh=mesh, in_specs=in_specs, out_specs=out_specs, check_vma=False
    )
```

```python
import functools

import jax
import jax.numpy as jnp
from jax import lax
from jax.experimental import pallas as pl
from jax.experimental.pallas import tpu as pltpu
from jax.sharding import PartitionSpec as P

EXPERTS = 4
CAP = 16
BACK = 2
LANES = 128
MIB = 1 << 20


def norm_kernel(ids_ref, logits_ref, act_ref, gain_ref, out_ref):
    tokens, width = act_ref.shape
    values = act_ref[...].astype(jnp.float32)
    mean_sq = jnp.mean(values * values, axis=-1, keepdims=True)
    normed = (values * lax.rsqrt(mean_sq + 1e-06) * gain_ref[...]).astype(jnp.bfloat16)
    out_ref[:, :width] = normed
    ids = ids_ref[...]
    lane = lax.broadcasted_iota(jnp.int32, (tokens, LANES), 1)
    named = ((ids[:, 0:1] == lane) | (ids[:, 1:2] == lane)).astype(jnp.float32)
    square = (tokens, tokens)
    earlier = lax.broadcasted_iota(jnp.int32, square, 0) > lax.broadcasted_iota(
        jnp.int32, square, 1
    )
    rank = jnp.dot(earlier.astype(jnp.float32), named, preferred_element_type=jnp.float32)
    slots = [
        jnp.sum(jnp.where(ids[:, j : j + 1] == lane, rank, 0.0), axis=1, keepdims=True)
        for j in range(2)
    ]
    logits = logits_ref[...]
    lead = logits[:, 0:1] - logits[:, 1:2]
    high = lead.astype(jnp.bfloat16).astype(jnp.float32)
    middle = (lead - high).astype(jnp.bfloat16).astype(jnp.float32)
    low = lead - high - middle
    notes = [ids[:, 0:1].astype(jnp.float32), ids[:, 1:2].astype(jnp.float32)]
    notes += slots + [high, middle, low]
    extra = jnp.zeros((tokens, LANES), jnp.float32)
    for j, note in enumerate(notes):
        extra = jnp.where(lane == j, note, extra)
    out_ref[:, width:] = extra.astype(jnp.bfloat16)


def norm(ids, logits, activations, gain):
    tokens, width = activations.shape
    return pl.pallas_call(
        norm_kernel,
        out_shape=jax.ShapeDtypeStruct((tokens, width + LANES), jnp.bfloat16),
        compiler_params=pltpu.CompilerParams(vmem_limit_bytes=16 * MIB),
        name="norm",
    )(ids, logits, activations, gain.reshape(1, width))


def placement(notes, plane, senders):
    tokens = notes.shape[0]
    notes = notes.astype(jnp.float32)
    here = plane.astype(jnp.float32)
    first, second = notes[:, 0:1] == here, notes[:, 1:2] == here
    slot = jnp.where(first, notes[:, 2:3], jnp.where(second, notes[:, 3:4], float(CAP)))
    shape = (tokens, senders * CAP)
    row = lax.broadcasted_iota(jnp.int32, shape, 0)
    lane = lax.broadcasted_iota(jnp.int32, shape, 1)
    per = tokens // senders
    match = (row // per == lane // CAP) & (slot == (lane % CAP).astype(jnp.float32))
    lead = notes[:, 4:5] + notes[:, 5:6] + notes[:, 6:7]
    weight = jax.nn.sigmoid(jnp.where(first, lead, -lead))
    return match.astype(jnp.float32).astype(jnp.bfloat16), jnp.where(first | second, weight, 0.0)


def gate_up_kernel(group, tok, rows_ref, gate_w, up_w, hidden_ref, held):
    plane = lax.axis_index("expert") // group
    width = gate_w.shape[1]
    senders = 8
    step = 1024

    @pl.when(pl.program_id(0) == 0)
    def _():
        for b in range(rows_ref.shape[0] // (senders * tok)):
            span = pl.ds(b * senders * tok, senders * tok)
            pick, _ = placement(rows_ref[span, width:], plane, senders)
            for c in range(width // step):
                held[pl.ds(b * senders * CAP, senders * CAP), c * step : (c + 1) * step] = (
                    lax.dot_general(
                        pick,
                        rows_ref[span, c * step : (c + 1) * step],
                        (((0,), (0,)), ((), ())),
                        preferred_element_type=jnp.float32,
                    ).astype(jnp.bfloat16)
                )

    dims = (((1,), (1,)), ((), ()))
    gate = lax.dot_general(held[...], gate_w[...], dims, preferred_element_type=jnp.float32)
    upper = lax.dot_general(held[...], up_w[...], dims, preferred_element_type=jnp.float32)
    hidden_ref[...] = (jax.nn.silu(gate) * upper).astype(jnp.bfloat16)


def gate_up(group, tok, rows, w_gate, w_up):
    hidden, width = w_gate.shape
    slots = rows.shape[0] // tok * CAP
    block = 128 if hidden % 128 == 0 else hidden
    weight_spec = pl.BlockSpec((block, width), lambda h: (h, 0))
    return pl.pallas_call(
        functools.partial(gate_up_kernel, group, tok),
        grid=(hidden // block,),
        in_specs=[pl.BlockSpec(rows.shape, lambda h: (0, 0)), weight_spec, weight_spec],
        out_specs=pl.BlockSpec((slots, block), lambda h: (0, h)),
        out_shape=jax.ShapeDtypeStruct((slots, hidden), jnp.bfloat16),
        scratch_shapes=[pltpu.VMEM((slots, width), jnp.bfloat16)],
        compiler_params=pltpu.CompilerParams(
            vmem_limit_bytes=(56 if slots > 256 else 32) * MIB
        ),
        cost_estimate=pl.CostEstimate(
            flops=4 * slots * hidden * width,
            bytes_accessed=4 * hidden * width + 2 * rows.size,
            transcendentals=0,
        ),
        name="gate_up",
    )(rows, w_gate, w_up)


def down_kernel(group, tok, hidden_ref, notes_ref, w_ref, out_ref):
    plane = lax.axis_index("expert") // group
    out = jnp.dot(hidden_ref[...], w_ref[...], preferred_element_type=jnp.float32)
    out = out.astype(jnp.bfloat16)
    senders = 8
    for b in range(notes_ref.shape[0] // (senders * tok)):
        span = pl.ds(b * senders * tok, senders * tok)
        place, weight = placement(notes_ref[span, :], plane, senders)
        rows = jnp.dot(
            place,
            out[b * senders * CAP : (b + 1) * senders * CAP],
            preferred_element_type=jnp.float32,
        )
        out_ref[span, :] = (rows * weight).astype(jnp.bfloat16)


def down(group, tok, k, hidden, rows, w_down):
    slots, depth = hidden.shape
    width = w_down.shape[1]
    part = width // BACK
    tokens = rows.shape[0]
    block = 512
    steps = part // block
    return pl.pallas_call(
        functools.partial(down_kernel, group, tok),
        grid=(steps,),
        in_specs=[
            pl.BlockSpec((slots, depth), lambda c: (0, 0)),
            pl.BlockSpec((tokens, LANES), lambda c: (0, width // LANES)),
            pl.BlockSpec((depth, block), lambda c: (0, k * steps + c)),
        ],
        out_specs=pl.BlockSpec((tokens, block), lambda c: (0, c)),
        out_shape=jax.ShapeDtypeStruct((tokens, part), jnp.bfloat16),
        compiler_params=pltpu.CompilerParams(vmem_limit_bytes=32 * MIB),
        cost_estimate=pl.CostEstimate(
            flops=2 * slots * depth * part,
            bytes_accessed=2 * (depth * part + slots * depth + tokens * part),
            transcendentals=0,
        ),
        name="down",
    )(hidden, rows, w_down)


def on_device(activations, expert_ids, route_logits, norm_gain, w_gate, w_up, w_down):
    group = lax.axis_size("expert") // EXPERTS
    tok = activations.shape[0]
    own = norm(expert_ids, route_logits, activations, norm_gain)
    rows = lax.all_gather(own, "expert", axis=0, tiled=True)
    hidden = gate_up(group, tok, rows, w_gate, w_up)
    summed = [
        lax.psum_scatter(
            down(group, tok, k, hidden, rows, w_down), "expert", scatter_dimension=0, tiled=True
        )
        for k in range(BACK)
    ]
    total = jnp.concatenate(summed, axis=1).astype(jnp.float32)
    return (activations.astype(jnp.float32) + total).astype(jnp.bfloat16)


def solution(mesh):
    in_specs = (
        P(("parts", "expert"), None),
        P(("parts", "expert"), None),
        P(("parts", "expert"), None),
        P(),
        P("expert", None),
        P("expert", None),
        P("expert", None),
    )
    out_specs = P(("parts", "expert"), None)
    return jax.shard_map(
        on_device, mesh=mesh, in_specs=in_specs, out_specs=out_specs, check_vma=False
    )
```

```python
import functools

import jax
import jax.numpy as jnp
from jax import lax
from jax.experimental import pallas as pl
from jax.experimental.pallas import tpu as pltpu
from jax.sharding import PartitionSpec as P

EXPERTS = 4
CAP = 16
CHUNKS = 2
BLOCK = 512
MIB = 1 << 20
SMALL = pltpu.CompilerParams(vmem_limit_bytes=16 * MIB)
LARGE = pltpu.CompilerParams(vmem_limit_bytes=52 * MIB)


def choices(ids, plane):
    tokens = ids.shape[1]
    line = lax.broadcasted_iota(jnp.int32, (EXPERTS * CAP, tokens), 0)
    expert = lax.rem(line // CAP + plane, EXPERTS)
    slot = (line % CAP).astype(jnp.float32)
    first = ids[0:1, :] == expert
    second = ids[1:2, :] == expert
    named = (first | second).astype(jnp.float32)
    square = (tokens, tokens)
    earlier = lax.broadcasted_iota(jnp.int32, square, 0) < lax.broadcasted_iota(
        jnp.int32, square, 1
    )
    rank = jnp.dot(named, earlier.astype(jnp.float32), preferred_element_type=jnp.float32)
    here = rank == slot
    return first & here, second & here


def pack_kernel(group, ids_ref, act_ref, gain_ref, own_ref, *out_refs):
    plane = lax.axis_index("expert") // group
    values = act_ref[...].astype(jnp.float32)
    mean_sq = jnp.mean(values * values, axis=-1, keepdims=True)
    normed = (values * lax.rsqrt(mean_sq + 1e-06) * gain_ref[...]).astype(jnp.bfloat16)
    first, second = choices(ids_ref[...], plane)
    pick = (first | second).astype(jnp.float32).astype(jnp.bfloat16)
    others = EXPERTS - 1
    width = out_refs[0].shape[1]
    for k in range(CHUNKS):
        columns = slice(k * width, (k + 1) * width)
        rows = jnp.dot(pick, normed[:, columns], preferred_element_type=jnp.float32)
        rows = rows.astype(jnp.bfloat16)
        own_ref[:, columns] = rows[:CAP]
        for s in range(others):
            out_refs[k * others + s][...] = rows[(s + 1) * CAP : (s + 2) * CAP]


def pack(group, ids, activations, gain):
    width = activations.shape[1]
    part = jax.ShapeDtypeStruct((CAP, width // CHUNKS), jnp.bfloat16)
    whole = jax.ShapeDtypeStruct((CAP, width), jnp.bfloat16)
    return pl.pallas_call(
        functools.partial(pack_kernel, group),
        out_shape=[whole] + [part] * (CHUNKS * (EXPERTS - 1)),
        compiler_params=SMALL,
        name="norm_and_pack",
    )(ids, activations, gain.reshape(1, width))


def gate_up_kernel(count, begin, end, *refs):
    pieces, refs = refs[:count], refs[count:]
    gate_w, up_w, refs = refs[0], refs[1], refs[2:]
    if not begin:
        gate_in, up_in, refs = refs[0], refs[1], refs[2:]
    if end:
        hidden_ref, gate_sum, up_sum = refs
    else:
        gate_sum, up_sum = refs
    step = pl.program_id(0)

    @pl.when(step == 0)
    def _():
        if begin:
            gate_sum[...] = jnp.zeros_like(gate_sum)
            up_sum[...] = jnp.zeros_like(up_sum)
        else:
            gate_sum[...] = gate_in[...]
            up_sum[...] = up_in[...]

    rows = jnp.concatenate([p[...] for p in pieces], axis=0).T
    gate_sum[...] += jnp.dot(gate_w[...], rows, preferred_element_type=jnp.float32)
    up_sum[...] += jnp.dot(up_w[...], rows, preferred_element_type=jnp.float32)
    if end:

        @pl.when(step == pl.num_programs(0) - 1)
        def _():
            hidden = (jax.nn.silu(gate_sum[...]) * up_sum[...]).astype(jnp.bfloat16)
            hidden_ref[...] = hidden.T


def gate_up(k, pieces, w_gate, w_up, totals):
    begin, end = k == 0, k == CHUNKS - 1
    hidden, width = w_gate.shape
    part = width // CHUNKS
    steps = part // BLOCK
    rows = sum(p.shape[0] for p in pieces)

    def columns(array):
        offset = k * steps if array.shape[1] == width else 0
        return lambda c: (0, offset + c)

    total = jax.ShapeDtypeStruct((hidden, rows), jnp.float32)
    total_spec = pl.BlockSpec((hidden, rows), lambda c: (0, 0))
    in_specs = [pl.BlockSpec((p.shape[0], BLOCK), columns(p)) for p in pieces]
    in_specs += [pl.BlockSpec((hidden, BLOCK), columns(w_gate))] * 2
    in_specs += [total_spec] * len(totals)
    if end:
        out_shape = [jax.ShapeDtypeStruct((rows, hidden), jnp.bfloat16)]
        out_specs = [pl.BlockSpec((rows, hidden), lambda c: (0, 0))]
        scratch = [pltpu.VMEM((hidden, rows), jnp.float32)] * 2
    else:
        out_shape, out_specs, scratch = [total] * 2, [total_spec] * 2, []
    return pl.pallas_call(
        functools.partial(gate_up_kernel, len(pieces), begin, end),
        grid=(steps,),
        in_specs=in_specs,
        out_specs=out_specs,
        out_shape=out_shape,
        scratch_shapes=scratch,
        compiler_params=LARGE,
        cost_estimate=pl.CostEstimate(
            flops=4 * rows * hidden * part,
            bytes_accessed=4 * hidden * part + 8 * rows * hidden,
            transcendentals=0,
        ),
        name="gate_up",
    )(*pieces, w_gate, w_up, *totals)


def down_kernel(hidden_ref, w_ref, keep_ref, send_ref):
    out = jnp.dot(hidden_ref[...], w_ref[...], preferred_element_type=jnp.float32)
    out = out.astype(jnp.bfloat16)
    half = keep_ref.shape[0]
    keep_ref[...] = out[:half]
    send_ref[...] = out[half:]


def down(k, hidden, w_down):
    rows, depth = hidden.shape
    part = w_down.shape[1] // CHUNKS
    steps = part // BLOCK
    half = pl.BlockSpec((rows // 2, BLOCK), lambda c: (0, c))
    return pl.pallas_call(
        down_kernel,
        grid=(steps,),
        in_specs=[
            pl.BlockSpec((rows, depth), lambda c: (0, 0)),
            pl.BlockSpec((depth, BLOCK), lambda c: (0, k * steps + c)),
        ],
        out_specs=[half, half],
        out_shape=[jax.ShapeDtypeStruct((rows // 2, part), jnp.bfloat16)] * 2,
        compiler_params=LARGE,
        cost_estimate=pl.CostEstimate(
            flops=2 * rows * depth * part,
            bytes_accessed=2 * (depth * part + rows * depth + rows * part),
            transcendentals=0,
        ),
        name="down",
    )(hidden, w_down)


def mix_kernel(group, ids_ref, logits_ref, act_ref, arrived_ref, *refs):
    pieces, out_ref = refs[:-1], refs[-1]
    plane = lax.axis_index("expert") // group
    first, second = choices(ids_ref[...], plane)
    lead = logits_ref[0:1, :] - logits_ref[1:2, :]
    weight = jnp.where(first, jax.nn.sigmoid(lead), 0.0)
    weight = (weight + jnp.where(second, jax.nn.sigmoid(-lead), 0.0)).T
    high = weight.astype(jnp.bfloat16)
    rest = weight - high.astype(jnp.float32)
    middle = rest.astype(jnp.bfloat16)
    low = (rest - middle.astype(jnp.float32)).astype(jnp.bfloat16)
    part = pieces[0].shape[1]
    for k in range(CHUNKS):
        columns = slice(k * part, (k + 1) * part)
        blocks = [p[...] for p in pieces[k * EXPERTS : (k + 1) * EXPERTS]]
        own = blocks[0].astype(jnp.float32) + arrived_ref[:, columns].astype(jnp.float32)
        rows = jnp.concatenate([own.astype(jnp.bfloat16)] + blocks[1:], axis=0)
        total = act_ref[:, columns].astype(jnp.float32)
        for term in (low, middle, high):
            total = total + jnp.dot(term, rows, preferred_element_type=jnp.float32)
        out_ref[:, columns] = total.astype(jnp.bfloat16)


def mix(group, ids, logits, activations, arrived, pieces):
    return pl.pallas_call(
        functools.partial(mix_kernel, group),
        out_shape=jax.ShapeDtypeStruct(activations.shape, jnp.bfloat16),
        compiler_params=SMALL,
        name="mix",
    )(ids, logits, activations, arrived, *pieces)


def on_device(activations, expert_ids, route_logits, norm_gain, w_gate, w_up, w_down):
    devices = lax.axis_size("expert")
    group = devices // EXPERTS
    others = EXPERTS - 1
    width = activations.shape[1]
    part = width // CHUNKS
    far = group // 2

    def shift(x, s):
        return lax.ppermute(
            x, "expert", [(i, (i + s * group) % devices) for i in range(devices)]
        )

    def swap(x, bit):
        return lax.ppermute(x, "expert", [(i, i ^ bit) for i in range(devices)])

    ids = expert_ids.T
    own, *packed = pack(group, ids, activations, norm_gain)
    far_own = swap(own, far)
    totals = []
    gathered = []
    for k in range(CHUNKS):
        sends = packed[k * others : (k + 1) * others]
        if gathered:
            sends, gathered = lax.optimization_barrier((sends, gathered))
        gathered = [shift(sends[s], s + 1) for s in range(others)]
        block = jnp.concatenate(gathered, axis=0)
        pieces = [own, block, far_own, swap(block, far)]
        bit = far // 2
        while bit:
            columns = slice(k * part, (k + 1) * part)
            block = [p[:, columns] if p.shape[1] == width else p for p in pieces]
            pieces.append(swap(jnp.concatenate(block, axis=0), bit))
            bit //= 2
        totals = gate_up(k, pieces, w_gate, w_up, totals)
    hidden = totals[0]
    returned, back_own = [], []
    for k in range(CHUNKS):
        keep, send = down(k, hidden, w_down)
        bit = 1
        while bit < far:
            total = keep.astype(jnp.float32) + swap(send, bit).astype(jnp.float32)
            total = total.astype(jnp.bfloat16)
            keep, send = total[: total.shape[0] // 2], total[total.shape[0] // 2 :]
            bit *= 2
        half = total.shape[0] // 2
        back_own.append(total[half : half + CAP])
        block = total[CAP:half].astype(jnp.float32)
        block = block + swap(total[half + CAP :], far).astype(jnp.float32)
        block = block.astype(jnp.bfloat16)
        returned.append(total[:CAP])
        returned += [shift(block[s * CAP : (s + 1) * CAP], -1 - s) for s in range(others)]
    arrived = swap(jnp.concatenate(back_own, axis=1), far)
    return mix(group, ids, route_logits.T, activations, arrived, returned)


def solution(mesh):
    in_specs = (
        P(("parts", "expert"), None),
        P(("parts", "expert"), None),
        P(("parts", "expert"), None),
        P(),
        P("expert", None),
        P("expert", None),
        P("expert", None),
    )
    out_specs = P(("parts", "expert"), None)
    return jax.shard_map(
        on_device, mesh=mesh, in_specs=in_specs, out_specs=out_specs, check_vma=False
    )
```

```python
import functools

import jax
import jax.numpy as jnp
from jax import lax
from jax.experimental import pallas as pl
from jax.experimental.pallas import tpu as pltpu
from jax.sharding import PartitionSpec as P

EXPERTS = 4
CAP = 16
BLOCK = 512
FORTH = (7, 5)
BACK = (5, 7)
MIB = 1 << 20
SMALL = pltpu.CompilerParams(vmem_limit_bytes=16 * MIB)
LARGE = pltpu.CompilerParams(vmem_limit_bytes=52 * MIB)


def spans(width, shares):
    unit = width // sum(shares)
    return [(sum(shares[:k]) * unit, n * unit) for k, n in enumerate(shares)]


def choices(ids, plane):
    tokens = ids.shape[1]
    line = lax.broadcasted_iota(jnp.int32, (EXPERTS * CAP, tokens), 0)
    expert = lax.rem(line // CAP + plane, EXPERTS)
    slot = (line % CAP).astype(jnp.float32)
    first = ids[0:1, :] == expert
    second = ids[1:2, :] == expert
    named = (first | second).astype(jnp.float32)
    square = (tokens, tokens)
    earlier = lax.broadcasted_iota(jnp.int32, square, 0) < lax.broadcasted_iota(
        jnp.int32, square, 1
    )
    rank = jnp.dot(named, earlier.astype(jnp.float32), preferred_element_type=jnp.float32)
    here = rank == slot
    return first & here, second & here


def pack_kernel(group, ids_ref, act_ref, gain_ref, own_ref, *out_refs):
    plane = lax.axis_index("expert") // group
    values = act_ref[...].astype(jnp.float32)
    mean_sq = jnp.mean(values * values, axis=-1, keepdims=True)
    normed = (values * lax.rsqrt(mean_sq + 1e-06) * gain_ref[...]).astype(jnp.bfloat16)
    first, second = choices(ids_ref[...], plane)
    pick = (first | second).astype(jnp.float32).astype(jnp.bfloat16)
    others = EXPERTS - 1
    for k, (at, part) in enumerate(spans(act_ref.shape[1], FORTH)):
        columns = slice(at, at + part)
        rows = jnp.dot(pick, normed[:, columns], preferred_element_type=jnp.float32)
        rows = rows.astype(jnp.bfloat16)
        own_ref[:, columns] = rows[:CAP]
        for s in range(others):
            out_refs[k * others + s][...] = rows[(s + 1) * CAP : (s + 2) * CAP]


def pack(group, ids, activations, gain):
    width = activations.shape[1]
    shapes = [width]
    for _, part in spans(width, FORTH):
        shapes += [part] * (EXPERTS - 1)
    return pl.pallas_call(
        functools.partial(pack_kernel, group),
        out_shape=[jax.ShapeDtypeStruct((CAP, n), jnp.bfloat16) for n in shapes],
        compiler_params=LARGE,
        name="norm_and_pack",
    )(ids, activations, gain.reshape(1, width))


def fetches(weights, at, held, sems):
    return [
        [
            pltpu.make_async_copy(
                w.at[:, at + c * BLOCK : at + (c + 1) * BLOCK], held.at[j, c], sems.at[j, c]
            )
            for c in range(held.shape[1])
        ]
        for j, w in enumerate(weights)
    ]


def gate_up_kernel(count, at, begin, end, *refs):
    pieces, refs = refs[:count], refs[count:]
    weights, refs = refs[:2], refs[2:]
    held, turned, sems, refs = *refs[-3:], refs[:-3]
    if not begin:
        before, refs = refs[:2], refs[2:]
    if end:
        hidden_ref, refs = refs[0], refs[1:]
    sums = refs
    steps, _, block = held.shape[1:]
    for pair in zip(*fetches(weights, at, held, sems)):
        for copy in pair:
            copy.start()
    for j in range(2):
        sums[j][...] = jnp.zeros_like(sums[j]) if begin else before[j][...]
    wide = steps * block

    @pl.loop(0, steps)
    def _(c):
        parts = []
        for p in pieces:
            first = at if p.shape[1] > wide else 0
            parts.append(p[:, pl.ds(pl.multiple_of(first + c * block, block), block)])
        turned[c] = jnp.concatenate(parts, axis=0).T

    @pl.loop(0, steps)
    def _(c):
        for j in range(2):
            pltpu.make_async_copy(held.at[j, c], held.at[j, c], sems.at[j, c]).wait()
        for j in range(2):
            sums[j][...] += jnp.dot(held[j, c], turned[c], preferred_element_type=jnp.float32)

    if end:
        hidden = (jax.nn.silu(sums[0][...]) * sums[1][...]).astype(jnp.bfloat16)
        hidden_ref[...] = hidden.T


def gate_up(at, part, pieces, w_gate, w_up, totals):
    hidden, width = w_gate.shape
    begin, end = at == 0, at + part == width
    steps = part // BLOCK
    rows = sum(p.shape[0] for p in pieces)
    total = jax.ShapeDtypeStruct((hidden, rows), jnp.float32)
    in_specs = [pl.BlockSpec(memory_space=pltpu.VMEM)] * len(pieces)
    in_specs += [pl.BlockSpec(memory_space=pl.ANY)] * 2
    in_specs += [pl.BlockSpec(memory_space=pltpu.VMEM)] * len(totals)
    out_shape, scratch = [total] * 2, []
    if end:
        out_shape = [jax.ShapeDtypeStruct((rows, hidden), jnp.bfloat16)]
        scratch = [pltpu.VMEM((hidden, rows), jnp.float32)] * 2
    scratch += [
        pltpu.VMEM((2, steps, hidden, BLOCK), jnp.bfloat16),
        pltpu.VMEM((steps, BLOCK, rows), jnp.bfloat16),
        pltpu.SemaphoreType.DMA((2, steps)),
    ]
    return pl.pallas_call(
        functools.partial(gate_up_kernel, len(pieces), at, begin, end),
        in_specs=in_specs,
        out_shape=out_shape,
        scratch_shapes=scratch,
        compiler_params=LARGE,
        cost_estimate=pl.CostEstimate(
            flops=4 * rows * hidden * part,
            bytes_accessed=4 * hidden * part + 8 * rows * hidden,
            transcendentals=0,
        ),
        name="gate_up",
    )(*pieces, w_gate, w_up, *totals)


def down_kernel(at, hidden_ref, w_ref, keep_ref, send_ref, held, sems):
    steps, _, block = held.shape[1:]
    for copy in fetches([w_ref], at, held, sems)[0]:
        copy.start()
    half = keep_ref.shape[0]

    @pl.loop(0, steps)
    def _(c):
        pltpu.make_async_copy(held.at[0, c], held.at[0, c], sems.at[0, c]).wait()
        out = jnp.dot(hidden_ref[...], held[0, c], preferred_element_type=jnp.float32)
        out = out.astype(jnp.bfloat16)
        columns = pl.ds(pl.multiple_of(c * block, block), block)
        keep_ref[:, columns] = out[:half]
        send_ref[:, columns] = out[half:]


def down(at, part, hidden, w_down):
    rows, depth = hidden.shape
    steps = part // BLOCK
    return pl.pallas_call(
        functools.partial(down_kernel, at),
        in_specs=[pl.BlockSpec(memory_space=pltpu.VMEM), pl.BlockSpec(memory_space=pl.ANY)],
        out_shape=[jax.ShapeDtypeStruct((rows // 2, part), jnp.bfloat16)] * 2,
        scratch_shapes=[
            pltpu.VMEM((1, steps, depth, BLOCK), jnp.bfloat16),
            pltpu.SemaphoreType.DMA((1, steps)),
        ],
        compiler_params=LARGE,
        cost_estimate=pl.CostEstimate(
            flops=2 * rows * depth * part,
            bytes_accessed=2 * (depth * part + rows * depth + rows * part),
            transcendentals=0,
        ),
        name="down",
    )(hidden, w_down)


def mix_kernel(group, ids_ref, logits_ref, act_ref, arrived_ref, *refs):
    pieces, out_ref = refs[:-1], refs[-1]
    plane = lax.axis_index("expert") // group
    first, second = choices(ids_ref[...], plane)
    lead = logits_ref[0:1, :] - logits_ref[1:2, :]
    weight = jnp.where(first, jax.nn.sigmoid(lead), 0.0)
    weight = (weight + jnp.where(second, jax.nn.sigmoid(-lead), 0.0)).T
    high = weight.astype(jnp.bfloat16)
    rest = weight - high.astype(jnp.float32)
    middle = rest.astype(jnp.bfloat16)
    low = (rest - middle.astype(jnp.float32)).astype(jnp.bfloat16)
    for k, (at, part) in enumerate(spans(act_ref.shape[1], BACK)):
        columns = slice(at, at + part)
        blocks = [p[...] for p in pieces[k * EXPERTS : (k + 1) * EXPERTS]]
        own = blocks[0].astype(jnp.float32) + arrived_ref[:, columns].astype(jnp.float32)
        rows = jnp.concatenate([own.astype(jnp.bfloat16)] + blocks[1:], axis=0)
        total = act_ref[:, columns].astype(jnp.float32)
        for term in (low, middle, high):
            total = total + jnp.dot(term, rows, preferred_element_type=jnp.float32)
        out_ref[:, columns] = total.astype(jnp.bfloat16)


def mix(group, ids, logits, activations, arrived, pieces):
    return pl.pallas_call(
        functools.partial(mix_kernel, group),
        out_shape=jax.ShapeDtypeStruct(activations.shape, jnp.bfloat16),
        compiler_params=SMALL,
        name="mix",
    )(ids, logits, activations, arrived, *pieces)


def on_device(activations, expert_ids, route_logits, norm_gain, w_gate, w_up, w_down):
    devices = lax.axis_size("expert")
    group = devices // EXPERTS
    others = EXPERTS - 1
    width = activations.shape[1]
    far = group // 2

    def shift(x, s):
        return lax.ppermute(
            x, "expert", [(i, (i + s * group) % devices) for i in range(devices)]
        )

    def swap(x, bit):
        return lax.ppermute(x, "expert", [(i, i ^ bit) for i in range(devices)])

    ids = expert_ids.T
    own, *packed = pack(group, ids, activations, norm_gain)
    far_own = swap(own, far)
    totals = []
    for k, (at, part) in enumerate(spans(width, FORTH)):
        sends = packed[k * others : (k + 1) * others]
        block = jnp.concatenate([shift(sends[s], s + 1) for s in range(others)], axis=0)
        pieces = [own, block, far_own, swap(block, far)]
        bit = far // 2
        while bit:
            block = [p[:, at : at + part] if p.shape[1] == width else p for p in pieces]
            block = jnp.concatenate(block, axis=0)
            if totals:
                block, totals = lax.optimization_barrier((block, totals))
            pieces.append(swap(block, bit))
            bit //= 2
        totals = gate_up(at, part, pieces, w_gate, w_up, totals)
    hidden = totals[0]
    returned, back_own = [], []
    for at, part in spans(width, BACK):
        keep, send = down(at, part, hidden, w_down)
        bit = 1
        while bit < far:
            total = keep.astype(jnp.float32) + swap(send, bit).astype(jnp.float32)
            total = total.astype(jnp.bfloat16)
            keep, send = total[: total.shape[0] // 2], total[total.shape[0] // 2 :]
            bit *= 2
        half = total.shape[0] // 2
        back_own.append(total[half : half + CAP])
        block = total[CAP:half].astype(jnp.float32)
        block = block + swap(total[half + CAP :], far).astype(jnp.float32)
        block = block.astype(jnp.bfloat16)
        returned.append(total[:CAP])
        returned += [shift(block[s * CAP : (s + 1) * CAP], -1 - s) for s in range(others)]
    arrived = swap(jnp.concatenate(back_own, axis=1), far)
    return mix(group, ids, route_logits.T, activations, arrived, returned)


def solution(mesh):
    in_specs = (
        P(("parts", "expert"), None),
        P(("parts", "expert"), None),
        P(("parts", "expert"), None),
        P(),
        P("expert", None),
        P("expert", None),
        P("expert", None),
    )
    out_specs = P(("parts", "expert"), None)
    return jax.shard_map(
        on_device, mesh=mesh, in_specs=in_specs, out_specs=out_specs, check_vma=False
    )
```

```python
import functools

import jax
import jax.numpy as jnp
from jax import lax
from jax.experimental import pallas as pl
from jax.experimental.pallas import tpu as pltpu
from jax.sharding import PartitionSpec as P

EXPERTS = 4
CAP = 16
CHUNKS = 2
BLOCK = 1024
FETCH_ROWS = 144
MIB = 1 << 20
LIMIT = pltpu.CompilerParams(vmem_limit_bytes=16 * MIB)
VMEM = pl.BlockSpec(memory_space=pltpu.VMEM)
ANY = pl.BlockSpec(memory_space=pl.ANY)


def choices(ids):
    tokens = ids.shape[1]
    line = lax.broadcasted_iota(jnp.int32, (EXPERTS * CAP, tokens), 0)
    expert = line // CAP
    slot = (line % CAP).astype(jnp.float32)
    first = ids[0:1, :] == expert
    second = ids[1:2, :] == expert
    named = (first | second).astype(jnp.float32)
    square = (tokens, tokens)
    earlier = lax.broadcasted_iota(jnp.int32, square, 0) < lax.broadcasted_iota(
        jnp.int32, square, 1
    )
    rank = jnp.dot(named, earlier.astype(jnp.float32), preferred_element_type=jnp.float32)
    here = rank == slot
    return first & here, second & here


def pack_kernel(ids_ref, act_ref, gain_ref, *out_refs):
    values = act_ref[...].astype(jnp.float32)
    mean_sq = jnp.mean(values * values, axis=-1, keepdims=True)
    normed = (values * lax.rsqrt(mean_sq + 1e-06) * gain_ref[...]).astype(jnp.bfloat16)
    first, second = choices(ids_ref[...])
    pick = (first | second).astype(jnp.float32).astype(jnp.bfloat16)
    width = out_refs[0].shape[1]
    for k in range(CHUNKS):
        columns = slice(k * width, (k + 1) * width)
        rows = jnp.dot(pick, normed[:, columns], preferred_element_type=jnp.float32)
        out_refs[k][...] = rows.astype(jnp.bfloat16)


def pack(ids, activations, gain):
    width = activations.shape[1]
    part = jax.ShapeDtypeStruct((EXPERTS * CAP, width // CHUNKS), jnp.bfloat16)
    return pl.pallas_call(
        pack_kernel,
        out_shape=[part] * CHUNKS,
        compiler_params=LIMIT,
        name="norm_and_pack",
    )(ids, activations, gain.reshape(1, width))


def fetch_kernel(count, at, *refs):
    weights, held, sems = refs[:count], refs[count + 1 : -1], refs[-1]
    copies = []
    for j in range(count):
        part = held[j].shape[1]
        for b in range(sems.shape[1]):
            rows = pl.ds(b * FETCH_ROWS, FETCH_ROWS)
            copies.append(
                pltpu.make_async_copy(
                    weights[j].at[rows, at : at + part], held[j].at[rows], sems.at[j, b]
                )
            )
    for copy in copies:
        copy.start()
    for copy in copies:
        copy.wait()


def fetch(weights, at, part, after):
    count = len(weights)
    rows = weights[0].shape[0]
    held = pltpu.VMEM((rows, part), jnp.bfloat16)
    return pl.pallas_call(
        functools.partial(fetch_kernel, count, at),
        in_specs=[ANY] * (count + 1),
        out_specs=[VMEM] * count,
        out_shape=[held] * count,
        scratch_shapes=[pltpu.SemaphoreType.DMA((count, rows // FETCH_ROWS))],
        compiler_params=LIMIT,
        cost_estimate=pl.CostEstimate(
            flops=0, bytes_accessed=4 * count * rows * part, transcendentals=0
        ),
        name="fetch",
    )(*[pltpu.with_memory_space_constraint(w, pltpu.HBM) for w in weights], after)


def gate_up_kernel(count, begin, end, *refs):
    pieces, refs = refs[:count], refs[count:]
    weights, refs = refs[:2], refs[2:]
    turned, refs = refs[-1], refs[:-1]
    if not begin:
        before, refs = refs[:2], refs[2:]
    if end:
        hidden_ref, refs = refs[0], refs[1:]
    sums = refs
    steps, block, _ = turned.shape

    @pl.loop(0, steps)
    def _(c):
        columns = pl.ds(pl.multiple_of(c * block, block), block)
        turned[c] = jnp.concatenate([p[:, columns] for p in pieces], axis=0).T

    for j in range(2):
        sums[j][...] = jnp.zeros_like(sums[j]) if begin else before[j][...]

    @pl.loop(0, steps)
    def _(c):
        columns = pl.ds(pl.multiple_of(c * block, block), block)
        for j in range(2):
            sums[j][...] += jnp.dot(
                weights[j][:, columns], turned[c], preferred_element_type=jnp.float32
            )

    if end:
        hidden = (jax.nn.silu(sums[0][...]) * sums[1][...]).astype(jnp.bfloat16)
        hidden_ref[...] = hidden.T


def gate_up(k, pieces, weights, totals):
    hidden, part = weights[0].shape
    begin, end = k == 0, k == CHUNKS - 1
    rows = sum(p.shape[0] for p in pieces)
    total = jax.ShapeDtypeStruct((hidden, rows), jnp.float32)
    out_shape, scratch = [total] * 2, []
    if end:
        out_shape = [jax.ShapeDtypeStruct((rows, hidden), jnp.bfloat16)]
        scratch = [pltpu.VMEM((hidden, rows), jnp.float32)] * 2
    scratch.append(pltpu.VMEM((part // BLOCK, BLOCK, rows), jnp.bfloat16))
    weights = [pltpu.with_memory_space_constraint(w, pltpu.VMEM) for w in weights]
    return pl.pallas_call(
        functools.partial(gate_up_kernel, len(pieces), begin, end),
        in_specs=[VMEM] * (len(pieces) + 2 + len(totals)),
        out_shape=out_shape,
        scratch_shapes=scratch,
        compiler_params=LIMIT,
        cost_estimate=pl.CostEstimate(
            flops=4 * rows * hidden * part,
            bytes_accessed=4 * hidden * part + 8 * rows * hidden,
            transcendentals=0,
        ),
        name="gate_up",
    )(*pieces, *weights, *totals)


def down_kernel(at, hidden_ref, w_ref, keep_ref, send_ref):
    half, part = keep_ref.shape
    block = BLOCK // 2

    @pl.loop(0, part // block)
    def _(c):
        columns = pl.ds(pl.multiple_of(at + c * block, block), block)
        out = jnp.dot(hidden_ref[...], w_ref[:, columns], preferred_element_type=jnp.float32)
        out = out.astype(jnp.bfloat16)
        columns = pl.ds(pl.multiple_of(c * block, block), block)
        keep_ref[:, columns] = out[:half]
        send_ref[:, columns] = out[half:]


def down(at, part, hidden, w_down):
    rows, depth = hidden.shape
    return pl.pallas_call(
        functools.partial(down_kernel, at),
        in_specs=[VMEM, VMEM],
        out_shape=[jax.ShapeDtypeStruct((rows // 2, part), jnp.bfloat16)] * 2,
        compiler_params=LIMIT,
        cost_estimate=pl.CostEstimate(
            flops=2 * rows * depth * part,
            bytes_accessed=2 * (depth * part + rows * depth + rows * part),
            transcendentals=0,
        ),
        name="down",
    )(hidden, pltpu.with_memory_space_constraint(w_down, pltpu.VMEM))


def mix_kernel(ids_ref, logits_ref, act_ref, *refs):
    pieces, out_ref = refs[:-1], refs[-1]
    first, second = choices(ids_ref[...])
    lead = logits_ref[0:1, :] - logits_ref[1:2, :]
    weight = jnp.where(first, jax.nn.sigmoid(lead), 0.0)
    weight = (weight + jnp.where(second, jax.nn.sigmoid(-lead), 0.0)).T
    high = weight.astype(jnp.bfloat16)
    rest = weight - high.astype(jnp.float32)
    middle = rest.astype(jnp.bfloat16)
    low = (rest - middle.astype(jnp.float32)).astype(jnp.bfloat16)
    part = pieces[0].shape[1]
    for k, piece in enumerate(pieces):
        columns = slice(k * part, (k + 1) * part)
        total = act_ref[:, columns].astype(jnp.float32)
        for term in (low, middle, high):
            total = total + jnp.dot(term, piece[...], preferred_element_type=jnp.float32)
        out_ref[:, columns] = total.astype(jnp.bfloat16)


def mix(ids, logits, activations, pieces):
    return pl.pallas_call(
        mix_kernel,
        out_shape=jax.ShapeDtypeStruct(activations.shape, jnp.bfloat16),
        compiler_params=LIMIT,
        name="mix",
    )(ids, logits, activations, *pieces)


def on_device(activations, expert_ids, route_logits, norm_gain, w_gate, w_up, w_down):
    devices = lax.axis_size("expert")
    group = devices // EXPERTS
    width = activations.shape[1]
    part = width // CHUNKS
    planes = [[g + e * group for e in range(EXPERTS)] for g in range(group)]

    def across(x):
        return lax.all_to_all(
            x, "expert", split_axis=0, concat_axis=0, tiled=True, axis_index_groups=planes
        )

    def swap(x, bit):
        return lax.ppermute(x, "expert", [(i, i ^ bit) for i in range(devices)])

    ids = expert_ids.T
    packed = pack(ids, activations, norm_gain)
    gate_up_w = [fetch([w_gate, w_up], k * part, part, packed[0]) for k in range(CHUNKS)]
    gathered = [across(p) for p in packed]
    totals = []
    for k in range(CHUNKS):
        block = gathered[k]
        if k:
            block, _ = lax.optimization_barrier((block, gathered[k - 1]))
        pieces = [block]
        bit = group // 2
        while bit:
            if bit == 1 and totals:
                block, totals = lax.optimization_barrier((block, totals))
            pieces.append(swap(block, bit))
            block = jnp.concatenate([block, pieces[-1]], axis=0)
            bit //= 2
        totals = gate_up(k, pieces, gate_up_w[k], totals)
        if k == CHUNKS - 2:
            (down_w,) = fetch([w_down], 0, width, totals[0])
    hidden = totals[0]
    returned = []
    for k in range(CHUNKS):
        keep, send = down(k * part, part, hidden, down_w)
        bit = 1
        while True:
            total = keep.astype(jnp.float32) + swap(send, bit).astype(jnp.float32)
            total = total.astype(jnp.bfloat16)
            bit *= 2
            if bit == group:
                break
            keep, send = total[: total.shape[0] // 2], total[total.shape[0] // 2 :]
        returned.append(across(total))
    return mix(ids, route_logits.T, activations, returned)


def solution(mesh):
    in_specs = (
        P(("parts", "expert"), None),
        P(("parts", "expert"), None),
        P(("parts", "expert"), None),
        P(),
        P("expert", None),
        P("expert", None),
        P("expert", None),
    )
    out_specs = P(("parts", "expert"), None)
    return jax.shard_map(
        on_device, mesh=mesh, in_specs=in_specs, out_specs=out_specs, check_vma=False
    )
```

```python
import functools

import jax
import jax.numpy as jnp
from jax import lax
from jax.experimental import pallas as pl
from jax.experimental.pallas import tpu as pltpu
from jax.sharding import PartitionSpec as P

EXPERTS = 4
CAP = 16
HALVES = 2
BLOCK = 1024
FETCH_ROWS = 144
MIB = 1 << 20
LIMIT = pltpu.CompilerParams(vmem_limit_bytes=16 * MIB)
VMEM = pl.BlockSpec(memory_space=pltpu.VMEM)
ANY = pl.BlockSpec(memory_space=pl.ANY)


def choices(ids, plane):
    tokens = ids.shape[1]
    line = lax.broadcasted_iota(jnp.int32, (EXPERTS * CAP, tokens), 0)
    expert = lax.rem(line // CAP + plane, EXPERTS)
    slot = (line % CAP).astype(jnp.float32)
    first = ids[0:1, :] == expert
    second = ids[1:2, :] == expert
    named = (first | second).astype(jnp.float32)
    square = (tokens, tokens)
    earlier = lax.broadcasted_iota(jnp.int32, square, 0) < lax.broadcasted_iota(
        jnp.int32, square, 1
    )
    rank = jnp.dot(named, earlier.astype(jnp.float32), preferred_element_type=jnp.float32)
    here = rank == slot
    return first & here, second & here


def pack_kernel(group, ids_ref, act_ref, gain_ref, *out_refs):
    plane = lax.axis_index("expert") // group
    values = act_ref[...].astype(jnp.float32)
    mean_sq = jnp.mean(values * values, axis=-1, keepdims=True)
    normed = (values * lax.rsqrt(mean_sq + 1e-06) * gain_ref[...]).astype(jnp.bfloat16)
    first, second = choices(ids_ref[...], plane)
    pick = (first | second).astype(jnp.float32).astype(jnp.bfloat16)
    rows = jnp.dot(pick, normed, preferred_element_type=jnp.float32).astype(jnp.bfloat16)
    for s, out_ref in zip((0, 1, 3), out_refs):
        out_ref[...] = rows[s * CAP : (s + 1) * CAP]
    part = out_refs[-1].shape[1]
    for k, out_ref in enumerate(out_refs[3:]):
        out_ref[...] = rows[2 * CAP : 3 * CAP, k * part : (k + 1) * part]


def pack(group, ids, activations, gain):
    width = activations.shape[1]
    widths = [width] * 3 + [width // HALVES] * HALVES
    return pl.pallas_call(
        functools.partial(pack_kernel, group),
        out_shape=[jax.ShapeDtypeStruct((CAP, n), jnp.bfloat16) for n in widths],
        compiler_params=LIMIT,
        name="norm_and_pack",
    )(ids, activations, gain.reshape(1, width))


def fetches(weights, at, held, sems):
    copies = []
    for j, w in enumerate(weights):
        part = held[j].shape[1]
        for b in range(sems.shape[1]):
            rows = pl.ds(b * FETCH_ROWS, FETCH_ROWS)
            copies.append(
                pltpu.make_async_copy(w.at[rows, at : at + part], held[j].at[rows], sems.at[j, b])
            )
    return copies


def fetch_kernel(at, w_ref, after_ref, held_ref, sems):
    copies = fetches([w_ref], at, [held_ref], sems)
    for copy in copies:
        copy.start()
    for copy in copies:
        copy.wait()


def fetch(w, at, part, after):
    rows = w.shape[0]
    return pl.pallas_call(
        functools.partial(fetch_kernel, at),
        in_specs=[ANY, ANY],
        out_specs=VMEM,
        out_shape=pltpu.VMEM((rows, part), jnp.bfloat16),
        scratch_shapes=[pltpu.SemaphoreType.DMA((1, rows // FETCH_ROWS))],
        compiler_params=LIMIT,
        cost_estimate=pl.CostEstimate(flops=0, bytes_accessed=4 * rows * part, transcendentals=0),
        name="fetch",
    )(pltpu.with_memory_space_constraint(w, pltpu.HBM), after)


def gate_up_kernel(count, ahead, at, begin, end, *refs):
    pieces, refs = refs[:count], refs[count:]
    weights, later, refs = refs[:2], refs[2 : 2 + ahead], refs[2 + ahead :]
    if not begin:
        before, refs = refs[:2], refs[2:]
    held, refs = refs[:ahead], refs[ahead:]
    turned, sems, refs = *refs[-2:], refs[:-2]
    if end:
        hidden_ref, refs = refs[0], refs[1:]
    sums = refs
    steps, block, _ = turned.shape
    copies = fetches(later, 0 if end else steps * block, held, sems)
    for copy in copies:
        copy.start()

    @pl.loop(0, steps)
    def _(c):
        parts = []
        for p in pieces:
            first = at if p.shape[1] > steps * block else 0
            parts.append(p[:, pl.ds(pl.multiple_of(first + c * block, block), block)])
        turned[c] = jnp.concatenate(parts, axis=0).T

    for j in range(2):
        sums[j][...] = jnp.zeros_like(sums[j]) if begin else before[j][...]

    @pl.loop(0, steps)
    def _(c):
        columns = pl.ds(pl.multiple_of(c * block, block), block)
        for j in range(2):
            sums[j][...] += jnp.dot(
                weights[j][:, columns], turned[c], preferred_element_type=jnp.float32
            )

    if end:
        hidden = (jax.nn.silu(sums[0][...]) * sums[1][...]).astype(jnp.bfloat16)
        hidden_ref[...] = hidden.T
    for copy in copies:
        copy.wait()


def gate_up(k, pieces, weights, later, totals):
    hidden, part = weights[0].shape
    begin, end = k == 0, k == HALVES - 1
    rows = sum(p.shape[0] for p in pieces)
    total = jax.ShapeDtypeStruct((hidden, rows), jnp.float32)
    width = later[0].shape[1] if end else part
    out_shape = [pltpu.VMEM((hidden, width), jnp.bfloat16)] * len(later)
    out_specs = [VMEM] * len(later)
    scratch = []
    if end:
        out_shape.append(jax.ShapeDtypeStruct((rows, hidden), jnp.bfloat16))
        scratch += [pltpu.VMEM((hidden, rows), jnp.float32)] * 2
    else:
        out_shape += [total] * 2
    out_specs += [VMEM] * (len(out_shape) - len(later))
    scratch.append(pltpu.VMEM((part // BLOCK, BLOCK, rows), jnp.bfloat16))
    scratch.append(pltpu.SemaphoreType.DMA((len(later), hidden // FETCH_ROWS)))
    weights = [pltpu.with_memory_space_constraint(w, pltpu.VMEM) for w in weights]
    later = [pltpu.with_memory_space_constraint(w, pltpu.HBM) for w in later]
    out = pl.pallas_call(
        functools.partial(gate_up_kernel, len(pieces), len(later), k * part, begin, end),
        in_specs=[VMEM] * (len(pieces) + 2) + [ANY] * len(later) + [VMEM] * len(totals),
        out_specs=out_specs,
        out_shape=out_shape,
        scratch_shapes=scratch,
        compiler_params=LIMIT,
        cost_estimate=pl.CostEstimate(
            flops=4 * rows * hidden * part,
            bytes_accessed=4 * hidden * part + 8 * rows * hidden,
            transcendentals=0,
        ),
        name="gate_up",
    )(*pieces, *weights, *later, *totals)
    return out[: len(later)], out[len(later) :]


def down_kernel(at, hidden_ref, w_ref, keep_ref, send_ref):
    half, part = keep_ref.shape
    first = 3 * half // 4
    block = BLOCK // 2

    @pl.loop(0, part // block)
    def _(c):
        columns = pl.ds(pl.multiple_of(at + c * block, block), block)
        out = jnp.dot(hidden_ref[...], w_ref[:, columns], preferred_element_type=jnp.float32)
        out = out.astype(jnp.bfloat16)
        columns = pl.ds(pl.multiple_of(c * block, block), block)
        for j, ref in enumerate((keep_ref, send_ref)):
            ref[:first, columns] = out[j * first : (j + 1) * first]
            far_rows = out[2 * first :]
            ref[first:, columns] = far_rows[j * (half - first) : (j + 1) * (half - first)]


def down(at, part, hidden, w_down):
    rows, depth = hidden.shape
    return pl.pallas_call(
        functools.partial(down_kernel, at),
        in_specs=[VMEM, VMEM],
        out_shape=[jax.ShapeDtypeStruct((rows // 2, part), jnp.bfloat16)] * 2,
        compiler_params=LIMIT,
        cost_estimate=pl.CostEstimate(
            flops=2 * rows * depth * part,
            bytes_accessed=2 * (depth * part + rows * depth + rows * part),
            transcendentals=0,
        ),
        name="down",
    )(hidden, pltpu.with_memory_space_constraint(w_down, pltpu.VMEM))


def mix_kernel(group, ids_ref, logits_ref, act_ref, arrived, near, last, *refs):
    out_ref, kept, middle_rows = refs[-1], refs[:HALVES], refs[HALVES:-1]
    plane = lax.axis_index("expert") // group
    first, second = choices(ids_ref[...], plane)
    lead = logits_ref[0:1, :] - logits_ref[1:2, :]
    weight = jnp.where(first, jax.nn.sigmoid(lead), 0.0)
    weight = (weight + jnp.where(second, jax.nn.sigmoid(-lead), 0.0)).T
    high = weight.astype(jnp.bfloat16)
    rest = weight - high.astype(jnp.float32)
    middle = rest.astype(jnp.bfloat16)
    low = (rest - middle.astype(jnp.float32)).astype(jnp.bfloat16)
    part = kept[0].shape[1]
    for k in range(HALVES):
        columns = slice(k * part, (k + 1) * part)
        own = kept[k][...].astype(jnp.float32) + arrived[:, columns].astype(jnp.float32)
        blocks = [own.astype(jnp.bfloat16), near[:, columns], middle_rows[k][...]]
        rows = jnp.concatenate(blocks + [last[:, columns]], axis=0)
        total = act_ref[:, columns].astype(jnp.float32)
        for term in (low, middle, high):
            total = total + jnp.dot(term, rows, preferred_element_type=jnp.float32)
        out_ref[:, columns] = total.astype(jnp.bfloat16)


def mix(group, ids, logits, activations, pieces):
    return pl.pallas_call(
        functools.partial(mix_kernel, group),
        out_shape=jax.ShapeDtypeStruct(activations.shape, jnp.bfloat16),
        compiler_params=LIMIT,
        name="mix",
    )(ids, logits, activations, *pieces)


def added(mine, arrived):
    total = mine.astype(jnp.float32) + arrived.astype(jnp.float32)
    return total.astype(jnp.bfloat16)


def on_device(activations, expert_ids, route_logits, norm_gain, w_gate, w_up, w_down):
    devices = lax.axis_size("expert")
    group = devices // EXPERTS
    far = group // 2
    width = activations.shape[1]
    part = width // HALVES

    def shift(x, s):
        return lax.ppermute(
            x, "expert", [(i, (i + s * group) % devices) for i in range(devices)]
        )

    def swap(x, bit):
        return lax.ppermute(x, "expert", [(i, i ^ bit) for i in range(devices)])

    def after(x, *others):
        return lax.optimization_barrier((x, *others))[0]

    def spread(block):
        pieces, bit = [], far // 2
        while bit:
            pieces.append(swap(block, bit))
            block = jnp.concatenate([block, pieces[-1]], axis=0)
            bit //= 2
        return pieces

    ids = expert_ids.T
    own, *sends = pack(group, ids, activations, norm_gain)
    far_own = swap(own, far)
    arrivals = [shift(sends[0], 1), shift(sends[1], 3)]
    for j in range(HALVES):
        arrivals.append(shift(after(sends[2 + j], arrivals[j]), 2))
    now = [fetch(w_gate, 0, part, own), fetch(w_up, 0, part, arrivals[1])]
    passed = [swap(after(arrivals[0], far_own), far)]
    for j in range(1, len(arrivals)):
        passed.append(swap(after(arrivals[j], arrivals[j - 1]), far))
    head = [own, *arrivals[:2], far_own, *passed[:2]]
    head += spread(after(jnp.concatenate(head, axis=0), *now, *arrivals[2:]))
    totals = []
    for k in range(HALVES):
        tail = [arrivals[2 + k], passed[2 + k]]
        tail += spread(jnp.concatenate(tail, axis=0))
        later = [w_down] if k == HALVES - 1 else [w_gate, w_up]
        now, totals = gate_up(k, head + tail, now, later, totals)
    hidden, (down_w,) = totals[0], now
    held = []
    for k in range(HALVES):
        keep, send = down(k * part, part, hidden, down_w)
        bit = 1
        while bit < far:
            total = added(keep, swap(send, bit))
            bit *= 2
            if bit < far:
                count = total.shape[0] // 8
                groups = [total[: 3 * count], total[3 * count : 6 * count]]
                groups += [total[6 * count : 7 * count], total[7 * count :]]
                keep = jnp.concatenate(groups[0::2], axis=0)
                send = jnp.concatenate(groups[1::2], axis=0)
        held.append([total[j * CAP : (j + 1) * CAP] for j in range(2 * EXPERTS)])
    crossed = [swap(h[7], far) for h in held]
    middle = [shift(added(h[6], x), -2) for h, x in zip(held, crossed)]
    mine = [jnp.concatenate([h[j] for h in held], axis=1) for j in range(6)]
    crossed.append(swap(after(mine[4], crossed[0]), far))
    crossed.append(swap(after(mine[5], crossed[1]), far))
    near = shift(added(mine[1], crossed[2]), -1)
    last = shift(added(mine[2], crossed[3]), -3)
    arrived = swap(after(mine[3], crossed[2]), far)
    pieces = [arrived, near, last, *[h[0] for h in held], *middle]
    return mix(group, ids, route_logits.T, activations, pieces)


def solution(mesh):
    in_specs = (
        P(("parts", "expert"), None),
        P(("parts", "expert"), None),
        P(("parts", "expert"), None),
        P(),
        P("expert", None),
        P("expert", None),
        P("expert", None),
    )
    out_specs = P(("parts", "expert"), None)
    return jax.shard_map(
        on_device, mesh=mesh, in_specs=in_specs, out_specs=out_specs, check_vma=False
    )
```

```python
import functools

import jax
import jax.numpy as jnp
from jax import lax
from jax.experimental import pallas as pl
from jax.experimental.pallas import tpu as pltpu
from jax.sharding import PartitionSpec as P

EXPERTS = 4
CAP = 16
HALVES = 2
BLOCK = 1024
FETCH_ROWS = 144
MIB = 1 << 20
LIMIT = pltpu.CompilerParams(vmem_limit_bytes=16 * MIB)
VMEM = pl.BlockSpec(memory_space=pltpu.VMEM)
ANY = pl.BlockSpec(memory_space=pl.ANY)


def choices(ids, plane):
    tokens = ids.shape[1]
    line = lax.broadcasted_iota(jnp.int32, (EXPERTS * CAP, tokens), 0)
    expert = lax.rem(line // CAP + plane, EXPERTS)
    slot = (line % CAP).astype(jnp.float32)
    first = ids[0:1, :] == expert
    second = ids[1:2, :] == expert
    named = (first | second).astype(jnp.float32)
    square = (tokens, tokens)
    earlier = lax.broadcasted_iota(jnp.int32, square, 0) < lax.broadcasted_iota(
        jnp.int32, square, 1
    )
    rank = jnp.dot(named, earlier.astype(jnp.float32), preferred_element_type=jnp.float32)
    here = rank == slot
    return first & here, second & here


def pack_kernel(group, ids_ref, act_ref, gain_ref, *out_refs):
    plane = lax.axis_index("expert") // group
    values = act_ref[...].astype(jnp.float32)
    mean_sq = jnp.mean(values * values, axis=-1, keepdims=True)
    normed = (values * lax.rsqrt(mean_sq + 1e-06) * gain_ref[...]).astype(jnp.bfloat16)
    first, second = choices(ids_ref[...], plane)
    pick = (first | second).astype(jnp.float32).astype(jnp.bfloat16)
    rows = jnp.dot(pick, normed, preferred_element_type=jnp.float32).astype(jnp.bfloat16)
    for s, out_ref in zip((0, 1, 3), out_refs):
        out_ref[...] = rows[s * CAP : (s + 1) * CAP]
    part = out_refs[-1].shape[1]
    for k, out_ref in enumerate(out_refs[3:]):
        out_ref[...] = rows[2 * CAP : 3 * CAP, k * part : (k + 1) * part]


def pack(group, ids, activations, gain):
    width = activations.shape[1]
    widths = [width] * 3 + [width // HALVES] * HALVES
    operands = [ids, activations, gain.reshape(1, width)]
    return pl.pallas_call(
        functools.partial(pack_kernel, group),
        grid=(1,),
        in_specs=[pl.BlockSpec(x.shape, lambda i: (0, 0)) for x in operands],
        out_specs=[pl.BlockSpec((CAP, n), lambda i: (0, 0)) for n in widths],
        out_shape=[jax.ShapeDtypeStruct((CAP, n), jnp.bfloat16) for n in widths],
        compiler_params=LIMIT,
        name="norm_and_pack",
    )(*[pltpu.with_memory_space_constraint(x, pltpu.HBM) for x in operands])


def fetches(weights, at, held, sems):
    copies = []
    for j, w in enumerate(weights):
        part = held[j].shape[1]
        for b in range(sems.shape[1]):
            rows = pl.ds(b * FETCH_ROWS, FETCH_ROWS)
            copies.append(
                pltpu.make_async_copy(w.at[rows, at : at + part], held[j].at[rows], sems.at[j, b])
            )
    return copies


def fetch_kernel(at, w_ref, after_ref, held_ref, sems):
    copies = fetches([w_ref], at, [held_ref], sems)
    for copy in copies:
        copy.start()
    for copy in copies:
        copy.wait()


def fetch(w, at, part, after):
    rows = w.shape[0]
    return pl.pallas_call(
        functools.partial(fetch_kernel, at),
        in_specs=[ANY, ANY],
        out_specs=VMEM,
        out_shape=pltpu.VMEM((rows, part), jnp.bfloat16),
        scratch_shapes=[pltpu.SemaphoreType.DMA((1, rows // FETCH_ROWS))],
        compiler_params=LIMIT,
        cost_estimate=pl.CostEstimate(flops=0, bytes_accessed=4 * rows * part, transcendentals=0),
        name="fetch",
    )(pltpu.with_memory_space_constraint(w, pltpu.HBM), after)


def gate_up_kernel(count, ahead, at, begin, end, *refs):
    pieces, refs = refs[:count], refs[count:]
    weights, later, refs = refs[:2], refs[2 : 2 + ahead], refs[2 + ahead :]
    if not begin:
        before, refs = refs[:2], refs[2:]
    held, refs = refs[:ahead], refs[ahead:]
    turned, sems, refs = *refs[-2:], refs[:-2]
    if end:
        hidden_ref, refs = refs[0], refs[1:]
    sums = refs
    steps, block, _ = turned.shape
    copies = fetches(later, 0 if end else steps * block, held, sems)
    for copy in copies:
        copy.start()

    @pl.loop(0, steps)
    def _(c):
        parts = []
        for p in pieces:
            first = at if p.shape[1] > steps * block else 0
            parts.append(p[:, pl.ds(pl.multiple_of(first + c * block, block), block)])
        turned[c] = jnp.concatenate(parts, axis=0).T

    for j in range(2):
        sums[j][...] = jnp.zeros_like(sums[j]) if begin else before[j][...]

    @pl.loop(0, steps)
    def _(c):
        columns = pl.ds(pl.multiple_of(c * block, block), block)
        for j in range(2):
            sums[j][...] += jnp.dot(
                weights[j][:, columns], turned[c], preferred_element_type=jnp.float32
            )

    if end:
        hidden = (jax.nn.silu(sums[0][...]) * sums[1][...]).astype(jnp.bfloat16)
        hidden_ref[...] = hidden.T
    for copy in copies:
        copy.wait()


def gate_up(k, pieces, weights, later, totals):
    hidden, part = weights[0].shape
    begin, end = k == 0, k == HALVES - 1
    rows = sum(p.shape[0] for p in pieces)
    total = jax.ShapeDtypeStruct((hidden, rows), jnp.float32)
    width = later[0].shape[1] if end else part
    out_shape = [pltpu.VMEM((hidden, width), jnp.bfloat16)] * len(later)
    out_specs = [VMEM] * len(later)
    scratch = []
    if end:
        out_shape.append(jax.ShapeDtypeStruct((rows, hidden), jnp.bfloat16))
        scratch += [pltpu.VMEM((hidden, rows), jnp.float32)] * 2
    else:
        out_shape += [total] * 2
    out_specs += [VMEM] * (len(out_shape) - len(later))
    scratch.append(pltpu.VMEM((part // BLOCK, BLOCK, rows), jnp.bfloat16))
    scratch.append(pltpu.SemaphoreType.DMA((len(later), hidden // FETCH_ROWS)))
    weights = [pltpu.with_memory_space_constraint(w, pltpu.VMEM) for w in weights]
    later = [pltpu.with_memory_space_constraint(w, pltpu.HBM) for w in later]
    out = pl.pallas_call(
        functools.partial(gate_up_kernel, len(pieces), len(later), k * part, begin, end),
        in_specs=[VMEM] * (len(pieces) + 2) + [ANY] * len(later) + [VMEM] * len(totals),
        out_specs=out_specs,
        out_shape=out_shape,
        scratch_shapes=scratch,
        compiler_params=LIMIT,
        cost_estimate=pl.CostEstimate(
            flops=4 * rows * hidden * part,
            bytes_accessed=4 * hidden * part + 8 * rows * hidden,
            transcendentals=0,
        ),
        name="gate_up",
    )(*pieces, *weights, *later, *totals)
    return out[: len(later)], out[len(later) :]


def down_kernel(at, hidden_ref, w_ref, keep_ref, send_ref):
    half, part = keep_ref.shape
    first = 3 * half // 4
    block = BLOCK // 2

    @pl.loop(0, part // block)
    def _(c):
        columns = pl.ds(pl.multiple_of(at + c * block, block), block)
        out = jnp.dot(hidden_ref[...], w_ref[:, columns], preferred_element_type=jnp.float32)
        out = out.astype(jnp.bfloat16)
        columns = pl.ds(pl.multiple_of(c * block, block), block)
        for j, ref in enumerate((keep_ref, send_ref)):
            ref[:first, columns] = out[j * first : (j + 1) * first]
            far_rows = out[2 * first :]
            ref[first:, columns] = far_rows[j * (half - first) : (j + 1) * (half - first)]


def down(at, part, hidden, w_down):
    rows, depth = hidden.shape
    return pl.pallas_call(
        functools.partial(down_kernel, at),
        in_specs=[VMEM, VMEM],
        out_shape=[jax.ShapeDtypeStruct((rows // 2, part), jnp.bfloat16)] * 2,
        compiler_params=LIMIT,
        cost_estimate=pl.CostEstimate(
            flops=2 * rows * depth * part,
            bytes_accessed=2 * (depth * part + rows * depth + rows * part),
            transcendentals=0,
        ),
        name="down",
    )(hidden, pltpu.with_memory_space_constraint(w_down, pltpu.VMEM))


def mix_kernel(group, ids_ref, logits_ref, act_ref, arrived, near, last, *refs):
    out_ref, kept, middle_rows = refs[-1], refs[:HALVES], refs[HALVES:-1]
    plane = lax.axis_index("expert") // group
    first, second = choices(ids_ref[...], plane)
    lead = logits_ref[0:1, :] - logits_ref[1:2, :]
    weight = jnp.where(first, jax.nn.sigmoid(lead), 0.0)
    weight = (weight + jnp.where(second, jax.nn.sigmoid(-lead), 0.0)).T
    high = weight.astype(jnp.bfloat16)
    rest = weight - high.astype(jnp.float32)
    middle = rest.astype(jnp.bfloat16)
    low = (rest - middle.astype(jnp.float32)).astype(jnp.bfloat16)
    part = kept[0].shape[1]
    for k in range(HALVES):
        columns = slice(k * part, (k + 1) * part)
        own = kept[k][...].astype(jnp.float32) + arrived[:, columns].astype(jnp.float32)
        blocks = [own.astype(jnp.bfloat16), near[:, columns], middle_rows[k][...]]
        rows = jnp.concatenate(blocks + [last[:, columns]], axis=0)
        total = act_ref[:, columns].astype(jnp.float32)
        for term in (low, middle, high):
            total = total + jnp.dot(term, rows, preferred_element_type=jnp.float32)
        out_ref[:, columns] = total.astype(jnp.bfloat16)


def mix(group, ids, logits, activations, pieces):
    return pl.pallas_call(
        functools.partial(mix_kernel, group),
        out_shape=jax.ShapeDtypeStruct(activations.shape, jnp.bfloat16),
        compiler_params=LIMIT,
        name="mix",
    )(ids, logits, activations, *pieces)


def added(mine, arrived):
    total = mine.astype(jnp.float32) + arrived.astype(jnp.float32)
    return total.astype(jnp.bfloat16)


def on_device(activations, expert_ids, route_logits, norm_gain, w_gate, w_up, w_down):
    devices = lax.axis_size("expert")
    group = devices // EXPERTS
    far = group // 2
    width = activations.shape[1]
    part = width // HALVES

    def shift(x, s):
        return lax.ppermute(
            x, "expert", [(i, (i + s * group) % devices) for i in range(devices)]
        )

    def swap(x, bit):
        return lax.ppermute(x, "expert", [(i, i ^ bit) for i in range(devices)])

    def after(x, *others):
        return lax.optimization_barrier((x, *others))[0]

    def spread(block):
        pieces, bit = [], far // 2
        while bit:
            pieces.append(swap(block, bit))
            block = jnp.concatenate([block, pieces[-1]], axis=0)
            bit //= 2
        return pieces

    ids = expert_ids.T
    own, *sends = pack(group, ids, activations, norm_gain)
    far_own = swap(own, far)
    arrivals = [shift(sends[0], 1), shift(sends[1], 3)]
    now = [fetch(w_gate, 0, part, own), fetch(w_up, 0, part, own)]
    for j in range(HALVES):
        arrivals.append(shift(after(sends[2 + j], arrivals[1], now[1]), 2))
    passed = [swap(after(arrivals[0], far_own), far), swap(arrivals[1], far)]
    for j in range(2, len(arrivals)):
        passed.append(swap(after(arrivals[j], arrivals[j - 1]), far))
    head = [own, *arrivals[:2], far_own, *passed[:2]]
    head += spread(after(jnp.concatenate(head, axis=0), *now, passed[2], arrivals[3]))
    totals = []
    for k in range(HALVES):
        tail = [arrivals[2 + k], passed[2 + k]]
        tail += spread(jnp.concatenate(tail, axis=0))
        later = [w_down] if k == HALVES - 1 else [w_gate, w_up]
        now, totals = gate_up(k, head + tail, now, later, totals)
    hidden, (down_w,) = totals[0], now
    held = []
    for k in range(HALVES):
        keep, send = down(k * part, part, hidden, down_w)
        bit = 1
        while bit < far:
            total = added(keep, swap(send, bit))
            bit *= 2
            if bit < far:
                count = total.shape[0] // 8
                groups = [total[: 3 * count], total[3 * count : 6 * count]]
                groups += [total[6 * count : 7 * count], total[7 * count :]]
                keep = jnp.concatenate(groups[0::2], axis=0)
                send = jnp.concatenate(groups[1::2], axis=0)
        held.append([total[j * CAP : (j + 1) * CAP] for j in range(2 * EXPERTS)])
    crossed = [swap(h[7], far) for h in held]
    middle = [shift(added(h[6], x), -2) for h, x in zip(held, crossed)]
    mine = [jnp.concatenate([h[j] for h in held], axis=1) for j in range(6)]
    crossed.append(swap(mine[4], far))
    crossed.append(swap(mine[5], far))
    near = shift(after(added(mine[1], crossed[2]), crossed[1]), -1)
    last = shift(added(mine[2], crossed[3]), -3)
    arrived = swap(after(mine[3], crossed[2]), far)
    pieces = [arrived, near, last, *[h[0] for h in held], *middle]
    return mix(group, ids, route_logits.T, activations, pieces)


def solution(mesh):
    in_specs = (
        P(("parts", "expert"), None),
        P(("parts", "expert"), None),
        P(("parts", "expert"), None),
        P(),
        P("expert", None),
        P("expert", None),
        P("expert", None),
    )
    out_specs = P(("parts", "expert"), None)
    return jax.shard_map(
        on_device, mesh=mesh, in_specs=in_specs, out_specs=out_specs, check_vma=False
    )
```

```python
import functools

import jax
import jax.numpy as jnp
from jax import lax
from jax.experimental import pallas as pl
from jax.experimental.pallas import tpu as pltpu
from jax.sharding import PartitionSpec as P

EXPERTS = 4
CAP = 16
HALVES = 2
BLOCK = 1024
FETCH_ROWS = 144
MIB = 1 << 20
LIMIT = pltpu.CompilerParams(vmem_limit_bytes=16 * MIB)
VMEM = pl.BlockSpec(memory_space=pltpu.VMEM)
ANY = pl.BlockSpec(memory_space=pl.ANY)


def choices(ids, plane):
    tokens = ids.shape[1]
    line = lax.broadcasted_iota(jnp.int32, (EXPERTS * CAP, tokens), 0)
    expert = lax.rem(line // CAP + plane, EXPERTS)
    slot = (line % CAP).astype(jnp.float32)
    first = ids[0:1, :] == expert
    second = ids[1:2, :] == expert
    named = (first | second).astype(jnp.float32)
    square = (tokens, tokens)
    earlier = lax.broadcasted_iota(jnp.int32, square, 0) < lax.broadcasted_iota(
        jnp.int32, square, 1
    )
    rank = jnp.dot(named, earlier.astype(jnp.float32), preferred_element_type=jnp.float32)
    here = rank == slot
    return first & here, second & here


def pack_kernel(group, ids_ref, act_ref, gain_ref, *out_refs):
    plane = lax.axis_index("expert") // group
    values = act_ref[...].astype(jnp.float32)
    mean_sq = jnp.mean(values * values, axis=-1, keepdims=True)
    normed = (values * lax.rsqrt(mean_sq + 1e-06) * gain_ref[...]).astype(jnp.bfloat16)
    first, second = choices(ids_ref[...], plane)
    pick = (first | second).astype(jnp.float32).astype(jnp.bfloat16)
    rows = jnp.dot(pick, normed, preferred_element_type=jnp.float32).astype(jnp.bfloat16)
    out_refs[0][...] = rows[:CAP]
    part = out_refs[-1].shape[1]
    for j, out_ref in enumerate(out_refs[1:]):
        k, s = j // (EXPERTS - 1), j % (EXPERTS - 1) + 1
        out_ref[...] = rows[s * CAP : (s + 1) * CAP, k * part : (k + 1) * part]


def pack(group, ids, activations, gain):
    width = activations.shape[1]
    widths = [width] + [width // HALVES] * (HALVES * (EXPERTS - 1))
    operands = [ids, activations, gain.reshape(1, width)]
    return pl.pallas_call(
        functools.partial(pack_kernel, group),
        grid=(1,),
        in_specs=[pl.BlockSpec(x.shape, lambda i: (0, 0)) for x in operands],
        out_specs=[pl.BlockSpec((CAP, n), lambda i: (0, 0)) for n in widths],
        out_shape=[jax.ShapeDtypeStruct((CAP, n), jnp.bfloat16) for n in widths],
        compiler_params=LIMIT,
        name="norm_and_pack",
    )(*[pltpu.with_memory_space_constraint(x, pltpu.HBM) for x in operands])


def fetches(weights, at, held, sems):
    copies = []
    for j, w in enumerate(weights):
        part = held[j].shape[1]
        for b in range(sems.shape[1]):
            rows = pl.ds(b * FETCH_ROWS, FETCH_ROWS)
            copies.append(
                pltpu.make_async_copy(w.at[rows, at : at + part], held[j].at[rows], sems.at[j, b])
            )
    return copies


def fetch_kernel(at, w_ref, after_ref, held_ref, sems):
    copies = fetches([w_ref], at, [held_ref], sems)
    for copy in copies:
        copy.start()
    for copy in copies:
        copy.wait()


def fetch(w, at, part, after):
    rows = w.shape[0]
    return pl.pallas_call(
        functools.partial(fetch_kernel, at),
        in_specs=[ANY, ANY],
        out_specs=VMEM,
        out_shape=pltpu.VMEM((rows, part), jnp.bfloat16),
        scratch_shapes=[pltpu.SemaphoreType.DMA((1, rows // FETCH_ROWS))],
        compiler_params=LIMIT,
        cost_estimate=pl.CostEstimate(flops=0, bytes_accessed=4 * rows * part, transcendentals=0),
        name="fetch",
    )(pltpu.with_memory_space_constraint(w, pltpu.HBM), after)


def gate_up_kernel(count, ahead, at, begin, end, *refs):
    pieces, refs = refs[:count], refs[count:]
    weights, later, refs = refs[:2], refs[2 : 2 + ahead], refs[2 + ahead :]
    if not begin:
        before, refs = refs[:2], refs[2:]
    held, refs = refs[:ahead], refs[ahead:]
    turned, sems, refs = *refs[-2:], refs[:-2]
    if end:
        hidden_ref, refs = refs[0], refs[1:]
    sums = refs
    steps, block, _ = turned.shape
    copies = fetches(later, 0 if end else steps * block, held, sems)
    for copy in copies:
        copy.start()

    @pl.loop(0, steps)
    def _(c):
        parts = []
        for p in pieces:
            first = at if p.shape[1] > steps * block else 0
            parts.append(p[:, pl.ds(pl.multiple_of(first + c * block, block), block)])
        turned[c] = jnp.concatenate(parts, axis=0).T

    for j in range(2):
        sums[j][...] = jnp.zeros_like(sums[j]) if begin else before[j][...]

    @pl.loop(0, steps)
    def _(c):
        columns = pl.ds(pl.multiple_of(c * block, block), block)
        for j in range(2):
            sums[j][...] += jnp.dot(
                weights[j][:, columns], turned[c], preferred_element_type=jnp.float32
            )

    if end:
        hidden = (jax.nn.silu(sums[0][...]) * sums[1][...]).astype(jnp.bfloat16)
        hidden_ref[...] = hidden.T
    for copy in copies:
        copy.wait()


def gate_up(k, pieces, weights, later, totals):
    hidden, part = weights[0].shape
    begin, end = k == 0, k == HALVES - 1
    rows = sum(p.shape[0] for p in pieces)
    total = jax.ShapeDtypeStruct((hidden, rows), jnp.float32)
    width = later[0].shape[1] if end else part
    out_shape = [pltpu.VMEM((hidden, width), jnp.bfloat16)] * len(later)
    out_specs = [VMEM] * len(later)
    scratch = []
    if end:
        out_shape.append(jax.ShapeDtypeStruct((rows, hidden), jnp.bfloat16))
        scratch += [pltpu.VMEM((hidden, rows), jnp.float32)] * 2
    else:
        out_shape += [total] * 2
    out_specs += [VMEM] * (len(out_shape) - len(later))
    scratch.append(pltpu.VMEM((part // BLOCK, BLOCK, rows), jnp.bfloat16))
    scratch.append(pltpu.SemaphoreType.DMA((len(later), hidden // FETCH_ROWS)))
    weights = [pltpu.with_memory_space_constraint(w, pltpu.VMEM) for w in weights]
    later = [pltpu.with_memory_space_constraint(w, pltpu.HBM) for w in later]
    out = pl.pallas_call(
        functools.partial(gate_up_kernel, len(pieces), len(later), k * part, begin, end),
        in_specs=[VMEM] * (len(pieces) + 2) + [ANY] * len(later) + [VMEM] * len(totals),
        out_specs=out_specs,
        out_shape=out_shape,
        scratch_shapes=scratch,
        compiler_params=LIMIT,
        cost_estimate=pl.CostEstimate(
            flops=4 * rows * hidden * part,
            bytes_accessed=4 * hidden * part + 8 * rows * hidden,
            transcendentals=0,
        ),
        name="gate_up",
    )(*pieces, *weights, *later, *totals)
    return out[: len(later)], out[len(later) :]


def down_kernel(at, hidden_ref, w_ref, keep_ref, send_ref):
    half, part = keep_ref.shape
    block = BLOCK // 2

    @pl.loop(0, part // block)
    def _(c):
        columns = pl.ds(pl.multiple_of(at + c * block, block), block)
        out = jnp.dot(hidden_ref[...], w_ref[:, columns], preferred_element_type=jnp.float32)
        out = out.astype(jnp.bfloat16)
        columns = pl.ds(pl.multiple_of(c * block, block), block)
        keep_ref[:, columns] = out[:half]
        send_ref[:, columns] = out[half:]


def down(at, part, hidden, w_down):
    rows, depth = hidden.shape
    return pl.pallas_call(
        functools.partial(down_kernel, at),
        in_specs=[VMEM, VMEM],
        out_shape=[jax.ShapeDtypeStruct((rows // 2, part), jnp.bfloat16)] * 2,
        compiler_params=LIMIT,
        cost_estimate=pl.CostEstimate(
            flops=2 * rows * depth * part,
            bytes_accessed=2 * (depth * part + rows * depth + rows * part),
            transcendentals=0,
        ),
        name="down",
    )(hidden, pltpu.with_memory_space_constraint(w_down, pltpu.VMEM))


def mix_kernel(group, ids_ref, logits_ref, act_ref, arrived, near, last, *refs):
    out_ref, kept, middle_rows = refs[-1], refs[:HALVES], refs[HALVES:-1]
    plane = lax.axis_index("expert") // group
    first, second = choices(ids_ref[...], plane)
    lead = logits_ref[0:1, :] - logits_ref[1:2, :]
    weight = jnp.where(first, jax.nn.sigmoid(lead), 0.0)
    weight = (weight + jnp.where(second, jax.nn.sigmoid(-lead), 0.0)).T
    high = weight.astype(jnp.bfloat16)
    rest = weight - high.astype(jnp.float32)
    middle = rest.astype(jnp.bfloat16)
    low = (rest - middle.astype(jnp.float32)).astype(jnp.bfloat16)
    part = kept[0].shape[1]
    for k in range(HALVES):
        columns = slice(k * part, (k + 1) * part)
        own = kept[k][...].astype(jnp.float32) + arrived[:, columns].astype(jnp.float32)
        blocks = [own.astype(jnp.bfloat16), near[:, columns], middle_rows[k][...]]
        rows = jnp.concatenate(blocks + [last[:, columns]], axis=0)
        total = act_ref[:, columns].astype(jnp.float32)
        for term in (low, middle, high):
            total = total + jnp.dot(term, rows, preferred_element_type=jnp.float32)
        out_ref[:, columns] = total.astype(jnp.bfloat16)


def mix(group, ids, logits, activations, pieces):
    return pl.pallas_call(
        functools.partial(mix_kernel, group),
        out_shape=jax.ShapeDtypeStruct(activations.shape, jnp.bfloat16),
        compiler_params=LIMIT,
        name="mix",
    )(ids, logits, activations, *pieces)


def added(mine, arrived):
    total = mine.astype(jnp.float32) + arrived.astype(jnp.float32)
    return total.astype(jnp.bfloat16)


def on_device(activations, expert_ids, route_logits, norm_gain, w_gate, w_up, w_down):
    devices = lax.axis_size("expert")
    group = devices // EXPERTS
    far = group // 2
    width = activations.shape[1]
    part = width // HALVES

    def shift(x, s):
        return lax.ppermute(
            x, "expert", [(i, (i + s * group) % devices) for i in range(devices)]
        )

    def swap(x, bit):
        return lax.ppermute(x, "expert", [(i, i ^ bit) for i in range(devices)])

    def after(x, *others):
        return lax.optimization_barrier((x, *others))[0]

    others = EXPERTS - 1
    ids = expert_ids.T
    own, *sends = pack(group, ids, activations, norm_gain)
    far_own = swap(own, far)
    now = [fetch(w, 0, part, own) for w in (w_gate, w_up)]
    blocks, earlier = [], []
    for k in range(HALVES):
        arrivals = []
        for s in range(others):
            x = sends[k * others + s]
            arrivals.append(shift(after(x, *earlier, *now) if k else x, s + 1))
        earlier = arrivals
        blocks.append(jnp.concatenate(arrivals, axis=0))
    totals = []
    for k in range(HALVES):
        columns = slice(k * part, (k + 1) * part)
        far_block = swap(blocks[k], far)
        if totals:
            far_block, totals = lax.optimization_barrier((far_block, totals))
        pieces = [own[:, columns], blocks[k], far_own[:, columns], far_block]
        bit = far // 2
        while bit:
            pieces.append(swap(jnp.concatenate(pieces, axis=0), bit))
            bit //= 2
        pieces[0], pieces[2] = own, far_own
        if k < HALVES - 1:
            pieces[1] = after(pieces[1], blocks[k + 1])
        later = [w_down] if k == HALVES - 1 else [w_gate, w_up]
        now, totals = gate_up(k, pieces, now, later, totals)
    hidden, (down_w,) = totals[0], now
    held = []
    for k in range(HALVES):
        keep, send = down(k * part, part, hidden, down_w)
        bit = 1
        while bit < far:
            total = added(keep, swap(send, bit))
            keep, send = total[: total.shape[0] // 2], total[total.shape[0] // 2 :]
            bit *= 2
        held.append([total[j * CAP : (j + 1) * CAP] for j in range(2 * EXPERTS)])
    crossed = [swap(h[6], far) for h in held]
    middle = [shift(added(h[2], x), -2) for h, x in zip(held, crossed)]
    mine = [jnp.concatenate([h[j] for h in held], axis=1) for j in range(2 * EXPERTS)]
    back = {}
    for s, ready in ((1, []), (3, middle[:1]), (0, middle)):
        crossed.append(swap(after(mine[EXPERTS + s], *crossed, *ready), far))
        back[s] = crossed[-1]
    near = shift(added(mine[1], back[1]), -1)
    last = shift(added(mine[3], back[3]), -3)
    arrived = back[0]
    pieces = [arrived, near, last, *[h[0] for h in held], *middle]
    return mix(group, ids, route_logits.T, activations, pieces)


def solution(mesh):
    in_specs = (
        P(("parts", "expert"), None),
        P(("parts", "expert"), None),
        P(("parts", "expert"), None),
        P(),
        P("expert", None),
        P("expert", None),
        P("expert", None),
    )
    out_specs = P(("parts", "expert"), None)
    return jax.shard_map(
        on_device, mesh=mesh, in_specs=in_specs, out_specs=out_specs, check_vma=False
    )
```

```python
import functools

import jax
import jax.numpy as jnp
from jax import lax
from jax.experimental import pallas as pl
from jax.experimental.pallas import tpu as pltpu
from jax.sharding import PartitionSpec as P

EXPERTS = 4
CAP = 16
HALVES = 2
BLOCK = 1024
FETCH_ROWS = 144
MIB = 1 << 20
LIMIT = pltpu.CompilerParams(vmem_limit_bytes=10 * MIB)
WIDE = pltpu.CompilerParams(vmem_limit_bytes=32 * MIB)
VMEM = pl.BlockSpec(memory_space=pltpu.VMEM)
ANY = pl.BlockSpec(memory_space=pl.ANY)


def choices(ids, plane):
    tokens = ids.shape[1]
    line = lax.broadcasted_iota(jnp.int32, (EXPERTS * CAP, tokens), 0)
    expert = lax.rem(line // CAP + plane, EXPERTS)
    slot = (line % CAP).astype(jnp.float32)
    first = ids[0:1, :] == expert
    second = ids[1:2, :] == expert
    named = (first | second).astype(jnp.float32)
    square = (tokens, tokens)
    earlier = lax.broadcasted_iota(jnp.int32, square, 0) < lax.broadcasted_iota(
        jnp.int32, square, 1
    )
    rank = jnp.dot(named, earlier.astype(jnp.float32), preferred_element_type=jnp.float32)
    here = rank == slot
    return first & here, second & here


def pack_kernel(group, ids_ref, act_ref, gain_ref, *out_refs):
    plane = lax.axis_index("expert") // group
    values = act_ref[...].astype(jnp.float32)
    mean_sq = jnp.mean(values * values, axis=-1, keepdims=True)
    normed = (values * lax.rsqrt(mean_sq + 1e-06) * gain_ref[...]).astype(jnp.bfloat16)
    first, second = choices(ids_ref[...], plane)
    pick = (first | second).astype(jnp.float32).astype(jnp.bfloat16)
    rows = jnp.dot(pick, normed, preferred_element_type=jnp.float32).astype(jnp.bfloat16)
    out_refs[0][...] = rows[:CAP]
    part = out_refs[-1].shape[1]
    for j, out_ref in enumerate(out_refs[1:]):
        k, s = j // (EXPERTS - 1), j % (EXPERTS - 1) + 1
        out_ref[...] = rows[s * CAP : (s + 1) * CAP, k * part : (k + 1) * part]


def pack(group, ids, activations, gain):
    width = activations.shape[1]
    widths = [width] + [width // HALVES] * (HALVES * (EXPERTS - 1))
    operands = [ids, activations, gain.reshape(1, width)]
    return pl.pallas_call(
        functools.partial(pack_kernel, group),
        grid=(1,),
        in_specs=[pl.BlockSpec(x.shape, lambda i: (0, 0)) for x in operands],
        out_specs=[pl.BlockSpec((CAP, n), lambda i: (0, 0)) for n in widths],
        out_shape=[jax.ShapeDtypeStruct((CAP, n), jnp.bfloat16) for n in widths],
        compiler_params=LIMIT,
        name="norm_and_pack",
    )(*[pltpu.with_memory_space_constraint(x, pltpu.HBM) for x in operands])


def fetches(weights, at, held, sems):
    copies = []
    for j, w in enumerate(weights):
        part = held[j].shape[1]
        for b in range(sems.shape[1]):
            rows = pl.ds(b * FETCH_ROWS, FETCH_ROWS)
            copies.append(
                pltpu.make_async_copy(w.at[rows, at : at + part], held[j].at[rows], sems.at[j, b])
            )
    return copies


def fetch_kernel(at, w_ref, after_ref, held_ref, sems):
    copies = fetches([w_ref], at, [held_ref], sems)
    for copy in copies:
        copy.start()
    for copy in copies:
        copy.wait()


def fetch(w, at, part, after):
    rows = w.shape[0]
    return pl.pallas_call(
        functools.partial(fetch_kernel, at),
        in_specs=[ANY, ANY],
        out_specs=VMEM,
        out_shape=pltpu.VMEM((rows, part), jnp.bfloat16),
        scratch_shapes=[pltpu.SemaphoreType.DMA((1, rows // FETCH_ROWS))],
        compiler_params=LIMIT,
        cost_estimate=pl.CostEstimate(flops=0, bytes_accessed=4 * rows * part, transcendentals=0),
        name="fetch",
    )(pltpu.with_memory_space_constraint(w, pltpu.HBM), after)


def gate_up_kernel(count, ahead, at, ahead_at, begin, end, *refs):
    pieces, refs = refs[:count], refs[count:]
    weights, later, refs = refs[:2], refs[2 : 2 + ahead], refs[2 + ahead :]
    if not begin:
        before, refs = refs[:2], refs[2:]
    held, refs = refs[:ahead], refs[ahead:]
    turned, sems, refs = *refs[-2:], refs[:-2]
    if end:
        hidden_ref, refs = refs[0], refs[1:]
    sums = refs
    part, rows = turned.shape
    copies = fetches(later, ahead_at, held, sems)
    for copy in copies:
        copy.start()
    for c in range(0, part, BLOCK):
        parts = []
        for p in pieces:
            first = c + (at if p.shape[1] > part else 0)
            parts.append(p[:, first : first + BLOCK])
        turned[c : c + BLOCK, :] = jnp.concatenate(parts, axis=0).T
    for j in range(2):
        total = jnp.dot(weights[j][...], turned[...], preferred_element_type=jnp.float32)
        sums[j][...] = total if begin else total + before[j][...]
    if end:
        hidden = (jax.nn.silu(sums[0][...]) * sums[1][...]).astype(jnp.bfloat16)
        hidden_ref[...] = hidden.T
    for copy in copies:
        copy.wait()


def gate_up(k, pieces, weights, later, totals):
    hidden, part = weights[0].shape
    begin, end = k == 0, k == HALVES - 1
    rows = sum(p.shape[0] for p in pieces)
    total = jax.ShapeDtypeStruct((hidden, rows), jnp.float32)
    out_shape = [pltpu.VMEM((hidden, part), jnp.bfloat16)] * len(later)
    out_specs = [VMEM] * len(later)
    scratch = []
    if end:
        out_shape.append(jax.ShapeDtypeStruct((rows, hidden), jnp.bfloat16))
        scratch += [pltpu.VMEM((hidden, rows), jnp.float32)] * 2
    else:
        out_shape += [total] * 2
    out_specs += [VMEM] * (len(out_shape) - len(later))
    scratch.append(pltpu.VMEM((part, rows), jnp.bfloat16))
    scratch.append(pltpu.SemaphoreType.DMA((len(later), hidden // FETCH_ROWS)))
    weights = [pltpu.with_memory_space_constraint(w, pltpu.VMEM) for w in weights]
    later = [pltpu.with_memory_space_constraint(w, pltpu.HBM) for w in later]
    out = pl.pallas_call(
        functools.partial(
            gate_up_kernel, len(pieces), len(later), k * part, 0 if end else part, begin, end
        ),
        in_specs=[VMEM] * (len(pieces) + 2) + [ANY] * len(later) + [VMEM] * len(totals),
        out_specs=out_specs,
        out_shape=out_shape,
        scratch_shapes=scratch,
        compiler_params=LIMIT if rows <= 256 else WIDE,
        cost_estimate=pl.CostEstimate(
            flops=4 * rows * hidden * part,
            bytes_accessed=4 * hidden * part + 8 * rows * hidden,
            transcendentals=0,
        ),
        name="gate_up",
    )(*pieces, *weights, *later, *totals)
    return out[: len(later)], out[len(later) :]


def down_kernel(ahead, hidden_ref, w_ref, *refs):
    later, held, refs = refs[:ahead], refs[ahead : 2 * ahead], refs[2 * ahead :]
    keep_ref, send_ref, sems = refs
    half, part = keep_ref.shape
    copies = fetches(later, part, held, sems)
    for copy in copies:
        copy.start()
    for c in range(0, part, BLOCK):
        columns = slice(c, c + BLOCK)
        out = jnp.dot(hidden_ref[...], w_ref[:, columns], preferred_element_type=jnp.float32)
        out = out.astype(jnp.bfloat16)
        keep_ref[:, columns] = out[:half]
        send_ref[:, columns] = out[half:]
    for copy in copies:
        copy.wait()


def down(hidden, w_down, later):
    rows, depth = hidden.shape
    part = w_down.shape[1]
    ahead = len(later)
    out_shape = [pltpu.VMEM((depth, part), jnp.bfloat16)] * ahead
    out_shape += [jax.ShapeDtypeStruct((rows // 2, part), jnp.bfloat16)] * 2
    w_down = pltpu.with_memory_space_constraint(w_down, pltpu.VMEM)
    later = [pltpu.with_memory_space_constraint(w, pltpu.HBM) for w in later]
    out = pl.pallas_call(
        functools.partial(down_kernel, ahead),
        in_specs=[VMEM, VMEM] + [ANY] * ahead,
        out_specs=[VMEM] * (ahead + 2),
        out_shape=out_shape,
        scratch_shapes=[pltpu.SemaphoreType.DMA((max(ahead, 1), depth // FETCH_ROWS))],
        compiler_params=LIMIT if rows <= 256 else WIDE,
        cost_estimate=pl.CostEstimate(
            flops=2 * rows * depth * part,
            bytes_accessed=2 * (depth * part + rows * depth + rows * part),
            transcendentals=0,
        ),
        name="down",
    )(hidden, w_down, *later)
    return out[:ahead], out[ahead:]


def mix_kernel(group, ids_ref, logits_ref, act_ref, arrived, near, last, *refs):
    out_ref, kept, middle_rows = refs[-1], refs[:HALVES], refs[HALVES:-1]
    plane = lax.axis_index("expert") // group
    first, second = choices(ids_ref[...], plane)
    lead = logits_ref[0:1, :] - logits_ref[1:2, :]
    weight = jnp.where(first, jax.nn.sigmoid(lead), 0.0)
    weight = (weight + jnp.where(second, jax.nn.sigmoid(-lead), 0.0)).T
    tokens = weight.shape[0]
    high = weight.astype(jnp.bfloat16).astype(jnp.float32)
    middle = (weight - high).astype(jnp.bfloat16).astype(jnp.float32)
    terms = jnp.concatenate([weight - high - middle, middle, high], axis=0).astype(jnp.bfloat16)
    part = kept[0].shape[1]
    for k in range(HALVES):
        columns = slice(k * part, (k + 1) * part)
        own = kept[k][...].astype(jnp.float32) + arrived[:, columns].astype(jnp.float32)
        blocks = [own.astype(jnp.bfloat16), near[:, columns], middle_rows[k][...]]
        rows = jnp.concatenate(blocks + [last[:, columns]], axis=0)
        sums = jnp.dot(terms, rows, preferred_element_type=jnp.float32)
        total = act_ref[:, columns].astype(jnp.float32)
        for j in range(3):
            total = total + sums[j * tokens : (j + 1) * tokens]
        out_ref[:, columns] = total.astype(jnp.bfloat16)


def mix(group, ids, logits, activations, pieces):
    return pl.pallas_call(
        functools.partial(mix_kernel, group),
        out_shape=jax.ShapeDtypeStruct(activations.shape, jnp.bfloat16),
        compiler_params=LIMIT,
        name="mix",
    )(ids, logits, activations, *pieces)


def added(mine, arrived):
    total = mine.astype(jnp.float32) + arrived.astype(jnp.float32)
    return total.astype(jnp.bfloat16)


def on_device(activations, expert_ids, route_logits, norm_gain, w_gate, w_up, w_down):
    devices = lax.axis_size("expert")
    group = devices // EXPERTS
    far = group // 2
    width = activations.shape[1]
    part = width // HALVES

    def shift(x, s):
        return lax.ppermute(
            x, "expert", [(i, (i + s * group) % devices) for i in range(devices)]
        )

    def swap(x, bit):
        return lax.ppermute(x, "expert", [(i, i ^ bit) for i in range(devices)])

    def after(x, *others):
        return lax.optimization_barrier((x, *others))[0]

    others = EXPERTS - 1
    ids = expert_ids.T
    own, *sends = pack(group, ids, activations, norm_gain)
    far_own = swap(own, far)
    now = [fetch(w, 0, part, own) for w in (w_gate, w_up)]
    blocks, earlier = [], []
    for k in range(HALVES):
        arrivals = []
        for s in range(others):
            x = sends[k * others + s]
            arrivals.append(shift(after(x, *earlier, *now) if k else x, s + 1))
        earlier = arrivals
        blocks.append(jnp.concatenate(arrivals, axis=0))
    totals = []
    for k in range(HALVES):
        columns = slice(k * part, (k + 1) * part)
        far_block = swap(blocks[k], far)
        if totals:
            far_block, totals = lax.optimization_barrier((far_block, totals))
        pieces = [own[:, columns], blocks[k], far_own[:, columns], far_block]
        bit = far // 2
        while bit:
            pieces.append(swap(jnp.concatenate(pieces, axis=0), bit))
            bit //= 2
        pieces[0], pieces[2] = own, far_own
        if k < HALVES - 1:
            pieces[1] = after(pieces[1], blocks[k + 1])
        later = [w_down] if k == HALVES - 1 else [w_gate, w_up]
        now, totals = gate_up(k, pieces, now, later, totals)
    hidden = totals[0]
    held = []
    for k in range(HALVES):
        later = [w_down] if k < HALVES - 1 else []
        now, (keep, send) = down(hidden, now[0], later)
        bit = 1
        while bit < far:
            total = added(keep, swap(send, bit))
            keep, send = total[: total.shape[0] // 2], total[total.shape[0] // 2 :]
            bit *= 2
        held.append([total[j * CAP : (j + 1) * CAP] for j in range(2 * EXPERTS)])
    crossed = [swap(h[6], far) for h in held]
    middle = [shift(added(h[2], x), -2) for h, x in zip(held, crossed)]
    mine = [jnp.concatenate([h[j] for h in held], axis=1) for j in range(2 * EXPERTS)]
    back = {}
    for s, ready in ((1, []), (3, []), (0, middle)):
        crossed.append(swap(after(mine[EXPERTS + s], *crossed, *ready), far))
        back[s] = crossed[-1]
    near = shift(added(mine[1], back[1]), -1)
    last = shift(added(mine[3], back[3]), -3)
    arrived = back[0]
    pieces = [arrived, near, last, *[h[0] for h in held], *middle]
    return mix(group, ids, route_logits.T, activations, pieces)


def solution(mesh):
    in_specs = (
        P(("parts", "expert"), None),
        P(("parts", "expert"), None),
        P(("parts", "expert"), None),
        P(),
        P("expert", None),
        P("expert", None),
        P("expert", None),
    )
    out_specs = P(("parts", "expert"), None)
    return jax.shard_map(
        on_device, mesh=mesh, in_specs=in_specs, out_specs=out_specs, check_vma=False
    )
```

```python
import functools

import jax
import jax.numpy as jnp
from jax import lax
from jax.experimental import pallas as pl
from jax.experimental.pallas import tpu as pltpu
from jax.sharding import PartitionSpec as P

EXPERTS = 4
CAP = 16
HALVES = 2
BLOCK = 1024
FETCH_ROWS = 144
MIB = 1 << 20
LIMIT = pltpu.CompilerParams(vmem_limit_bytes=10 * MIB)
WIDE = pltpu.CompilerParams(vmem_limit_bytes=32 * MIB)
VMEM = pl.BlockSpec(memory_space=pltpu.VMEM)
ANY = pl.BlockSpec(memory_space=pl.ANY)


def choices(ids, plane):
    tokens = ids.shape[1]
    line = lax.broadcasted_iota(jnp.int32, (EXPERTS * CAP, tokens), 0)
    expert = lax.rem(line // CAP + plane, EXPERTS)
    slot = (line % CAP).astype(jnp.float32)
    first = ids[0:1, :] == expert
    second = ids[1:2, :] == expert
    named = (first | second).astype(jnp.float32)
    square = (tokens, tokens)
    earlier = lax.broadcasted_iota(jnp.int32, square, 0) < lax.broadcasted_iota(
        jnp.int32, square, 1
    )
    rank = jnp.dot(named, earlier.astype(jnp.float32), preferred_element_type=jnp.float32)
    here = rank == slot
    return first & here, second & here


def pack_kernel(group, ids_ref, act_ref, gain_ref, *out_refs):
    plane = lax.axis_index("expert") // group
    values = act_ref[...].astype(jnp.float32)
    mean_sq = jnp.mean(values * values, axis=-1, keepdims=True)
    normed = (values * lax.rsqrt(mean_sq + 1e-06) * gain_ref[...]).astype(jnp.bfloat16)
    first, second = choices(ids_ref[...], plane)
    pick = (first | second).astype(jnp.float32).astype(jnp.bfloat16)
    rows = jnp.dot(pick, normed, preferred_element_type=jnp.float32).astype(jnp.bfloat16)
    out_refs[0][...] = rows[:CAP]
    part = out_refs[-1].shape[1]
    for j, out_ref in enumerate(out_refs[1:]):
        k, s = j // (EXPERTS - 1), j % (EXPERTS - 1) + 1
        out_ref[...] = rows[s * CAP : (s + 1) * CAP, k * part : (k + 1) * part]


def pack(group, ids, activations, gain):
    width = activations.shape[1]
    widths = [width] + [width // HALVES] * (HALVES * (EXPERTS - 1))
    operands = [ids, activations, gain.reshape(1, width)]
    return pl.pallas_call(
        functools.partial(pack_kernel, group),
        grid=(1,),
        in_specs=[pl.BlockSpec(x.shape, lambda i: (0, 0)) for x in operands],
        out_specs=[pl.BlockSpec((CAP, n), lambda i: (0, 0)) for n in widths],
        out_shape=[jax.ShapeDtypeStruct((CAP, n), jnp.bfloat16) for n in widths],
        compiler_params=LIMIT,
        name="norm_and_pack",
    )(*[pltpu.with_memory_space_constraint(x, pltpu.HBM) for x in operands])


def fetches(weights, at, held, sems):
    copies = []
    for j, w in enumerate(weights):
        part = held[j].shape[1]
        for b in range(sems.shape[1]):
            rows = pl.ds(b * FETCH_ROWS, FETCH_ROWS)
            copies.append(
                pltpu.make_async_copy(w.at[rows, at : at + part], held[j].at[rows], sems.at[j, b])
            )
    return copies


def fetch_kernel(at, w_ref, after_ref, held_ref, sems):
    copies = fetches([w_ref], at, [held_ref], sems)
    for copy in copies:
        copy.start()
    for copy in copies:
        copy.wait()


def fetch(w, at, part, after):
    rows = w.shape[0]
    return pl.pallas_call(
        functools.partial(fetch_kernel, at),
        in_specs=[ANY, ANY],
        out_specs=VMEM,
        out_shape=pltpu.VMEM((rows, part), jnp.bfloat16),
        scratch_shapes=[pltpu.SemaphoreType.DMA((1, rows // FETCH_ROWS))],
        compiler_params=LIMIT,
        cost_estimate=pl.CostEstimate(flops=0, bytes_accessed=4 * rows * part, transcendentals=0),
        name="fetch",
    )(pltpu.with_memory_space_constraint(w, pltpu.HBM), after)


def relay_kernel(count, *refs):
    for x_ref, out_ref in zip(refs[:count], refs[count + 1 :]):
        out_ref[...] = x_ref[...]


def relay(arrays, after):
    count = len(arrays)
    return pl.pallas_call(
        functools.partial(relay_kernel, count),
        in_specs=[VMEM] * count + [ANY],
        out_specs=[VMEM] * count,
        out_shape=[jax.ShapeDtypeStruct(x.shape, x.dtype) for x in arrays],
        compiler_params=LIMIT,
        cost_estimate=pl.CostEstimate(flops=0, bytes_accessed=16 * MIB, transcendentals=0),
        name="relay",
    )(*arrays, after)


def gate_up_kernel(count, ahead, at, ahead_at, begin, end, *refs):
    pieces, refs = refs[:count], refs[count:]
    weights, later, refs = refs[:2], refs[2 : 2 + ahead], refs[2 + ahead :]
    if not begin:
        before, refs = refs[:2], refs[2:]
    held, refs = refs[:ahead], refs[ahead:]
    turned, sems, refs = *refs[-2:], refs[:-2]
    if end:
        hidden_ref, refs = refs[0], refs[1:]
    sums = refs
    part, rows = turned.shape
    copies = fetches(later, ahead_at, held, sems)
    for copy in copies:
        copy.start()

    @pl.loop(0, part // BLOCK)
    def _(c):
        parts = []
        for p in pieces:
            first = c * BLOCK + (at if p.shape[1] > part else 0)
            parts.append(p[:, pl.ds(pl.multiple_of(first, BLOCK), BLOCK)])
        turned[pl.ds(pl.multiple_of(c * BLOCK, BLOCK), BLOCK), :] = jnp.concatenate(parts, axis=0).T

    for j in range(2):
        total = jnp.dot(weights[j][...], turned[...], preferred_element_type=jnp.float32)
        sums[j][...] = total if begin else total + before[j][...]
    if end:
        hidden = (jax.nn.silu(sums[0][...]) * sums[1][...]).astype(jnp.bfloat16)
        hidden_ref[...] = hidden.T
    for copy in copies:
        copy.wait()


def gate_up(k, pieces, weights, later, totals):
    hidden, part = weights[0].shape
    begin, end = k == 0, k == HALVES - 1
    rows = sum(p.shape[0] for p in pieces)
    total = jax.ShapeDtypeStruct((hidden, rows), jnp.float32)
    out_shape = [pltpu.VMEM((hidden, part), jnp.bfloat16)] * len(later)
    out_specs = [VMEM] * len(later)
    scratch = []
    if end:
        out_shape.append(jax.ShapeDtypeStruct((rows, hidden), jnp.bfloat16))
        scratch += [pltpu.VMEM((hidden, rows), jnp.float32)] * 2
    else:
        out_shape += [total] * 2
    out_specs += [VMEM] * (len(out_shape) - len(later))
    scratch.append(pltpu.VMEM((part, rows), jnp.bfloat16))
    scratch.append(pltpu.SemaphoreType.DMA((len(later), hidden // FETCH_ROWS)))
    weights = [pltpu.with_memory_space_constraint(w, pltpu.VMEM) for w in weights]
    later = [pltpu.with_memory_space_constraint(w, pltpu.HBM) for w in later]
    out = pl.pallas_call(
        functools.partial(gate_up_kernel, len(pieces), len(later), k * part, part, begin, end),
        in_specs=[VMEM] * (len(pieces) + 2) + [ANY] * len(later) + [VMEM] * len(totals),
        out_specs=out_specs,
        out_shape=out_shape,
        scratch_shapes=scratch,
        compiler_params=LIMIT if rows <= 256 else WIDE,
        cost_estimate=pl.CostEstimate(
            flops=4 * rows * hidden * part,
            bytes_accessed=4 * hidden * part + 8 * rows * hidden,
            transcendentals=0,
        ),
        name="gate_up",
    )(*pieces, *weights, *later, *totals)
    return out[: len(later)], out[len(later) :]


def down_kernel(ahead, hidden_ref, w_ref, *refs):
    later, held, refs = refs[:ahead], refs[ahead : 2 * ahead], refs[2 * ahead :]
    keep_ref, send_ref, sems = refs
    half, part = keep_ref.shape
    copies = fetches(later, 0, held, sems)
    for copy in copies:
        copy.start()

    @pl.loop(0, part // BLOCK)
    def _(c):
        columns = pl.ds(pl.multiple_of(c * BLOCK, BLOCK), BLOCK)
        out = jnp.dot(hidden_ref[...], w_ref[:, columns], preferred_element_type=jnp.float32)
        out = out.astype(jnp.bfloat16)
        keep_ref[:, columns] = out[:half]
        send_ref[:, columns] = out[half:]

    for copy in copies:
        copy.wait()


def down(hidden, w_down, later):
    rows, depth = hidden.shape
    part = w_down.shape[1]
    ahead = len(later)
    out_shape = [pltpu.VMEM((depth, part), jnp.bfloat16)] * ahead
    out_shape += [jax.ShapeDtypeStruct((rows // 2, part), jnp.bfloat16)] * 2
    w_down = pltpu.with_memory_space_constraint(w_down, pltpu.VMEM)
    later = [pltpu.with_memory_space_constraint(w, pltpu.HBM) for w in later]
    out = pl.pallas_call(
        functools.partial(down_kernel, ahead),
        in_specs=[VMEM, VMEM] + [ANY] * ahead,
        out_specs=[VMEM] * (ahead + 2),
        out_shape=out_shape,
        scratch_shapes=[pltpu.SemaphoreType.DMA((max(ahead, 1), depth // FETCH_ROWS))],
        compiler_params=LIMIT if rows <= 256 else WIDE,
        cost_estimate=pl.CostEstimate(
            flops=2 * rows * depth * part,
            bytes_accessed=2 * (depth * part + rows * depth + rows * part),
            transcendentals=0,
        ),
        name="down",
    )(hidden, w_down, *later)
    return out[:ahead], out[ahead:]


def mix_kernel(group, ids_ref, logits_ref, act_ref, arrived, near, last, *refs):
    out_ref, kept, middle_rows = refs[-1], refs[:HALVES], refs[HALVES:-1]
    plane = lax.axis_index("expert") // group
    first, second = choices(ids_ref[...], plane)
    lead = logits_ref[0:1, :] - logits_ref[1:2, :]
    weight = jnp.where(first, jax.nn.sigmoid(lead), 0.0)
    weight = (weight + jnp.where(second, jax.nn.sigmoid(-lead), 0.0)).T
    tokens = weight.shape[0]
    high = weight.astype(jnp.bfloat16).astype(jnp.float32)
    middle = (weight - high).astype(jnp.bfloat16).astype(jnp.float32)
    terms = jnp.concatenate([weight - high - middle, middle, high], axis=0).astype(jnp.bfloat16)
    part = kept[0].shape[1]
    for k in range(HALVES):
        columns = slice(k * part, (k + 1) * part)
        own = kept[k][...].astype(jnp.float32) + arrived[:, columns].astype(jnp.float32)
        blocks = [own.astype(jnp.bfloat16), near[:, columns], middle_rows[k][...]]
        rows = jnp.concatenate(blocks + [last[:, columns]], axis=0)
        sums = jnp.dot(terms, rows, preferred_element_type=jnp.float32)
        total = act_ref[:, columns].astype(jnp.float32)
        for j in range(3):
            total = total + sums[j * tokens : (j + 1) * tokens]
        out_ref[:, columns] = total.astype(jnp.bfloat16)


def mix(group, ids, logits, activations, pieces):
    return pl.pallas_call(
        functools.partial(mix_kernel, group),
        out_shape=jax.ShapeDtypeStruct(activations.shape, jnp.bfloat16),
        compiler_params=LIMIT,
        name="mix",
    )(ids, logits, activations, *pieces)


def added(mine, arrived):
    total = mine.astype(jnp.float32) + arrived.astype(jnp.float32)
    return total.astype(jnp.bfloat16)


def on_device(activations, expert_ids, route_logits, norm_gain, w_gate, w_up, w_down):
    devices = lax.axis_size("expert")
    group = devices // EXPERTS
    far = group // 2
    width = activations.shape[1]
    part = width // HALVES

    def shift(x, s):
        return lax.ppermute(
            x, "expert", [(i, (i + s * group) % devices) for i in range(devices)]
        )

    def swap(x, bit):
        return lax.ppermute(x, "expert", [(i, i ^ bit) for i in range(devices)])

    def after(x, *others):
        return lax.optimization_barrier((x, *others))[0]

    others = EXPERTS - 1
    ids = expert_ids.T
    own, *sends = pack(group, ids, activations, norm_gain)
    far_own = swap(own, far)
    now = [fetch(w, 0, part, own) for w in (w_gate, w_up)]
    blocks = []
    for k in range(HALVES):
        x = sends[k * others : (k + 1) * others]
        if k:
            x = relay(after(x, *now, far_own), blocks[-1])
        arrivals = [shift(x[s], s + 1) for s in range(others)]
        blocks.append(jnp.concatenate(arrivals, axis=0))
    totals = []
    for k in range(HALVES):
        columns = slice(k * part, (k + 1) * part)
        far_block = swap(blocks[k], far)
        if totals:
            far_block, totals = lax.optimization_barrier((far_block, totals))
        pieces = [own[:, columns], blocks[k], far_own[:, columns], far_block]
        bit = far // 2
        while bit:
            pieces.append(swap(jnp.concatenate(pieces, axis=0), bit))
            bit //= 2
        pieces[0], pieces[2] = own, far_own
        if k < HALVES - 1:
            pieces[1] = after(pieces[1], blocks[k + 1])
        later = [w_down] if k == HALVES - 1 else [w_gate, w_up]
        now, totals = gate_up(k, pieces, now, later, totals)
    hidden = totals[0]
    held = []
    for k in reversed(range(HALVES)):
        later = [w_down] if k else []
        now, (keep, send) = down(hidden, now[0], later)
        bit = 1
        while bit < far:
            total = added(keep, swap(send, bit))
            keep, send = total[: total.shape[0] // 2], total[total.shape[0] // 2 :]
            bit *= 2
        held.insert(0, [total[j * CAP : (j + 1) * CAP] for j in range(2 * EXPERTS)])
    crossed = [swap(h[6], far) for h in held]
    middle = [shift(added(h[2], x), -2) for h, x in zip(held, crossed)]
    mine = [jnp.concatenate([h[j] for h in held], axis=1) for j in range(2 * EXPERTS)]
    back = {}
    back[1] = swap(after(mine[EXPERTS + 1], crossed[0]), far)
    back[3] = swap(after(mine[EXPERTS + 3], *crossed), far)
    back[0] = swap(after(mine[EXPERTS], back[1], back[3]), far)
    near = shift(after(added(mine[1], back[1]), middle[0]), -1)
    last = shift(after(added(mine[3], back[3]), middle[1]), -3)
    arrived = back[0]
    pieces = [arrived, near, last, *[h[0] for h in held], *middle]
    return mix(group, ids, route_logits.T, activations, pieces)


def solution(mesh):
    in_specs = (
        P(("parts", "expert"), None),
        P(("parts", "expert"), None),
        P(("parts", "expert"), None),
        P(),
        P("expert", None),
        P("expert", None),
        P("expert", None),
    )
    out_specs = P(("parts", "expert"), None)
    return jax.shard_map(
        on_device, mesh=mesh, in_specs=in_specs, out_specs=out_specs, check_vma=False
    )
```

```python
import functools

import jax
import jax.numpy as jnp
from jax import lax
from jax.experimental import pallas as pl
from jax.experimental.pallas import tpu as pltpu
from jax.sharding import PartitionSpec as P

EXPERTS = 4
CAP = 16
HALVES = 2
ORDER = (2, 1, 3)
FORTH = (7, 5)
BLOCK = 512
WIDE_BLOCK = 1024
FETCH_ROWS = 144
MIB = 1 << 20
LIMIT = pltpu.CompilerParams(vmem_limit_bytes=10 * MIB)
WIDE = pltpu.CompilerParams(vmem_limit_bytes=32 * MIB)
VMEM = pl.BlockSpec(memory_space=pltpu.VMEM)
ANY = pl.BlockSpec(memory_space=pl.ANY)


def spans(width):
    unit = width // sum(FORTH)
    return [(sum(FORTH[:k]) * unit, n * unit) for k, n in enumerate(FORTH)]


def choices(ids, plane):
    tokens = ids.shape[1]
    line = lax.broadcasted_iota(jnp.int32, (EXPERTS * CAP, tokens), 0)
    expert = lax.rem(line // CAP + plane, EXPERTS)
    slot = (line % CAP).astype(jnp.float32)
    first = ids[0:1, :] == expert
    second = ids[1:2, :] == expert
    named = (first | second).astype(jnp.float32)
    square = (tokens, tokens)
    earlier = lax.broadcasted_iota(jnp.int32, square, 0) < lax.broadcasted_iota(
        jnp.int32, square, 1
    )
    rank = jnp.dot(named, earlier.astype(jnp.float32), preferred_element_type=jnp.float32)
    here = rank == slot
    return first & here, second & here


def pack_kernel(group, ids_ref, act_ref, gain_ref, *out_refs):
    plane = lax.axis_index("expert") // group
    values = act_ref[...].astype(jnp.float32)
    mean_sq = jnp.mean(values * values, axis=-1, keepdims=True)
    normed = (values * lax.rsqrt(mean_sq + 1e-06) * gain_ref[...]).astype(jnp.bfloat16)
    first, second = choices(ids_ref[...], plane)
    pick = (first | second).astype(jnp.float32).astype(jnp.bfloat16)
    rows = jnp.dot(pick, normed, preferred_element_type=jnp.float32).astype(jnp.bfloat16)
    out_refs[0][...] = rows[:CAP]
    for j, out_ref in enumerate(out_refs[1:]):
        k, s = j // (EXPERTS - 1), j % (EXPERTS - 1) + 1
        at, part = spans(rows.shape[1])[k]
        out_ref[...] = rows[s * CAP : (s + 1) * CAP, at : at + part]


def pack(group, ids, activations, gain):
    width = activations.shape[1]
    widths = [width] + [part for _, part in spans(width) for _ in range(EXPERTS - 1)]
    operands = [ids, activations, gain.reshape(1, width)]
    return pl.pallas_call(
        functools.partial(pack_kernel, group),
        grid=(1,),
        in_specs=[pl.BlockSpec(x.shape, lambda i: (0, 0)) for x in operands],
        out_specs=[pl.BlockSpec((CAP, n), lambda i: (0, 0)) for n in widths],
        out_shape=[jax.ShapeDtypeStruct((CAP, n), jnp.bfloat16) for n in widths],
        compiler_params=LIMIT,
        name="norm_and_pack",
    )(*[pltpu.with_memory_space_constraint(x, pltpu.HBM) for x in operands])


def fetches(weights, at, held, sems):
    copies = []
    for j, w in enumerate(weights):
        part = held[j].shape[1]
        for b in range(sems.shape[1]):
            rows = pl.ds(b * FETCH_ROWS, FETCH_ROWS)
            copies.append(
                pltpu.make_async_copy(w.at[rows, at : at + part], held[j].at[rows], sems.at[j, b])
            )
    return copies


def fetch_kernel(at, w_ref, after_ref, held_ref, sems):
    copies = fetches([w_ref], at, [held_ref], sems)
    for copy in copies:
        copy.start()
    for copy in copies:
        copy.wait()


def fetch(w, at, part, after):
    rows = w.shape[0]
    return pl.pallas_call(
        functools.partial(fetch_kernel, at),
        in_specs=[ANY, ANY],
        out_specs=VMEM,
        out_shape=pltpu.VMEM((rows, part), jnp.bfloat16),
        scratch_shapes=[pltpu.SemaphoreType.DMA((1, rows // FETCH_ROWS))],
        compiler_params=LIMIT,
        cost_estimate=pl.CostEstimate(flops=0, bytes_accessed=4 * rows * part, transcendentals=0),
        name="fetch",
    )(pltpu.with_memory_space_constraint(w, pltpu.HBM), after)


def relay_kernel(count, *refs):
    for x_ref, out_ref in zip(refs[:count], refs[count + 1 :]):
        out_ref[...] = x_ref[...]


def relay(arrays, after):
    count = len(arrays)
    return pl.pallas_call(
        functools.partial(relay_kernel, count),
        in_specs=[VMEM] * count + [ANY],
        out_specs=[VMEM] * count,
        out_shape=[jax.ShapeDtypeStruct(x.shape, x.dtype) for x in arrays],
        compiler_params=LIMIT,
        cost_estimate=pl.CostEstimate(flops=0, bytes_accessed=16 * MIB, transcendentals=0),
        name="relay",
    )(*arrays, after)


def gate_up_kernel(count, ahead, at, ahead_at, begin, end, *refs):
    pieces, refs = refs[:count], refs[count:]
    weights, later, refs = refs[:2], refs[2 : 2 + ahead], refs[2 + ahead :]
    if not begin:
        before, refs = refs[:2], refs[2:]
    held, refs = refs[:ahead], refs[ahead:]
    turned, sems, refs = *refs[-2:], refs[:-2]
    if end:
        hidden_ref, refs = refs[0], refs[1:]
    sums = refs
    part, rows = turned.shape
    copies = fetches(later, ahead_at, held, sems)
    for copy in copies:
        copy.start()

    @pl.loop(0, part // BLOCK)
    def _(c):
        parts = []
        for p in pieces:
            first = c * BLOCK + (at if p.shape[1] > part else 0)
            parts.append(p[:, pl.ds(pl.multiple_of(first, BLOCK), BLOCK)])
        turned[pl.ds(pl.multiple_of(c * BLOCK, BLOCK), BLOCK), :] = jnp.concatenate(parts, axis=0).T

    for j in range(2):
        total = jnp.dot(weights[j][...], turned[...], preferred_element_type=jnp.float32)
        sums[j][...] = total if begin else total + before[j][...]
    if end:
        hidden = (jax.nn.silu(sums[0][...]) * sums[1][...]).astype(jnp.bfloat16)
        hidden_ref[...] = hidden.T
    for copy in copies:
        copy.wait()


def gate_up(k, pieces, weights, later, ahead, totals):
    hidden, part = weights[0].shape
    begin, end = k == 0, k == HALVES - 1
    width = later[0].shape[1]
    rows = sum(p.shape[0] for p in pieces)
    total = jax.ShapeDtypeStruct((hidden, rows), jnp.float32)
    out_shape = [pltpu.VMEM((hidden, ahead[1]), jnp.bfloat16)] * len(later)
    out_specs = [VMEM] * len(later)
    scratch = []
    if end:
        out_shape.append(jax.ShapeDtypeStruct((rows, hidden), jnp.bfloat16))
        scratch += [pltpu.VMEM((hidden, rows), jnp.float32)] * 2
    else:
        out_shape += [total] * 2
    out_specs += [VMEM] * (len(out_shape) - len(later))
    scratch.append(pltpu.VMEM((part, rows), jnp.bfloat16))
    scratch.append(pltpu.SemaphoreType.DMA((len(later), hidden // FETCH_ROWS)))
    weights = [pltpu.with_memory_space_constraint(w, pltpu.VMEM) for w in weights]
    later = [pltpu.with_memory_space_constraint(w, pltpu.HBM) for w in later]
    out = pl.pallas_call(
        functools.partial(
            gate_up_kernel, len(pieces), len(later), spans(width)[k][0], ahead[0], begin, end
        ),
        in_specs=[VMEM] * (len(pieces) + 2) + [ANY] * len(later) + [VMEM] * len(totals),
        out_specs=out_specs,
        out_shape=out_shape,
        scratch_shapes=scratch,
        compiler_params=LIMIT if rows <= 256 else WIDE,
        cost_estimate=pl.CostEstimate(
            flops=4 * rows * hidden * part,
            bytes_accessed=4 * hidden * part + 8 * rows * hidden,
            transcendentals=0,
        ),
        name="gate_up",
    )(*pieces, *weights, *later, *totals)
    return out[: len(later)], out[len(later) :]


def down_kernel(ahead, hidden_ref, w_ref, *refs):
    later, held, refs = refs[:ahead], refs[ahead : 2 * ahead], refs[2 * ahead :]
    keep_ref, send_ref, sems = refs
    half, part = keep_ref.shape
    copies = fetches(later, part, held, sems)
    for copy in copies:
        copy.start()

    @pl.loop(0, part // WIDE_BLOCK)
    def _(c):
        columns = pl.ds(pl.multiple_of(c * WIDE_BLOCK, WIDE_BLOCK), WIDE_BLOCK)
        out = jnp.dot(hidden_ref[...], w_ref[:, columns], preferred_element_type=jnp.float32)
        out = out.astype(jnp.bfloat16)
        keep_ref[:, columns] = out[:half]
        send_ref[:, columns] = out[half:]

    for copy in copies:
        copy.wait()


def down(hidden, w_down, later):
    rows, depth = hidden.shape
    part = w_down.shape[1]
    ahead = len(later)
    out_shape = [pltpu.VMEM((depth, part), jnp.bfloat16)] * ahead
    out_shape += [jax.ShapeDtypeStruct((rows // 2, part), jnp.bfloat16)] * 2
    w_down = pltpu.with_memory_space_constraint(w_down, pltpu.VMEM)
    later = [pltpu.with_memory_space_constraint(w, pltpu.HBM) for w in later]
    out = pl.pallas_call(
        functools.partial(down_kernel, ahead),
        in_specs=[VMEM, VMEM] + [ANY] * ahead,
        out_specs=[VMEM] * (ahead + 2),
        out_shape=out_shape,
        scratch_shapes=[pltpu.SemaphoreType.DMA((max(ahead, 1), depth // FETCH_ROWS))],
        compiler_params=LIMIT if rows <= 256 else WIDE,
        cost_estimate=pl.CostEstimate(
            flops=2 * rows * depth * part,
            bytes_accessed=2 * (depth * part + rows * depth + rows * part),
            transcendentals=0,
        ),
        name="down",
    )(hidden, w_down, *later)
    return out[:ahead], out[ahead:]


def mix_kernel(group, ids_ref, logits_ref, act_ref, arrived, near, last, *refs):
    out_ref, kept, middle_rows = refs[-1], refs[:HALVES], refs[HALVES:-1]
    plane = lax.axis_index("expert") // group
    first, second = choices(ids_ref[...], plane)
    lead = logits_ref[0:1, :] - logits_ref[1:2, :]
    weight = jnp.where(first, jax.nn.sigmoid(lead), 0.0)
    weight = (weight + jnp.where(second, jax.nn.sigmoid(-lead), 0.0)).T
    tokens = weight.shape[0]
    high = weight.astype(jnp.bfloat16).astype(jnp.float32)
    middle = (weight - high).astype(jnp.bfloat16).astype(jnp.float32)
    terms = jnp.concatenate([weight - high - middle, middle, high], axis=0).astype(jnp.bfloat16)
    part = kept[0].shape[1]
    for k in range(HALVES):
        columns = slice(k * part, (k + 1) * part)
        own = kept[k][...].astype(jnp.float32) + arrived[:, columns].astype(jnp.float32)
        blocks = [own.astype(jnp.bfloat16), near[:, columns], middle_rows[k][...]]
        rows = jnp.concatenate(blocks + [last[:, columns]], axis=0)
        sums = jnp.dot(terms, rows, preferred_element_type=jnp.float32)
        total = act_ref[:, columns].astype(jnp.float32)
        for j in range(3):
            total = total + sums[j * tokens : (j + 1) * tokens]
        out_ref[:, columns] = total.astype(jnp.bfloat16)


def mix(group, ids, logits, activations, pieces):
    return pl.pallas_call(
        functools.partial(mix_kernel, group),
        out_shape=jax.ShapeDtypeStruct(activations.shape, jnp.bfloat16),
        compiler_params=LIMIT,
        name="mix",
    )(ids, logits, activations, *pieces)


def added(mine, arrived):
    total = mine.astype(jnp.float32) + arrived.astype(jnp.float32)
    return total.astype(jnp.bfloat16)


def on_device(activations, expert_ids, route_logits, norm_gain, w_gate, w_up, w_down):
    devices = lax.axis_size("expert")
    group = devices // EXPERTS
    far = group // 2
    width = activations.shape[1]
    part = width // HALVES

    def shift(x, s):
        return lax.ppermute(
            x, "expert", [(i, (i + s * group) % devices) for i in range(devices)]
        )

    def swap(x, bit):
        return lax.ppermute(x, "expert", [(i, i ^ bit) for i in range(devices)])

    def after(x, *others):
        return lax.optimization_barrier((x, *others))[0]

    others = EXPERTS - 1
    ids = expert_ids.T
    own, *sends = pack(group, ids, activations, norm_gain)
    far_own = swap(own, far)
    now = [fetch(w, 0, spans(width)[0][1], own) for w in (w_gate, w_up)]
    blocks = []
    for k in range(HALVES):
        x = sends[k * others : (k + 1) * others]
        if k:
            x = relay(after(x, *now, far_own), blocks[-1])
        arrivals = [shift(x[s - 1], s) for s in ORDER]
        blocks.append(jnp.concatenate(arrivals, axis=0))
    totals = []
    for k in range(HALVES):
        at, size = spans(width)[k]
        columns = slice(at, at + size)
        far_block = swap(blocks[k], far)
        if totals:
            far_block, totals = lax.optimization_barrier((far_block, totals))
        pieces = [own[:, columns], blocks[k], far_own[:, columns], far_block]
        bit = far // 2
        while bit:
            pieces.append(swap(jnp.concatenate(pieces, axis=0), bit))
            bit //= 2
        pieces[0], pieces[2] = own, far_own
        if k < HALVES - 1:
            pieces[1] = after(pieces[1], blocks[k + 1])
        later, ahead = [w_gate, w_up], (size, width - size)
        if k == HALVES - 1:
            later, ahead = [w_down], (0, part)
        now, totals = gate_up(k, pieces, now, later, ahead, totals)
    hidden = totals[0]
    held = []
    for k in range(HALVES):
        later = [w_down] if k == 0 else []
        now, (keep, send) = down(hidden, now[0], later)
        bit = 1
        while bit < far:
            total = added(keep, swap(send, bit))
            keep, send = total[: total.shape[0] // 2], total[total.shape[0] // 2 :]
            bit *= 2
        held.append([total[j * CAP : (j + 1) * CAP] for j in range(2 * EXPERTS)])
    place = {s: 1 + j for j, s in enumerate(ORDER)}
    crossed = [swap(h[EXPERTS + place[2]], far) for h in held]
    middle = [shift(added(h[place[2]], x), -2) for h, x in zip(held, crossed)]
    mine = [jnp.concatenate([h[j] for h in held], axis=1) for j in range(2 * EXPERTS)]
    back = {}
    back[1] = swap(after(mine[EXPERTS + place[1]], crossed[0]), far)
    back[3] = swap(after(mine[EXPERTS + place[3]], *crossed), far)
    back[0] = swap(after(mine[EXPERTS], back[1], back[3]), far)
    near = shift(after(added(mine[place[1]], back[1]), middle[1]), -1)
    last = shift(after(added(mine[place[3]], back[3]), middle[0]), -3)
    arrived = back[0]
    pieces = [arrived, near, last, *[h[0] for h in held], *middle]
    return mix(group, ids, route_logits.T, activations, pieces)


def solution(mesh):
    in_specs = (
        P(("parts", "expert"), None),
        P(("parts", "expert"), None),
        P(("parts", "expert"), None),
        P(),
        P("expert", None),
        P("expert", None),
        P("expert", None),
    )
    out_specs = P(("parts", "expert"), None)
    return jax.shard_map(
        on_device, mesh=mesh, in_specs=in_specs, out_specs=out_specs, check_vma=False
    )
```

```python
import functools

import jax
import jax.numpy as jnp
from jax import lax
from jax.experimental import pallas as pl
from jax.experimental.pallas import tpu as pltpu
from jax.sharding import PartitionSpec as P

EXPERTS = 4
CAP = 16
HALVES = 2
ORDER = (2, 3, 1)
FORTH = (7, 5)
BACK = (1, 1)
BLOCK = 512
FETCH_ROWS = 144
MIB = 1 << 20
LIMIT = pltpu.CompilerParams(vmem_limit_bytes=10 * MIB)
WIDE = pltpu.CompilerParams(vmem_limit_bytes=32 * MIB)
VMEM = pl.BlockSpec(memory_space=pltpu.VMEM)
ANY = pl.BlockSpec(memory_space=pl.ANY)


def spans(width, shares=FORTH):
    unit = width // sum(shares)
    return [(sum(shares[:k]) * unit, n * unit) for k, n in enumerate(shares)]


def choices(ids, plane):
    tokens = ids.shape[1]
    line = lax.broadcasted_iota(jnp.int32, (EXPERTS * CAP, tokens), 0)
    expert = lax.rem(line // CAP + plane, EXPERTS)
    slot = (line % CAP).astype(jnp.float32)
    first = ids[0:1, :] == expert
    second = ids[1:2, :] == expert
    named = (first | second).astype(jnp.float32)
    square = (tokens, tokens)
    earlier = lax.broadcasted_iota(jnp.int32, square, 0) < lax.broadcasted_iota(
        jnp.int32, square, 1
    )
    rank = jnp.dot(named, earlier.astype(jnp.float32), preferred_element_type=jnp.float32)
    here = rank == slot
    return first & here, second & here


def pack_kernel(group, ids_ref, act_ref, gain_ref, *out_refs):
    plane = lax.axis_index("expert") // group
    values = act_ref[...].astype(jnp.float32)
    mean_sq = jnp.mean(values * values, axis=-1, keepdims=True)
    normed = (values * lax.rsqrt(mean_sq + 1e-06) * gain_ref[...]).astype(jnp.bfloat16)
    first, second = choices(ids_ref[...], plane)
    pick = (first | second).astype(jnp.float32).astype(jnp.bfloat16)
    rows = jnp.dot(pick, normed, preferred_element_type=jnp.float32).astype(jnp.bfloat16)
    out_refs[0][...] = rows[:CAP]
    for j, out_ref in enumerate(out_refs[1:]):
        k, s = j // (EXPERTS - 1), j % (EXPERTS - 1) + 1
        at, part = spans(rows.shape[1])[k]
        out_ref[...] = rows[s * CAP : (s + 1) * CAP, at : at + part]


def pack(group, ids, activations, gain):
    width = activations.shape[1]
    widths = [width] + [part for _, part in spans(width) for _ in range(EXPERTS - 1)]
    operands = [ids, activations, gain.reshape(1, width)]
    return pl.pallas_call(
        functools.partial(pack_kernel, group),
        grid=(1,),
        in_specs=[pl.BlockSpec(x.shape, lambda i: (0, 0)) for x in operands],
        out_specs=[pl.BlockSpec((CAP, n), lambda i: (0, 0)) for n in widths],
        out_shape=[jax.ShapeDtypeStruct((CAP, n), jnp.bfloat16) for n in widths],
        compiler_params=LIMIT,
        name="norm_and_pack",
    )(*[pltpu.with_memory_space_constraint(x, pltpu.HBM) for x in operands])


def fetches(weights, at, held, sems):
    copies = []
    for j, w in enumerate(weights):
        part = held[j].shape[1]
        for b in range(sems.shape[1]):
            rows = pl.ds(b * FETCH_ROWS, FETCH_ROWS)
            copies.append(
                pltpu.make_async_copy(w.at[rows, at : at + part], held[j].at[rows], sems.at[j, b])
            )
    return copies


def fetch_kernel(at, w_ref, after_ref, held_ref, sems):
    copies = fetches([w_ref], at, [held_ref], sems)
    for copy in copies:
        copy.start()
    for copy in copies:
        copy.wait()


def fetch(w, at, part, after):
    rows = w.shape[0]
    return pl.pallas_call(
        functools.partial(fetch_kernel, at),
        in_specs=[ANY, ANY],
        out_specs=VMEM,
        out_shape=pltpu.VMEM((rows, part), jnp.bfloat16),
        scratch_shapes=[pltpu.SemaphoreType.DMA((1, rows // FETCH_ROWS))],
        compiler_params=LIMIT,
        cost_estimate=pl.CostEstimate(flops=0, bytes_accessed=4 * rows * part, transcendentals=0),
        name="fetch",
    )(pltpu.with_memory_space_constraint(w, pltpu.HBM), after)


def relay_kernel(count, *refs):
    for x_ref, out_ref in zip(refs[:count], refs[count + 1 :]):
        out_ref[...] = x_ref[...]


def relay(arrays, after):
    count = len(arrays)
    return pl.pallas_call(
        functools.partial(relay_kernel, count),
        in_specs=[VMEM] * count + [ANY],
        out_specs=[VMEM] * count,
        out_shape=[jax.ShapeDtypeStruct(x.shape, x.dtype) for x in arrays],
        compiler_params=LIMIT,
        cost_estimate=pl.CostEstimate(flops=0, bytes_accessed=16 * MIB, transcendentals=0),
        name="relay",
    )(*arrays, after)


def gate_up_kernel(count, ahead, at, ahead_at, begin, end, *refs):
    pieces, refs = refs[:count], refs[count:]
    weights, later, refs = refs[:2], refs[2 : 2 + ahead], refs[2 + ahead :]
    if not begin:
        before, refs = refs[:2], refs[2:]
    held, refs = refs[:ahead], refs[ahead:]
    turned, sems, refs = *refs[-2:], refs[:-2]
    if end:
        hidden_ref, refs = refs[0], refs[1:]
    sums = refs
    part, rows = turned.shape
    copies = fetches(later, ahead_at, held, sems)
    for copy in copies:
        copy.start()

    @pl.loop(0, part // BLOCK)
    def _(c):
        parts = []
        for p in pieces:
            first = c * BLOCK + (at if p.shape[1] > part else 0)
            parts.append(p[:, pl.ds(pl.multiple_of(first, BLOCK), BLOCK)])
        turned[pl.ds(pl.multiple_of(c * BLOCK, BLOCK), BLOCK), :] = jnp.concatenate(parts, axis=0).T

    for j in range(2):
        total = jnp.dot(weights[j][...], turned[...], preferred_element_type=jnp.float32)
        sums[j][...] = total if begin else total + before[j][...]
    if end:
        hidden = (jax.nn.silu(sums[0][...]) * sums[1][...]).astype(jnp.bfloat16)
        hidden_ref[...] = hidden.T
    for copy in copies:
        copy.wait()


def gate_up(k, pieces, weights, later, ahead, totals):
    hidden, part = weights[0].shape
    begin, end = k == 0, k == HALVES - 1
    width = later[0].shape[1]
    rows = sum(p.shape[0] for p in pieces)
    total = jax.ShapeDtypeStruct((hidden, rows), jnp.float32)
    out_shape = [pltpu.VMEM((hidden, ahead[1]), jnp.bfloat16)] * len(later)
    out_specs = [VMEM] * len(later)
    scratch = []
    if end:
        out_shape.append(jax.ShapeDtypeStruct((rows, hidden), jnp.bfloat16))
        scratch += [pltpu.VMEM((hidden, rows), jnp.float32)] * 2
    else:
        out_shape += [total] * 2
    out_specs += [VMEM] * (len(out_shape) - len(later))
    scratch.append(pltpu.VMEM((part, rows), jnp.bfloat16))
    scratch.append(pltpu.SemaphoreType.DMA((len(later), hidden // FETCH_ROWS)))
    weights = [pltpu.with_memory_space_constraint(w, pltpu.VMEM) for w in weights]
    later = [pltpu.with_memory_space_constraint(w, pltpu.HBM) for w in later]
    out = pl.pallas_call(
        functools.partial(
            gate_up_kernel, len(pieces), len(later), spans(width)[k][0], ahead[0], begin, end
        ),
        in_specs=[VMEM] * (len(pieces) + 2) + [ANY] * len(later) + [VMEM] * len(totals),
        out_specs=out_specs,
        out_shape=out_shape,
        scratch_shapes=scratch,
        compiler_params=LIMIT if rows <= 256 else WIDE,
        cost_estimate=pl.CostEstimate(
            flops=4 * rows * hidden * part,
            bytes_accessed=4 * hidden * part + 8 * rows * hidden,
            transcendentals=0,
        ),
        name="gate_up",
    )(*pieces, *weights, *later, *totals)
    return out[: len(later)], out[len(later) :]


def down_kernel(ahead, hidden_ref, w_ref, *refs):
    later, held, refs = refs[:ahead], refs[ahead : 2 * ahead], refs[2 * ahead :]
    keep_ref, send_ref, sems = refs
    half, part = keep_ref.shape
    block = part // 2
    copies = fetches(later, part, held, sems)
    for copy in copies:
        copy.start()

    @pl.loop(0, 2)
    def _(c):
        columns = pl.ds(pl.multiple_of(c * block, block), block)
        out = jnp.dot(hidden_ref[...], w_ref[:, columns], preferred_element_type=jnp.float32)
        out = out.astype(jnp.bfloat16)
        keep_ref[:, columns] = out[:half]
        send_ref[:, columns] = out[half:]

    for copy in copies:
        copy.wait()


def down(hidden, w_down, later):
    rows, depth = hidden.shape
    part = w_down.shape[1]
    ahead = len(later)
    out_shape = [pltpu.VMEM((depth, w.shape[1] - part), jnp.bfloat16) for w in later]
    out_shape += [jax.ShapeDtypeStruct((rows // 2, part), jnp.bfloat16)] * 2
    w_down = pltpu.with_memory_space_constraint(w_down, pltpu.VMEM)
    later = [pltpu.with_memory_space_constraint(w, pltpu.HBM) for w in later]
    out = pl.pallas_call(
        functools.partial(down_kernel, ahead),
        in_specs=[VMEM, VMEM] + [ANY] * ahead,
        out_specs=[VMEM] * (ahead + 2),
        out_shape=out_shape,
        scratch_shapes=[pltpu.SemaphoreType.DMA((max(ahead, 1), depth // FETCH_ROWS))],
        compiler_params=LIMIT if rows <= 256 else WIDE,
        cost_estimate=pl.CostEstimate(
            flops=2 * rows * depth * part,
            bytes_accessed=2 * (depth * part + rows * depth + rows * part),
            transcendentals=0,
        ),
        name="down",
    )(hidden, w_down, *later)
    return out[:ahead], out[ahead:]


def mix_kernel(group, ids_ref, logits_ref, act_ref, arrived, near, last, *refs):
    out_ref, kept, middle_rows = refs[-1], refs[:HALVES], refs[HALVES:-1]
    plane = lax.axis_index("expert") // group
    first, second = choices(ids_ref[...], plane)
    lead = logits_ref[0:1, :] - logits_ref[1:2, :]
    weight = jnp.where(first, jax.nn.sigmoid(lead), 0.0)
    weight = (weight + jnp.where(second, jax.nn.sigmoid(-lead), 0.0)).T
    tokens = weight.shape[0]
    high = weight.astype(jnp.bfloat16).astype(jnp.float32)
    middle = (weight - high).astype(jnp.bfloat16).astype(jnp.float32)
    terms = jnp.concatenate([weight - high - middle, middle, high], axis=0).astype(jnp.bfloat16)
    for k, (at, part) in enumerate(spans(act_ref.shape[1], BACK)):
        columns = slice(at, at + part)
        own = kept[k][...].astype(jnp.float32) + arrived[:, columns].astype(jnp.float32)
        blocks = [own.astype(jnp.bfloat16), near[:, columns], middle_rows[k][...]]
        rows = jnp.concatenate(blocks + [last[:, columns]], axis=0)
        sums = jnp.dot(terms, rows, preferred_element_type=jnp.float32)
        total = act_ref[:, columns].astype(jnp.float32)
        for j in range(3):
            total = total + sums[j * tokens : (j + 1) * tokens]
        out_ref[:, columns] = total.astype(jnp.bfloat16)


def mix(group, ids, logits, activations, pieces):
    return pl.pallas_call(
        functools.partial(mix_kernel, group),
        out_shape=jax.ShapeDtypeStruct(activations.shape, jnp.bfloat16),
        compiler_params=LIMIT,
        name="mix",
    )(ids, logits, activations, *pieces)


def added(mine, arrived):
    total = mine.astype(jnp.float32) + arrived.astype(jnp.float32)
    return total.astype(jnp.bfloat16)


def on_device(activations, expert_ids, route_logits, norm_gain, w_gate, w_up, w_down):
    devices = lax.axis_size("expert")
    group = devices // EXPERTS
    far = group // 2
    width = activations.shape[1]
    part = width // HALVES

    def shift(x, s):
        return lax.ppermute(
            x, "expert", [(i, (i + s * group) % devices) for i in range(devices)]
        )

    def swap(x, bit):
        return lax.ppermute(x, "expert", [(i, i ^ bit) for i in range(devices)])

    def after(x, *others):
        return lax.optimization_barrier((x, *others))[0]

    others = EXPERTS - 1
    ids = expert_ids.T
    own, *sends = pack(group, ids, activations, norm_gain)
    far_own = swap(own, far)
    now = [fetch(w_gate, 0, spans(width)[0][1], own)]
    blocks = []
    for k in range(HALVES):
        x = sends[k * others : (k + 1) * others]
        if k:
            x = relay(after(x, *now, far_own), blocks[-1])
            now.append(fetch(w_up, 0, spans(width)[0][1], x[0]))
        arrivals = [shift(x[s - 1], s) for s in ORDER]
        blocks.append(jnp.concatenate(arrivals, axis=0))
    totals = []
    for k in range(HALVES):
        at, size = spans(width)[k]
        columns = slice(at, at + size)
        far_block = swap(blocks[k], far)
        if totals:
            far_block, totals = lax.optimization_barrier((far_block, totals))
        pieces = [own[:, columns], blocks[k], far_own[:, columns], far_block]
        bit = far // 2
        while bit:
            pieces.append(swap(jnp.concatenate(pieces, axis=0), bit))
            bit //= 2
        pieces[0], pieces[2] = own, far_own
        if k < HALVES - 1:
            pieces[1] = after(pieces[1], blocks[k + 1])
        later, ahead = [w_gate, w_up], (size, width - size)
        if k == HALVES - 1:
            later, ahead = [w_down], spans(width, BACK)[0]
        now, totals = gate_up(k, pieces, now, later, ahead, totals)
    hidden = totals[0]
    held = []
    for k in range(HALVES):
        later = [w_down] if k == 0 else []
        now, (keep, send) = down(hidden, now[0], later)
        bit = 1
        while bit < far:
            total = added(keep, swap(send, bit))
            keep, send = total[: total.shape[0] // 2], total[total.shape[0] // 2 :]
            bit *= 2
        held.append([total[j * CAP : (j + 1) * CAP] for j in range(2 * EXPERTS)])
    place = {s: 1 + j for j, s in enumerate(ORDER)}
    crossed = [swap(h[EXPERTS + place[2]], far) for h in held]
    middle = [shift(added(h[place[2]], x), -2) for h, x in zip(held, crossed)]
    mine = [jnp.concatenate([h[j] for h in held], axis=1) for j in range(2 * EXPERTS)]
    back = {}
    back[1] = swap(after(mine[EXPERTS + place[1]], crossed[1]), far)
    back[3] = swap(after(mine[EXPERTS + place[3]], crossed[0]), far)
    back[0] = swap(after(mine[EXPERTS], back[1], back[3]), far)
    near = shift(after(added(mine[place[1]], back[1]), middle[1]), -1)
    last = shift(after(added(mine[place[3]], back[3]), middle[0]), -3)
    arrived = back[0]
    pieces = [arrived, near, last, *[h[0] for h in held], *middle]
    return mix(group, ids, route_logits.T, activations, pieces)


def solution(mesh):
    in_specs = (
        P(("parts", "expert"), None),
        P(("parts", "expert"), None),
        P(("parts", "expert"), None),
        P(),
        P("expert", None),
        P("expert", None),
        P("expert", None),
    )
    out_specs = P(("parts", "expert"), None)
    return jax.shard_map(
        on_device, mesh=mesh, in_specs=in_specs, out_specs=out_specs, check_vma=False
    )
```

```python
import functools

import jax
import jax.numpy as jnp
from jax import lax
from jax.experimental import pallas as pl
from jax.experimental.pallas import tpu as pltpu
from jax.sharding import PartitionSpec as P

EXPERTS = 4
CAP = 16
HALVES = 2
ORDER = (2, 1, 3)
FORTH = (7, 5)
BACK = (1, 1)
BLOCK = 512
AHEAD = 8
FETCH_ROWS = 144
MIB = 1 << 20
LIMIT = pltpu.CompilerParams(vmem_limit_bytes=10 * MIB)
WIDE = pltpu.CompilerParams(vmem_limit_bytes=32 * MIB)
VMEM = pl.BlockSpec(memory_space=pltpu.VMEM)
ANY = pl.BlockSpec(memory_space=pl.ANY)


def spans(width, shares=FORTH):
    unit = width // sum(shares)
    return [(sum(shares[:k]) * unit, n * unit) for k, n in enumerate(shares)]


def choices(ids, plane):
    tokens = ids.shape[1]
    line = lax.broadcasted_iota(jnp.int32, (EXPERTS * CAP, tokens), 0)
    expert = lax.rem(line // CAP + plane, EXPERTS)
    slot = (line % CAP).astype(jnp.float32)
    first = ids[0:1, :] == expert
    second = ids[1:2, :] == expert
    named = (first | second).astype(jnp.float32)
    square = (tokens, tokens)
    earlier = lax.broadcasted_iota(jnp.int32, square, 0) < lax.broadcasted_iota(
        jnp.int32, square, 1
    )
    rank = jnp.dot(named, earlier.astype(jnp.float32), preferred_element_type=jnp.float32)
    here = rank == slot
    return first & here, second & here


def pack_kernel(group, ids_ref, act_ref, gain_ref, *out_refs):
    plane = lax.axis_index("expert") // group
    values = act_ref[...].astype(jnp.float32)
    mean_sq = jnp.mean(values * values, axis=-1, keepdims=True)
    normed = (values * lax.rsqrt(mean_sq + 1e-06) * gain_ref[...]).astype(jnp.bfloat16)
    first, second = choices(ids_ref[...], plane)
    pick = (first | second).astype(jnp.float32).astype(jnp.bfloat16)
    rows = jnp.dot(pick, normed, preferred_element_type=jnp.float32).astype(jnp.bfloat16)
    out_refs[0][...] = rows[:CAP]
    for j, out_ref in enumerate(out_refs[1:]):
        k, s = j // (EXPERTS - 1), j % (EXPERTS - 1) + 1
        at, part = spans(rows.shape[1])[k]
        out_ref[...] = rows[s * CAP : (s + 1) * CAP, at : at + part]


def pack(group, ids, activations, gain):
    width = activations.shape[1]
    widths = [width] + [part for _, part in spans(width) for _ in range(EXPERTS - 1)]
    operands = [ids, activations, gain.reshape(1, width)]
    return pl.pallas_call(
        functools.partial(pack_kernel, group),
        grid=(1,),
        in_specs=[pl.BlockSpec(x.shape, lambda i: (0, 0)) for x in operands],
        out_specs=[pl.BlockSpec((CAP, n), lambda i: (0, 0)) for n in widths],
        out_shape=[jax.ShapeDtypeStruct((CAP, n), jnp.bfloat16) for n in widths],
        compiler_params=LIMIT,
        name="norm_and_pack",
    )(*[pltpu.with_memory_space_constraint(x, pltpu.HBM) for x in operands])


def fetches(weights, at, held, sems):
    copies = []
    for j, w in enumerate(weights):
        part = held[j].shape[1]
        for b in range(sems.shape[1]):
            rows = pl.ds(b * FETCH_ROWS, FETCH_ROWS)
            copies.append(
                pltpu.make_async_copy(w.at[rows, at : at + part], held[j].at[rows], sems.at[j, b])
            )
    return copies


def fetch_kernel(at, w_ref, after_ref, held_ref, sems):
    copies = fetches([w_ref], at, [held_ref], sems)
    for copy in copies:
        copy.start()
    for copy in copies:
        copy.wait()


def fetch(w, at, part, after):
    rows = w.shape[0]
    return pl.pallas_call(
        functools.partial(fetch_kernel, at),
        in_specs=[ANY, ANY],
        out_specs=VMEM,
        out_shape=pltpu.VMEM((rows, part), jnp.bfloat16),
        scratch_shapes=[pltpu.SemaphoreType.DMA((1, rows // FETCH_ROWS))],
        compiler_params=LIMIT,
        cost_estimate=pl.CostEstimate(flops=0, bytes_accessed=4 * rows * part, transcendentals=0),
        name="fetch",
    )(pltpu.with_memory_space_constraint(w, pltpu.HBM), after)


def relay_kernel(count, *refs):
    for x_ref, out_ref in zip(refs[:count], refs[count + 1 :]):
        out_ref[...] = x_ref[...]


def relay(arrays, after):
    count = len(arrays)
    return pl.pallas_call(
        functools.partial(relay_kernel, count),
        in_specs=[VMEM] * count + [ANY],
        out_specs=[VMEM] * count,
        out_shape=[jax.ShapeDtypeStruct(x.shape, x.dtype) for x in arrays],
        compiler_params=LIMIT,
        cost_estimate=pl.CostEstimate(flops=0, bytes_accessed=16 * MIB, transcendentals=0),
        name="relay",
    )(*arrays, after)


def gate_up_kernel(count, ahead, at, ahead_at, begin, end, *refs):
    pieces, refs = refs[:count], refs[count:]
    weights, later, refs = refs[:2], refs[2 : 2 + ahead], refs[2 + ahead :]
    if not begin:
        before, refs = refs[:2], refs[2:]
    held, refs = refs[:ahead], refs[ahead:]
    turned, sems, refs = *refs[-2:], refs[:-2]
    if end:
        hidden_ref, refs = refs[0], refs[1:]
    sums = refs
    part, rows = turned.shape
    copies = fetches(later, ahead_at, held, sems)
    for copy in copies:
        copy.start()

    @pl.loop(0, part // BLOCK)
    def _(c):
        parts = []
        for p in pieces:
            first = c * BLOCK + (at if p.shape[1] > part else 0)
            parts.append(p[:, pl.ds(pl.multiple_of(first, BLOCK), BLOCK)])
        turned[pl.ds(pl.multiple_of(c * BLOCK, BLOCK), BLOCK), :] = jnp.concatenate(parts, axis=0).T

    for j in range(2):
        total = jnp.dot(weights[j][...], turned[...], preferred_element_type=jnp.float32)
        sums[j][...] = total if begin else total + before[j][...]
    if end:
        hidden = (jax.nn.silu(sums[0][...]) * sums[1][...]).astype(jnp.bfloat16)
        hidden_ref[...] = hidden.T
    for copy in copies:
        copy.wait()


def gate_up(k, pieces, weights, later, ahead, totals):
    hidden, part = weights[0].shape
    begin, end = k == 0, k == HALVES - 1
    width = later[0].shape[1]
    rows = sum(p.shape[0] for p in pieces)
    total = jax.ShapeDtypeStruct((hidden, rows), jnp.float32)
    out_shape = [pltpu.VMEM((hidden, ahead[1]), jnp.bfloat16)] * len(later)
    out_specs = [VMEM] * len(later)
    scratch = []
    if end:
        out_shape.append(jax.ShapeDtypeStruct((rows, hidden), jnp.bfloat16))
        scratch += [pltpu.VMEM((hidden, rows), jnp.float32)] * 2
    else:
        out_shape += [total] * 2
    out_specs += [VMEM] * (len(out_shape) - len(later))
    scratch.append(pltpu.VMEM((part, rows), jnp.bfloat16))
    scratch.append(pltpu.SemaphoreType.DMA((len(later), hidden // FETCH_ROWS)))
    weights = [pltpu.with_memory_space_constraint(w, pltpu.VMEM) for w in weights]
    later = [pltpu.with_memory_space_constraint(w, pltpu.HBM) for w in later]
    out = pl.pallas_call(
        functools.partial(
            gate_up_kernel, len(pieces), len(later), spans(width)[k][0], ahead[0], begin, end
        ),
        in_specs=[VMEM] * (len(pieces) + 2) + [ANY] * len(later) + [VMEM] * len(totals),
        out_specs=out_specs,
        out_shape=out_shape,
        scratch_shapes=scratch,
        compiler_params=LIMIT if rows <= 256 else WIDE,
        cost_estimate=pl.CostEstimate(
            flops=4 * rows * hidden * part,
            bytes_accessed=4 * hidden * part + 8 * rows * hidden,
            transcendentals=0,
        ),
        name="gate_up",
    )(*pieces, *weights, *later, *totals)
    return out[: len(later)], out[len(later) :]


def down_kernel(ahead, segments, hidden_ref, *refs):
    weights, refs = refs[: len(segments)], refs[len(segments) :]
    later, held, refs = refs[:ahead], refs[ahead : 2 * ahead], refs[2 * ahead :]
    keep_ref, send_ref, sems = refs
    half, part = keep_ref.shape
    copies = fetches(later, AHEAD * BLOCK, held, sems)
    for copy in copies:
        copy.start()
    done = 0
    for w_ref, (first, size) in zip(weights, segments):
        block = size // 2

        @pl.loop(0, 2)
        def _(c, first=first, done=done, block=block, w_ref=w_ref):
            columns = pl.ds(pl.multiple_of(first + c * block, BLOCK), block)
            out = jnp.dot(hidden_ref[...], w_ref[:, columns], preferred_element_type=jnp.float32)
            out = out.astype(jnp.bfloat16)
            columns = pl.ds(pl.multiple_of(done + c * block, BLOCK), block)
            keep_ref[:, columns] = out[:half]
            send_ref[:, columns] = out[half:]

        done += size
    for copy in copies:
        copy.wait()


def down(hidden, weights, segments, later):
    rows, depth = hidden.shape
    part = sum(size for _, size in segments)
    ahead = len(later)
    out_shape = [pltpu.VMEM((depth, w.shape[1] - AHEAD * BLOCK), jnp.bfloat16) for w in later]
    out_shape += [jax.ShapeDtypeStruct((rows // 2, part), jnp.bfloat16)] * 2
    weights = [pltpu.with_memory_space_constraint(w, pltpu.VMEM) for w in weights]
    later = [pltpu.with_memory_space_constraint(w, pltpu.HBM) for w in later]
    out = pl.pallas_call(
        functools.partial(down_kernel, ahead, segments),
        in_specs=[VMEM] * (1 + len(weights)) + [ANY] * ahead,
        out_specs=[VMEM] * (ahead + 2),
        out_shape=out_shape,
        scratch_shapes=[pltpu.SemaphoreType.DMA((max(ahead, 1), depth // FETCH_ROWS))],
        compiler_params=LIMIT if rows <= 256 else WIDE,
        cost_estimate=pl.CostEstimate(
            flops=2 * rows * depth * part,
            bytes_accessed=2 * (depth * part + rows * depth + rows * part),
            transcendentals=0,
        ),
        name="down",
    )(hidden, *weights, *later)
    return out[:ahead], out[ahead:]


def mix_kernel(group, ids_ref, logits_ref, act_ref, arrived, near, last, *refs):
    out_ref, kept, middle_rows = refs[-1], refs[:HALVES], refs[HALVES:-1]
    plane = lax.axis_index("expert") // group
    first, second = choices(ids_ref[...], plane)
    lead = logits_ref[0:1, :] - logits_ref[1:2, :]
    weight = jnp.where(first, jax.nn.sigmoid(lead), 0.0)
    weight = (weight + jnp.where(second, jax.nn.sigmoid(-lead), 0.0)).T
    tokens = weight.shape[0]
    high = weight.astype(jnp.bfloat16).astype(jnp.float32)
    middle = (weight - high).astype(jnp.bfloat16).astype(jnp.float32)
    terms = jnp.concatenate([weight - high - middle, middle, high], axis=0).astype(jnp.bfloat16)
    for k, (at, part) in enumerate(spans(act_ref.shape[1], BACK)):
        columns = slice(at, at + part)
        own = kept[k][...].astype(jnp.float32) + arrived[:, columns].astype(jnp.float32)
        blocks = [own.astype(jnp.bfloat16), near[:, columns], middle_rows[k][...]]
        rows = jnp.concatenate(blocks + [last[:, columns]], axis=0)
        sums = jnp.dot(terms, rows, preferred_element_type=jnp.float32)
        total = act_ref[:, columns].astype(jnp.float32)
        for j in range(3):
            total = total + sums[j * tokens : (j + 1) * tokens]
        out_ref[:, columns] = total.astype(jnp.bfloat16)


def mix(group, ids, logits, activations, pieces):
    return pl.pallas_call(
        functools.partial(mix_kernel, group),
        out_shape=jax.ShapeDtypeStruct(activations.shape, jnp.bfloat16),
        compiler_params=LIMIT,
        name="mix",
    )(ids, logits, activations, *pieces)


def added(mine, arrived):
    total = mine.astype(jnp.float32) + arrived.astype(jnp.float32)
    return total.astype(jnp.bfloat16)


def on_device(activations, expert_ids, route_logits, norm_gain, w_gate, w_up, w_down):
    devices = lax.axis_size("expert")
    group = devices // EXPERTS
    far = group // 2
    width = activations.shape[1]
    part = width // HALVES

    def shift(x, s):
        return lax.ppermute(
            x, "expert", [(i, (i + s * group) % devices) for i in range(devices)]
        )

    def swap(x, bit):
        return lax.ppermute(x, "expert", [(i, i ^ bit) for i in range(devices)])

    def after(x, *others):
        return lax.optimization_barrier((x, *others))[0]

    others = EXPERTS - 1
    ids = expert_ids.T
    own, *sends = pack(group, ids, activations, norm_gain)
    far_own = swap(own, far)
    now = [fetch(w, 0, spans(width)[0][1], own) for w in (w_gate, w_up)]
    blocks = []
    for k in range(HALVES):
        x = sends[k * others : (k + 1) * others]
        if k:
            x = relay(after(x, *now, far_own), blocks[-1])
        arrivals = [shift(x[s - 1], s) for s in ORDER]
        blocks.append(jnp.concatenate(arrivals, axis=0))
    totals = []
    for k in range(HALVES):
        at, size = spans(width)[k]
        columns = slice(at, at + size)
        far_block = swap(blocks[k], far)
        if totals:
            far_block, totals = lax.optimization_barrier((far_block, totals))
        pieces = [own[:, columns], blocks[k], far_own[:, columns], far_block]
        bit = far // 2
        while bit:
            pieces.append(swap(jnp.concatenate(pieces, axis=0), bit))
            bit //= 2
        pieces[0], pieces[2] = own, far_own
        if k < HALVES - 1:
            pieces[1] = after(pieces[1], blocks[k + 1])
        later, ahead = [w_gate, w_up], (size, width - size)
        if k == HALVES - 1:
            later, ahead = [w_down], (0, AHEAD * BLOCK)
        now, totals = gate_up(k, pieces, now, later, ahead, totals)
    hidden = totals[0]
    held = []
    early = AHEAD * BLOCK
    for k, (at, size) in enumerate(spans(width, BACK)):
        if k == 0:
            rest, (keep, send) = down(hidden, now, [(at, size)], [w_down])
        else:
            segments = [(at, early - at), (0, width - early)]
            _, (keep, send) = down(hidden, [*now, *rest], segments, [])
        bit = 1
        while bit < far:
            total = added(keep, swap(send, bit))
            keep, send = total[: total.shape[0] // 2], total[total.shape[0] // 2 :]
            bit *= 2
        held.append([total[j * CAP : (j + 1) * CAP] for j in range(2 * EXPERTS)])
    place = {s: 1 + j for j, s in enumerate(ORDER)}
    crossed = [swap(h[EXPERTS + place[2]], far) for h in held]
    middle = [shift(added(h[place[2]], x), -2) for h, x in zip(held, crossed)]
    mine = [jnp.concatenate([h[j] for h in held], axis=1) for j in range(2 * EXPERTS)]
    back = {}
    back[1] = swap(after(mine[EXPERTS + place[1]], crossed[1]), far)
    back[3] = swap(after(mine[EXPERTS + place[3]], crossed[0]), far)
    back[0] = swap(after(mine[EXPERTS], back[1], back[3]), far)
    near = shift(after(added(mine[place[1]], back[1]), middle[1]), -1)
    last = shift(after(added(mine[place[3]], back[3]), middle[0]), -3)
    arrived = back[0]
    pieces = [arrived, near, last, *[h[0] for h in held], *middle]
    return mix(group, ids, route_logits.T, activations, pieces)


def solution(mesh):
    in_specs = (
        P(("parts", "expert"), None),
        P(("parts", "expert"), None),
        P(("parts", "expert"), None),
        P(),
        P("expert", None),
        P("expert", None),
        P("expert", None),
    )
    out_specs = P(("parts", "expert"), None)
    return jax.shard_map(
        on_device, mesh=mesh, in_specs=in_specs, out_specs=out_specs, check_vma=False
    )
```

```python
import functools

import jax
import jax.numpy as jnp
from jax import lax
from jax.experimental import pallas as pl
from jax.experimental.pallas import tpu as pltpu
from jax.sharding import PartitionSpec as P

EXPERTS = 4
CAP = 16
HALVES = 2
ORDER = (1, 2, 3)
FORTH = (7, 5)
BACK = (1, 1)
BLOCK = 512
AHEAD = 8
FETCH_ROWS = 144
MIB = 1 << 20
LIMIT = pltpu.CompilerParams(vmem_limit_bytes=10 * MIB)
WIDE = pltpu.CompilerParams(vmem_limit_bytes=32 * MIB)
VMEM = pl.BlockSpec(memory_space=pltpu.VMEM)
ANY = pl.BlockSpec(memory_space=pl.ANY)


def spans(width, shares=FORTH):
    unit = width // sum(shares)
    return [(sum(shares[:k]) * unit, n * unit) for k, n in enumerate(shares)]


def choices(ids, plane):
    tokens = ids.shape[1]
    line = lax.broadcasted_iota(jnp.int32, (EXPERTS * CAP, tokens), 0)
    expert = lax.rem(line // CAP + plane, EXPERTS)
    slot = (line % CAP).astype(jnp.float32)
    first = ids[0:1, :] == expert
    second = ids[1:2, :] == expert
    named = (first | second).astype(jnp.float32)
    square = (tokens, tokens)
    earlier = lax.broadcasted_iota(jnp.int32, square, 0) < lax.broadcasted_iota(
        jnp.int32, square, 1
    )
    rank = jnp.dot(named, earlier.astype(jnp.float32), preferred_element_type=jnp.float32)
    here = rank == slot
    return first & here, second & here


def pack_kernel(group, ids_ref, act_ref, gain_ref, *out_refs):
    plane = lax.axis_index("expert") // group
    values = act_ref[...].astype(jnp.float32)
    mean_sq = jnp.mean(values * values, axis=-1, keepdims=True)
    normed = (values * lax.rsqrt(mean_sq + 1e-06) * gain_ref[...]).astype(jnp.bfloat16)
    first, second = choices(ids_ref[...], plane)
    pick = (first | second).astype(jnp.float32).astype(jnp.bfloat16)
    rows = jnp.dot(pick, normed, preferred_element_type=jnp.float32).astype(jnp.bfloat16)
    out_refs[0][...] = rows[:CAP]
    for j, out_ref in enumerate(out_refs[1:]):
        k, s = j // (EXPERTS - 1), j % (EXPERTS - 1) + 1
        at, part = spans(rows.shape[1])[k]
        out_ref[...] = rows[s * CAP : (s + 1) * CAP, at : at + part]


def pack(group, ids, activations, gain):
    width = activations.shape[1]
    widths = [width] + [part for _, part in spans(width) for _ in range(EXPERTS - 1)]
    operands = [ids, activations, gain.reshape(1, width)]
    return pl.pallas_call(
        functools.partial(pack_kernel, group),
        grid=(1,),
        in_specs=[pl.BlockSpec(x.shape, lambda i: (0, 0)) for x in operands],
        out_specs=[pl.BlockSpec((CAP, n), lambda i: (0, 0)) for n in widths],
        out_shape=[jax.ShapeDtypeStruct((CAP, n), jnp.bfloat16) for n in widths],
        compiler_params=LIMIT,
        name="norm_and_pack",
    )(*[pltpu.with_memory_space_constraint(x, pltpu.HBM) for x in operands])


def fetches(weights, at, held, sems):
    copies = []
    for j, w in enumerate(weights):
        part = held[j].shape[1]
        for b in range(sems.shape[1]):
            rows = pl.ds(b * FETCH_ROWS, FETCH_ROWS)
            copies.append(
                pltpu.make_async_copy(w.at[rows, at : at + part], held[j].at[rows], sems.at[j, b])
            )
    return copies


def fetch_kernel(at, w_ref, after_ref, held_ref, sems):
    copies = fetches([w_ref], at, [held_ref], sems)
    for copy in copies:
        copy.start()
    for copy in copies:
        copy.wait()


def fetch(w, at, part, after):
    rows = w.shape[0]
    return pl.pallas_call(
        functools.partial(fetch_kernel, at),
        in_specs=[ANY, ANY],
        out_specs=VMEM,
        out_shape=pltpu.VMEM((rows, part), jnp.bfloat16),
        scratch_shapes=[pltpu.SemaphoreType.DMA((1, rows // FETCH_ROWS))],
        compiler_params=LIMIT,
        cost_estimate=pl.CostEstimate(flops=0, bytes_accessed=4 * rows * part, transcendentals=0),
        name="fetch",
    )(pltpu.with_memory_space_constraint(w, pltpu.HBM), after)


def relay_kernel(count, *refs):
    for x_ref, out_ref in zip(refs[:count], refs[count + 1 :]):
        out_ref[...] = x_ref[...]


def relay(arrays, after):
    count = len(arrays)
    return pl.pallas_call(
        functools.partial(relay_kernel, count),
        in_specs=[VMEM] * count + [ANY],
        out_specs=[VMEM] * count,
        out_shape=[jax.ShapeDtypeStruct(x.shape, x.dtype) for x in arrays],
        compiler_params=LIMIT,
        cost_estimate=pl.CostEstimate(flops=0, bytes_accessed=16 * MIB, transcendentals=0),
        name="relay",
    )(*arrays, after)


def gate_up_kernel(count, ahead, at, ahead_at, begin, end, *refs):
    pieces, refs = refs[:count], refs[count:]
    weights, later, refs = refs[:2], refs[2 : 2 + ahead], refs[2 + ahead :]
    if not begin:
        before, refs = refs[:2], refs[2:]
    held, refs = refs[:ahead], refs[ahead:]
    turned, sems, refs = *refs[-2:], refs[:-2]
    if end:
        hidden_ref, refs = refs[0], refs[1:]
    sums = refs
    part, rows = turned.shape
    copies = fetches(later, ahead_at, held, sems)
    for copy in copies:
        copy.start()

    @pl.loop(0, part // BLOCK)
    def _(c):
        parts = []
        for p in pieces:
            first = c * BLOCK + (at if p.shape[1] > part else 0)
            parts.append(p[:, pl.ds(pl.multiple_of(first, BLOCK), BLOCK)])
        turned[pl.ds(pl.multiple_of(c * BLOCK, BLOCK), BLOCK), :] = jnp.concatenate(parts, axis=0).T

    for j in range(2):
        total = jnp.dot(weights[j][...], turned[...], preferred_element_type=jnp.float32)
        sums[j][...] = total if begin else total + before[j][...]
    if end:
        hidden = (jax.nn.silu(sums[0][...]) * sums[1][...]).astype(jnp.bfloat16)
        hidden_ref[...] = hidden.T
    for copy in copies:
        copy.wait()


def gate_up(k, pieces, weights, later, ahead, totals):
    hidden, part = weights[0].shape
    begin, end = k == 0, k == HALVES - 1
    width = later[0].shape[1]
    rows = sum(p.shape[0] for p in pieces)
    total = jax.ShapeDtypeStruct((hidden, rows), jnp.float32)
    out_shape = [pltpu.VMEM((hidden, ahead[1]), jnp.bfloat16)] * len(later)
    out_specs = [VMEM] * len(later)
    scratch = []
    if end:
        out_shape.append(jax.ShapeDtypeStruct((rows, hidden), jnp.bfloat16))
        scratch += [pltpu.VMEM((hidden, rows), jnp.float32)] * 2
    else:
        out_shape += [total] * 2
    out_specs += [VMEM] * (len(out_shape) - len(later))
    scratch.append(pltpu.VMEM((part, rows), jnp.bfloat16))
    scratch.append(pltpu.SemaphoreType.DMA((len(later), hidden // FETCH_ROWS)))
    weights = [pltpu.with_memory_space_constraint(w, pltpu.VMEM) for w in weights]
    later = [pltpu.with_memory_space_constraint(w, pltpu.HBM) for w in later]
    out = pl.pallas_call(
        functools.partial(
            gate_up_kernel, len(pieces), len(later), spans(width)[k][0], ahead[0], begin, end
        ),
        in_specs=[VMEM] * (len(pieces) + 2) + [ANY] * len(later) + [VMEM] * len(totals),
        out_specs=out_specs,
        out_shape=out_shape,
        scratch_shapes=scratch,
        compiler_params=LIMIT if rows <= 256 else WIDE,
        cost_estimate=pl.CostEstimate(
            flops=4 * rows * hidden * part,
            bytes_accessed=4 * hidden * part + 8 * rows * hidden,
            transcendentals=0,
        ),
        name="gate_up",
    )(*pieces, *weights, *later, *totals)
    return out[: len(later)], out[len(later) :]


def down_kernel(ahead, segments, hidden_ref, *refs):
    weights, refs = refs[: len(segments)], refs[len(segments) :]
    later, held, refs = refs[:ahead], refs[ahead : 2 * ahead], refs[2 * ahead :]
    keep_ref, send_ref, sems = refs
    half, part = keep_ref.shape
    copies = fetches(later, AHEAD * BLOCK, held, sems)
    for copy in copies:
        copy.start()
    done = 0
    for w_ref, (first, size) in zip(weights, segments):
        block = size // 2

        @pl.loop(0, 2)
        def _(c, first=first, done=done, block=block, w_ref=w_ref):
            columns = pl.ds(pl.multiple_of(first + c * block, BLOCK), block)
            out = jnp.dot(hidden_ref[...], w_ref[:, columns], preferred_element_type=jnp.float32)
            out = out.astype(jnp.bfloat16)
            columns = pl.ds(pl.multiple_of(done + c * block, BLOCK), block)
            keep_ref[:, columns] = out[:half]
            send_ref[:, columns] = out[half:]

        done += size
    for copy in copies:
        copy.wait()


def down(hidden, weights, segments, later):
    rows, depth = hidden.shape
    part = sum(size for _, size in segments)
    ahead = len(later)
    out_shape = [pltpu.VMEM((depth, w.shape[1] - AHEAD * BLOCK), jnp.bfloat16) for w in later]
    out_shape += [jax.ShapeDtypeStruct((rows // 2, part), jnp.bfloat16)] * 2
    weights = [pltpu.with_memory_space_constraint(w, pltpu.VMEM) for w in weights]
    later = [pltpu.with_memory_space_constraint(w, pltpu.HBM) for w in later]
    out = pl.pallas_call(
        functools.partial(down_kernel, ahead, segments),
        in_specs=[VMEM] * (1 + len(weights)) + [ANY] * ahead,
        out_specs=[VMEM] * (ahead + 2),
        out_shape=out_shape,
        scratch_shapes=[pltpu.SemaphoreType.DMA((max(ahead, 1), depth // FETCH_ROWS))],
        compiler_params=LIMIT if rows <= 256 else WIDE,
        cost_estimate=pl.CostEstimate(
            flops=2 * rows * depth * part,
            bytes_accessed=2 * (depth * part + rows * depth + rows * part),
            transcendentals=0,
        ),
        name="down",
    )(hidden, *weights, *later)
    return out[:ahead], out[ahead:]


def mix_kernel(group, ids_ref, logits_ref, act_ref, arrived, near, last, *refs):
    out_ref, kept, middle_rows = refs[-1], refs[:HALVES], refs[HALVES:-1]
    plane = lax.axis_index("expert") // group
    first, second = choices(ids_ref[...], plane)
    lead = logits_ref[0:1, :] - logits_ref[1:2, :]
    weight = jnp.where(first, jax.nn.sigmoid(lead), 0.0)
    weight = (weight + jnp.where(second, jax.nn.sigmoid(-lead), 0.0)).T
    tokens = weight.shape[0]
    high = weight.astype(jnp.bfloat16).astype(jnp.float32)
    middle = (weight - high).astype(jnp.bfloat16).astype(jnp.float32)
    terms = jnp.concatenate([weight - high - middle, middle, high], axis=0).astype(jnp.bfloat16)
    for k, (at, part) in enumerate(spans(act_ref.shape[1], BACK)):
        columns = slice(at, at + part)
        own = kept[k][...].astype(jnp.float32) + arrived[:, columns].astype(jnp.float32)
        blocks = [own.astype(jnp.bfloat16), near[:, columns], middle_rows[k][...]]
        rows = jnp.concatenate(blocks + [last[:, columns]], axis=0)
        sums = jnp.dot(terms, rows, preferred_element_type=jnp.float32)
        total = act_ref[:, columns].astype(jnp.float32)
        for j in range(3):
            total = total + sums[j * tokens : (j + 1) * tokens]
        out_ref[:, columns] = total.astype(jnp.bfloat16)


def mix(group, ids, logits, activations, pieces):
    return pl.pallas_call(
        functools.partial(mix_kernel, group),
        out_shape=jax.ShapeDtypeStruct(activations.shape, jnp.bfloat16),
        compiler_params=LIMIT,
        name="mix",
    )(ids, logits, activations, *pieces)


def added(mine, arrived):
    total = mine.astype(jnp.float32) + arrived.astype(jnp.float32)
    return total.astype(jnp.bfloat16)


def on_device(activations, expert_ids, route_logits, norm_gain, w_gate, w_up, w_down):
    devices = lax.axis_size("expert")
    group = devices // EXPERTS
    far = group // 2
    width = activations.shape[1]
    part = width // HALVES

    def shift(x, s):
        return lax.ppermute(
            x, "expert", [(i, (i + s * group) % devices) for i in range(devices)]
        )

    def swap(x, bit):
        return lax.ppermute(x, "expert", [(i, i ^ bit) for i in range(devices)])

    def after(x, *others):
        return lax.optimization_barrier((x, *others))[0]

    others = EXPERTS - 1
    ids = expert_ids.T
    own, *sends = pack(group, ids, activations, norm_gain)
    far_own = swap(own, far)
    now = [fetch(w, 0, spans(width)[0][1], own) for w in (w_gate, w_up)]
    blocks = []
    for k in range(HALVES):
        x = sends[k * others : (k + 1) * others]
        if k:
            x = relay(after(x, *now, far_own), blocks[-1])
        arrivals = [shift(x[s - 1], s) for s in ORDER]
        blocks.append(jnp.concatenate(arrivals, axis=0))
    totals = []
    for k in range(HALVES):
        at, size = spans(width)[k]
        columns = slice(at, at + size)
        far_block = swap(blocks[k], far)
        if totals:
            far_block, totals = lax.optimization_barrier((far_block, totals))
        pieces = [own[:, columns], blocks[k], far_own[:, columns], far_block]
        bit = far // 2
        while bit:
            if k and len(pieces) == EXPERTS:
                early = swap(jnp.concatenate(pieces[:-1], axis=0), bit)
                pieces += [early, swap(far_block, bit)]
            else:
                pieces.append(swap(jnp.concatenate(pieces, axis=0), bit))
            bit //= 2
        pieces[0], pieces[2] = own, far_own
        if k < HALVES - 1:
            pieces[1] = after(pieces[1], blocks[k + 1])
        later, ahead = [w_gate, w_up], (size, width - size)
        if k == HALVES - 1:
            later, ahead = [w_down], (0, AHEAD * BLOCK)
        now, totals = gate_up(k, pieces, now, later, ahead, totals)
    hidden = totals[0]
    held = []
    early = AHEAD * BLOCK
    for k, (at, size) in enumerate(spans(width, BACK)):
        if k == 0:
            rest, (keep, send) = down(hidden, now, [(at, size)], [w_down])
        else:
            segments = [(at, early - at), (0, width - early)]
            _, (keep, send) = down(hidden, [*now, *rest], segments, [])
        bit = 1
        while bit < far:
            total = added(keep, swap(send, bit))
            keep, send = total[: total.shape[0] // 2], total[total.shape[0] // 2 :]
            bit *= 2
        held.append([total[j * CAP : (j + 1) * CAP] for j in range(2 * EXPERTS)])
    place = {s: 1 + j for j, s in enumerate(ORDER)}
    crossed = [swap(h[EXPERTS + place[2]], far) for h in held]
    middle = [shift(added(h[place[2]], x), -2) for h, x in zip(held, crossed)]
    mine = [jnp.concatenate([h[j] for h in held], axis=1) for j in range(2 * EXPERTS)]
    back = {}
    back[1] = swap(after(mine[EXPERTS + place[1]], crossed[1]), far)
    back[3] = swap(after(mine[EXPERTS + place[3]], crossed[0]), far)
    back[0] = swap(after(mine[EXPERTS], back[1], back[3]), far)
    near = shift(after(added(mine[place[1]], back[1]), middle[1]), -1)
    last = shift(after(added(mine[place[3]], back[3]), middle[0]), -3)
    arrived = back[0]
    pieces = [arrived, near, last, *[h[0] for h in held], *middle]
    return mix(group, ids, route_logits.T, activations, pieces)


def solution(mesh):
    in_specs = (
        P(("parts", "expert"), None),
        P(("parts", "expert"), None),
        P(("parts", "expert"), None),
        P(),
        P("expert", None),
        P("expert", None),
        P("expert", None),
    )
    out_specs = P(("parts", "expert"), None)
    return jax.shard_map(
        on_device, mesh=mesh, in_specs=in_specs, out_specs=out_specs, check_vma=False
    )
```

```python
import functools

import jax
import jax.numpy as jnp
from jax import lax
from jax.experimental import pallas as pl
from jax.experimental.pallas import tpu as pltpu
from jax.sharding import PartitionSpec as P

EXPERTS = 4
CAP = 16
HALVES = 2
ORDER = (1, 2, 3)
FORTH = (7, 5)
BACK = (1, 1)
BLOCK = 512
AHEAD = 8
FETCH_ROWS = 144
MIB = 1 << 20
LIMIT = pltpu.CompilerParams(vmem_limit_bytes=10 * MIB)
WIDE = pltpu.CompilerParams(vmem_limit_bytes=32 * MIB)
VMEM = pl.BlockSpec(memory_space=pltpu.VMEM)
ANY = pl.BlockSpec(memory_space=pl.ANY)


def spans(width, shares=FORTH):
    unit = width // sum(shares)
    return [(sum(shares[:k]) * unit, n * unit) for k, n in enumerate(shares)]


def choices(ids, plane):
    tokens = ids.shape[1]
    line = lax.broadcasted_iota(jnp.int32, (EXPERTS * CAP, tokens), 0)
    expert = lax.rem(line // CAP + plane, EXPERTS)
    slot = (line % CAP).astype(jnp.float32)
    first = ids[0:1, :] == expert
    second = ids[1:2, :] == expert
    named = (first | second).astype(jnp.float32)
    square = (tokens, tokens)
    earlier = lax.broadcasted_iota(jnp.int32, square, 0) < lax.broadcasted_iota(
        jnp.int32, square, 1
    )
    rank = jnp.dot(named, earlier.astype(jnp.float32), preferred_element_type=jnp.float32)
    here = rank == slot
    return first & here, second & here


def pack_kernel(group, ids_ref, act_ref, gain_ref, *out_refs):
    plane = lax.axis_index("expert") // group
    values = act_ref[...].astype(jnp.float32)
    mean_sq = jnp.mean(values * values, axis=-1, keepdims=True)
    normed = (values * lax.rsqrt(mean_sq + 1e-06) * gain_ref[...]).astype(jnp.bfloat16)
    first, second = choices(ids_ref[...], plane)
    pick = (first | second).astype(jnp.float32).astype(jnp.bfloat16)
    rows = jnp.dot(pick, normed, preferred_element_type=jnp.float32).astype(jnp.bfloat16)
    out_refs[0][...] = rows[:CAP]
    for j, out_ref in enumerate(out_refs[1:]):
        k, s = j // (EXPERTS - 1), j % (EXPERTS - 1) + 1
        at, part = spans(rows.shape[1])[k]
        out_ref[...] = rows[s * CAP : (s + 1) * CAP, at : at + part]


def pack(group, ids, activations, gain):
    width = activations.shape[1]
    widths = [width] + [part for _, part in spans(width) for _ in range(EXPERTS - 1)]
    operands = [ids, activations, gain.reshape(1, width)]
    return pl.pallas_call(
        functools.partial(pack_kernel, group),
        grid=(1,),
        in_specs=[pl.BlockSpec(x.shape, lambda i: (0, 0)) for x in operands],
        out_specs=[pl.BlockSpec((CAP, n), lambda i: (0, 0)) for n in widths],
        out_shape=[jax.ShapeDtypeStruct((CAP, n), jnp.bfloat16) for n in widths],
        compiler_params=LIMIT,
        name="norm_and_pack",
    )(*[pltpu.with_memory_space_constraint(x, pltpu.HBM) for x in operands])


def fetches(weights, at, held, sems):
    copies = []
    for j, w in enumerate(weights):
        part = held[j].shape[1]
        for b in range(sems.shape[1]):
            rows = pl.ds(b * FETCH_ROWS, FETCH_ROWS)
            copies.append(
                pltpu.make_async_copy(w.at[rows, at : at + part], held[j].at[rows], sems.at[j, b])
            )
    return copies


def fetch_kernel(at, w_ref, after_ref, held_ref, sems):
    copies = fetches([w_ref], at, [held_ref], sems)
    for copy in copies:
        copy.start()
    for copy in copies:
        copy.wait()


def fetch(w, at, part, after):
    rows = w.shape[0]
    return pl.pallas_call(
        functools.partial(fetch_kernel, at),
        in_specs=[ANY, ANY],
        out_specs=VMEM,
        out_shape=pltpu.VMEM((rows, part), jnp.bfloat16),
        scratch_shapes=[pltpu.SemaphoreType.DMA((1, rows // FETCH_ROWS))],
        compiler_params=LIMIT,
        cost_estimate=pl.CostEstimate(flops=0, bytes_accessed=4 * rows * part, transcendentals=0),
        name="fetch",
    )(pltpu.with_memory_space_constraint(w, pltpu.HBM), after)


def relay_kernel(count, *refs):
    for x_ref, out_ref in zip(refs[:count], refs[count + 1 :]):
        out_ref[...] = x_ref[...]


def relay(arrays, after):
    count = len(arrays)
    return pl.pallas_call(
        functools.partial(relay_kernel, count),
        in_specs=[VMEM] * count + [ANY],
        out_specs=[VMEM] * count,
        out_shape=[jax.ShapeDtypeStruct(x.shape, x.dtype) for x in arrays],
        compiler_params=LIMIT,
        cost_estimate=pl.CostEstimate(flops=0, bytes_accessed=16 * MIB, transcendentals=0),
        name="relay",
    )(*arrays, after)


def gate_up_kernel(count, ahead, at, ahead_at, begin, end, *refs):
    pieces, refs = refs[:count], refs[count:]
    weights, later, refs = refs[:2], refs[2 : 2 + ahead], refs[2 + ahead :]
    if not begin:
        before, refs = refs[:2], refs[2:]
    held, refs = refs[:ahead], refs[ahead:]
    turned, sems, refs = *refs[-2:], refs[:-2]
    if end:
        hidden_ref, refs = refs[0], refs[1:]
    sums = refs
    part, rows = turned.shape
    copies = fetches(later, ahead_at, held, sems)
    for copy in copies:
        copy.start()

    @pl.loop(0, part // BLOCK)
    def _(c):
        parts = []
        for p in pieces:
            first = c * BLOCK + (at if p.shape[1] > part else 0)
            parts.append(p[:, pl.ds(pl.multiple_of(first, BLOCK), BLOCK)])
        turned[pl.ds(pl.multiple_of(c * BLOCK, BLOCK), BLOCK), :] = jnp.concatenate(parts, axis=0).T

    for j in range(2):
        total = jnp.dot(weights[j][...], turned[...], preferred_element_type=jnp.float32)
        sums[j][...] = total if begin else total + before[j][...]
    if end:
        hidden = (jax.nn.silu(sums[0][...]) * sums[1][...]).astype(jnp.bfloat16)
        hidden_ref[...] = hidden.T
    for copy in copies:
        copy.wait()


def gate_up(k, pieces, weights, later, ahead, totals):
    hidden, part = weights[0].shape
    begin, end = k == 0, k == HALVES - 1
    width = later[0].shape[1]
    rows = sum(p.shape[0] for p in pieces)
    total = jax.ShapeDtypeStruct((hidden, rows), jnp.float32)
    out_shape = [pltpu.VMEM((hidden, ahead[1]), jnp.bfloat16)] * len(later)
    out_specs = [VMEM] * len(later)
    scratch = []
    if end:
        out_shape.append(jax.ShapeDtypeStruct((rows, hidden), jnp.bfloat16))
        scratch += [pltpu.VMEM((hidden, rows), jnp.float32)] * 2
    else:
        out_shape += [total] * 2
    out_specs += [VMEM] * (len(out_shape) - len(later))
    scratch.append(pltpu.VMEM((part, rows), jnp.bfloat16))
    scratch.append(pltpu.SemaphoreType.DMA((len(later), hidden // FETCH_ROWS)))
    weights = [pltpu.with_memory_space_constraint(w, pltpu.VMEM) for w in weights]
    later = [pltpu.with_memory_space_constraint(w, pltpu.HBM) for w in later]
    out = pl.pallas_call(
        functools.partial(
            gate_up_kernel, len(pieces), len(later), spans(width)[k][0], ahead[0], begin, end
        ),
        in_specs=[VMEM] * (len(pieces) + 2) + [ANY] * len(later) + [VMEM] * len(totals),
        out_specs=out_specs,
        out_shape=out_shape,
        scratch_shapes=scratch,
        compiler_params=LIMIT if rows <= 256 else WIDE,
        cost_estimate=pl.CostEstimate(
            flops=4 * rows * hidden * part,
            bytes_accessed=4 * hidden * part + 8 * rows * hidden,
            transcendentals=0,
        ),
        name="gate_up",
    )(*pieces, *weights, *later, *totals)
    return out[: len(later)], out[len(later) :]


def down_kernel(ahead, segments, hidden_ref, *refs):
    weights, refs = refs[: len(segments)], refs[len(segments) :]
    later, held, refs = refs[:ahead], refs[ahead : 2 * ahead], refs[2 * ahead :]
    keep_ref, send_ref, sems = refs
    half, part = keep_ref.shape
    copies = fetches(later, AHEAD * BLOCK, held, sems)
    for copy in copies:
        copy.start()
    done = 0
    for w_ref, (first, size) in zip(weights, segments):
        block = size // 2

        @pl.loop(0, 2)
        def _(c, first=first, done=done, block=block, w_ref=w_ref):
            columns = pl.ds(pl.multiple_of(first + c * block, BLOCK), block)
            out = jnp.dot(hidden_ref[...], w_ref[:, columns], preferred_element_type=jnp.float32)
            out = out.astype(jnp.bfloat16)
            columns = pl.ds(pl.multiple_of(done + c * block, BLOCK), block)
            keep_ref[:, columns] = out[:half]
            send_ref[:, columns] = out[half:]

        done += size
    for copy in copies:
        copy.wait()


def down(hidden, weights, segments, later):
    rows, depth = hidden.shape
    part = sum(size for _, size in segments)
    ahead = len(later)
    out_shape = [pltpu.VMEM((depth, w.shape[1] - AHEAD * BLOCK), jnp.bfloat16) for w in later]
    out_shape += [jax.ShapeDtypeStruct((rows // 2, part), jnp.bfloat16)] * 2
    weights = [pltpu.with_memory_space_constraint(w, pltpu.VMEM) for w in weights]
    later = [pltpu.with_memory_space_constraint(w, pltpu.HBM) for w in later]
    out = pl.pallas_call(
        functools.partial(down_kernel, ahead, segments),
        in_specs=[VMEM] * (1 + len(weights)) + [ANY] * ahead,
        out_specs=[VMEM] * (ahead + 2),
        out_shape=out_shape,
        scratch_shapes=[pltpu.SemaphoreType.DMA((max(ahead, 1), depth // FETCH_ROWS))],
        compiler_params=LIMIT if rows <= 256 else WIDE,
        cost_estimate=pl.CostEstimate(
            flops=2 * rows * depth * part,
            bytes_accessed=2 * (depth * part + rows * depth + rows * part),
            transcendentals=0,
        ),
        name="down",
    )(hidden, *weights, *later)
    return out[:ahead], out[ahead:]


def mix_kernel(group, ids_ref, logits_ref, act_ref, arrived, near, last, *refs):
    out_ref, kept, middle_rows = refs[-1], refs[:HALVES], refs[HALVES:-1]
    plane = lax.axis_index("expert") // group
    first, second = choices(ids_ref[...], plane)
    lead = logits_ref[0:1, :] - logits_ref[1:2, :]
    weight = jnp.where(first, jax.nn.sigmoid(lead), 0.0)
    weight = (weight + jnp.where(second, jax.nn.sigmoid(-lead), 0.0)).T
    tokens = weight.shape[0]
    high = weight.astype(jnp.bfloat16).astype(jnp.float32)
    middle = (weight - high).astype(jnp.bfloat16).astype(jnp.float32)
    terms = jnp.concatenate([weight - high - middle, middle, high], axis=0).astype(jnp.bfloat16)
    for k, (at, part) in enumerate(spans(act_ref.shape[1], BACK)):
        columns = slice(at, at + part)
        own = kept[k][...].astype(jnp.float32) + arrived[:, columns].astype(jnp.float32)
        blocks = [own.astype(jnp.bfloat16), near[:, columns], middle_rows[k][...]]
        rows = jnp.concatenate(blocks + [last[:, columns]], axis=0)
        sums = jnp.dot(terms, rows, preferred_element_type=jnp.float32)
        total = act_ref[:, columns].astype(jnp.float32)
        for j in range(3):
            total = total + sums[j * tokens : (j + 1) * tokens]
        out_ref[:, columns] = total.astype(jnp.bfloat16)


def mix(group, ids, logits, activations, pieces):
    return pl.pallas_call(
        functools.partial(mix_kernel, group),
        out_shape=jax.ShapeDtypeStruct(activations.shape, jnp.bfloat16),
        compiler_params=LIMIT,
        name="mix",
    )(ids, logits, activations, *pieces)


def fold_kernel(mine_ref, arrived_ref, out_ref):
    total = mine_ref[...].astype(jnp.float32) + arrived_ref[...].astype(jnp.float32)
    out_ref[...] = total.astype(jnp.bfloat16)


def fold(mine, arrived):
    return pl.pallas_call(
        fold_kernel,
        in_specs=[VMEM, VMEM],
        out_specs=VMEM,
        out_shape=jax.ShapeDtypeStruct(mine.shape, mine.dtype),
        compiler_params=LIMIT,
        cost_estimate=pl.CostEstimate(flops=0, bytes_accessed=16 * MIB, transcendentals=0),
        name="fold",
    )(mine, arrived)


def added(mine, arrived):
    total = mine.astype(jnp.float32) + arrived.astype(jnp.float32)
    return total.astype(jnp.bfloat16)


def on_device(activations, expert_ids, route_logits, norm_gain, w_gate, w_up, w_down):
    devices = lax.axis_size("expert")
    group = devices // EXPERTS
    far = group // 2
    width = activations.shape[1]
    part = width // HALVES

    def shift(x, s):
        return lax.ppermute(
            x, "expert", [(i, (i + s * group) % devices) for i in range(devices)]
        )

    def swap(x, bit):
        return lax.ppermute(x, "expert", [(i, i ^ bit) for i in range(devices)])

    def after(x, *others):
        return lax.optimization_barrier((x, *others))[0]

    others = EXPERTS - 1
    ids = expert_ids.T
    own, *sends = pack(group, ids, activations, norm_gain)
    far_own = swap(own, far)
    now = [fetch(w, 0, spans(width)[0][1], own) for w in (w_gate, w_up)]
    blocks = []
    for k in range(HALVES):
        x = sends[k * others : (k + 1) * others]
        if k:
            x = relay(after(x, *now, far_own), blocks[-1])
        arrivals = [shift(x[s - 1], s) for s in ORDER]
        blocks.append(jnp.concatenate(arrivals, axis=0))
    totals = []
    for k in range(HALVES):
        at, size = spans(width)[k]
        columns = slice(at, at + size)
        far_block = swap(blocks[k], far)
        if totals:
            far_block, totals = lax.optimization_barrier((far_block, totals))
        pieces = [own[:, columns], blocks[k], far_own[:, columns], far_block]
        bit = far // 2
        while bit:
            if k and len(pieces) == EXPERTS:
                early = swap(jnp.concatenate(pieces[:-1], axis=0), bit)
                pieces += [early, swap(far_block, bit)]
            else:
                pieces.append(swap(jnp.concatenate(pieces, axis=0), bit))
            bit //= 2
        pieces[0], pieces[2] = own, far_own
        if k < HALVES - 1:
            pieces[1] = after(pieces[1], blocks[k + 1])
        later, ahead = [w_gate, w_up], (size, width - size)
        if k == HALVES - 1:
            later, ahead = [w_down], (0, AHEAD * BLOCK)
        now, totals = gate_up(k, pieces, now, later, ahead, totals)
    hidden = totals[0]
    held = []
    early = AHEAD * BLOCK
    for k, (at, size) in enumerate(spans(width, BACK)):
        if k == 0:
            rest, (keep, send) = down(hidden, now, [(at, size)], [w_down])
        else:
            segments = [(at, early - at), (0, width - early)]
            _, (keep, send) = down(hidden, [*now, *rest], segments, [])
        bit = 1
        while bit < far:
            total = added(keep, swap(send, bit))
            keep, send = total[: total.shape[0] // 2], total[total.shape[0] // 2 :]
            bit *= 2
        held.append([total[j * CAP : (j + 1) * CAP] for j in range(2 * EXPERTS)])
    place = {s: 1 + j for j, s in enumerate(ORDER)}
    crossed = [swap(h[EXPERTS + place[2]], far) for h in held]
    middle = [shift(added(h[place[2]], x), -2) for h, x in zip(held, crossed)]
    mine = [jnp.concatenate([h[j] for h in held], axis=1) for j in range(2 * EXPERTS)]
    back = {}
    back[3] = swap(after(mine[EXPERTS + place[3]], crossed[0]), far)
    back[1] = swap(after(mine[EXPERTS + place[1]], back[3]), far)
    near_rows = fold(mine[place[1]], back[1])
    last_rows = fold(mine[place[3]], back[3])
    back[0] = swap(after(mine[EXPERTS], last_rows, *middle), far)
    near = shift(near_rows, -1)
    last = shift(last_rows, -3)
    arrived = back[0]
    pieces = [arrived, near, last, *[h[0] for h in held], *middle]
    return mix(group, ids, route_logits.T, activations, pieces)


def solution(mesh):
    in_specs = (
        P(("parts", "expert"), None),
        P(("parts", "expert"), None),
        P(("parts", "expert"), None),
        P(),
        P("expert", None),
        P("expert", None),
        P("expert", None),
    )
    out_specs = P(("parts", "expert"), None)
    return jax.shard_map(
        on_device, mesh=mesh, in_specs=in_specs, out_specs=out_specs, check_vma=False
    )
```

```python
import functools

import jax
import jax.numpy as jnp
from jax import lax
from jax.experimental import pallas as pl
from jax.experimental.pallas import tpu as pltpu
from jax.sharding import PartitionSpec as P

EXPERTS = 4
CAP = 16
HALVES = 2
ORDER = (1, 2, 3)
FORTH = (7, 5)
BACK = (1, 1)
BLOCK = 512
AHEAD = 8
FETCH_ROWS = 144
MIB = 1 << 20
LIMIT = pltpu.CompilerParams(vmem_limit_bytes=10 * MIB)
WIDE = pltpu.CompilerParams(vmem_limit_bytes=32 * MIB)
VMEM = pl.BlockSpec(memory_space=pltpu.VMEM)
ANY = pl.BlockSpec(memory_space=pl.ANY)


def spans(width, shares=FORTH):
    unit = width // sum(shares)
    return [(sum(shares[:k]) * unit, n * unit) for k, n in enumerate(shares)]


def choices(ids, plane):
    tokens = ids.shape[1]
    line = lax.broadcasted_iota(jnp.int32, (EXPERTS * CAP, tokens), 0)
    expert = lax.rem(line // CAP + plane, EXPERTS)
    slot = (line % CAP).astype(jnp.float32)
    first = ids[0:1, :] == expert
    second = ids[1:2, :] == expert
    named = (first | second).astype(jnp.float32)
    square = (tokens, tokens)
    earlier = lax.broadcasted_iota(jnp.int32, square, 0) < lax.broadcasted_iota(
        jnp.int32, square, 1
    )
    rank = jnp.dot(named, earlier.astype(jnp.float32), preferred_element_type=jnp.float32)
    here = rank == slot
    return first & here, second & here


def pack_kernel(group, ids_ref, act_ref, gain_ref, *out_refs):
    plane = lax.axis_index("expert") // group
    values = act_ref[...].astype(jnp.float32)
    mean_sq = jnp.mean(values * values, axis=-1, keepdims=True)
    normed = (values * lax.rsqrt(mean_sq + 1e-06) * gain_ref[...]).astype(jnp.bfloat16)
    first, second = choices(ids_ref[...], plane)
    pick = (first | second).astype(jnp.float32).astype(jnp.bfloat16)
    rows = jnp.dot(pick, normed, preferred_element_type=jnp.float32).astype(jnp.bfloat16)
    out_refs[0][...] = rows[:CAP]
    for j, out_ref in enumerate(out_refs[1:]):
        k, s = j // (EXPERTS - 1), j % (EXPERTS - 1) + 1
        at, part = spans(rows.shape[1])[k]
        out_ref[...] = rows[s * CAP : (s + 1) * CAP, at : at + part]


def pack(group, ids, activations, gain):
    width = activations.shape[1]
    widths = [width] + [part for _, part in spans(width) for _ in range(EXPERTS - 1)]
    operands = [ids, activations, gain.reshape(1, width)]
    return pl.pallas_call(
        functools.partial(pack_kernel, group),
        grid=(1,),
        in_specs=[pl.BlockSpec(x.shape, lambda i: (0, 0)) for x in operands],
        out_specs=[pl.BlockSpec((CAP, n), lambda i: (0, 0)) for n in widths],
        out_shape=[jax.ShapeDtypeStruct((CAP, n), jnp.bfloat16) for n in widths],
        compiler_params=LIMIT,
        name="norm_and_pack",
    )(*[pltpu.with_memory_space_constraint(x, pltpu.HBM) for x in operands])


def fetches(weights, at, held, sems):
    copies = []
    for j, w in enumerate(weights):
        part = held[j].shape[1]
        for b in range(sems.shape[1]):
            rows = pl.ds(b * FETCH_ROWS, FETCH_ROWS)
            copies.append(
                pltpu.make_async_copy(w.at[rows, at : at + part], held[j].at[rows], sems.at[j, b])
            )
    return copies


def fetch_kernel(at, w_ref, after_ref, held_ref, sems):
    copies = fetches([w_ref], at, [held_ref], sems)
    for copy in copies:
        copy.start()
    for copy in copies:
        copy.wait()


def fetch(w, at, part, after):
    rows = w.shape[0]
    return pl.pallas_call(
        functools.partial(fetch_kernel, at),
        in_specs=[ANY, ANY],
        out_specs=VMEM,
        out_shape=pltpu.VMEM((rows, part), jnp.bfloat16),
        scratch_shapes=[pltpu.SemaphoreType.DMA((1, rows // FETCH_ROWS))],
        compiler_params=LIMIT,
        cost_estimate=pl.CostEstimate(flops=0, bytes_accessed=4 * rows * part, transcendentals=0),
        name="fetch",
    )(pltpu.with_memory_space_constraint(w, pltpu.HBM), after)


def relay_kernel(count, *refs):
    for x_ref, out_ref in zip(refs[:count], refs[count + 1 :]):
        out_ref[...] = x_ref[...]


def relay(arrays, after):
    count = len(arrays)
    return pl.pallas_call(
        functools.partial(relay_kernel, count),
        in_specs=[VMEM] * count + [ANY],
        out_specs=[VMEM] * count,
        out_shape=[jax.ShapeDtypeStruct(x.shape, x.dtype) for x in arrays],
        compiler_params=LIMIT,
        cost_estimate=pl.CostEstimate(flops=0, bytes_accessed=16 * MIB, transcendentals=0),
        name="relay",
    )(*arrays, after)


def gate_up_kernel(count, ahead, at, ahead_at, begin, end, *refs):
    pieces, refs = refs[:count], refs[count:]
    weights, later, refs = refs[:2], refs[2 : 2 + ahead], refs[2 + ahead :]
    if not begin:
        before, refs = refs[:2], refs[2:]
    held, refs = refs[:ahead], refs[ahead:]
    turned, sems, refs = *refs[-2:], refs[:-2]
    if end:
        hidden_ref, refs = refs[0], refs[1:]
    sums = refs
    part, rows = turned.shape
    copies = fetches(later, ahead_at, held, sems)
    for copy in copies:
        copy.start()

    @pl.loop(0, part // BLOCK)
    def _(c):
        parts = []
        for p in pieces:
            first = c * BLOCK + (at if p.shape[1] > part else 0)
            parts.append(p[:, pl.ds(pl.multiple_of(first, BLOCK), BLOCK)])
        turned[pl.ds(pl.multiple_of(c * BLOCK, BLOCK), BLOCK), :] = jnp.concatenate(parts, axis=0).T

    for j in range(2):
        total = jnp.dot(weights[j][...], turned[...], preferred_element_type=jnp.float32)
        sums[j][...] = total if begin else total + before[j][...]
    if end:
        hidden = (jax.nn.silu(sums[0][...]) * sums[1][...]).astype(jnp.bfloat16)
        hidden_ref[...] = hidden.T
    for copy in copies:
        copy.wait()


def gate_up(k, pieces, weights, later, ahead, totals):
    hidden, part = weights[0].shape
    begin, end = k == 0, k == HALVES - 1
    width = later[0].shape[1]
    rows = sum(p.shape[0] for p in pieces)
    total = jax.ShapeDtypeStruct((hidden, rows), jnp.float32)
    out_shape = [pltpu.VMEM((hidden, ahead[1]), jnp.bfloat16)] * len(later)
    out_specs = [VMEM] * len(later)
    scratch = []
    if end:
        out_shape.append(jax.ShapeDtypeStruct((rows, hidden), jnp.bfloat16))
        scratch += [pltpu.VMEM((hidden, rows), jnp.float32)] * 2
    else:
        out_shape += [total] * 2
    out_specs += [VMEM] * (len(out_shape) - len(later))
    scratch.append(pltpu.VMEM((part, rows), jnp.bfloat16))
    scratch.append(pltpu.SemaphoreType.DMA((len(later), hidden // FETCH_ROWS)))
    weights = [pltpu.with_memory_space_constraint(w, pltpu.VMEM) for w in weights]
    later = [pltpu.with_memory_space_constraint(w, pltpu.HBM) for w in later]
    out = pl.pallas_call(
        functools.partial(
            gate_up_kernel, len(pieces), len(later), spans(width)[k][0], ahead[0], begin, end
        ),
        in_specs=[VMEM] * (len(pieces) + 2) + [ANY] * len(later) + [VMEM] * len(totals),
        out_specs=out_specs,
        out_shape=out_shape,
        scratch_shapes=scratch,
        compiler_params=LIMIT if rows <= 256 else WIDE,
        cost_estimate=pl.CostEstimate(
            flops=4 * rows * hidden * part,
            bytes_accessed=4 * hidden * part + 8 * rows * hidden,
            transcendentals=0,
        ),
        name="gate_up",
    )(*pieces, *weights, *later, *totals)
    return out[: len(later)], out[len(later) :]


def down_kernel(ahead, segments, hidden_ref, *refs):
    weights, refs = refs[: len(segments)], refs[len(segments) :]
    later, held, refs = refs[:ahead], refs[ahead : 2 * ahead], refs[2 * ahead :]
    keep_ref, send_ref, sems = refs
    half, part = keep_ref.shape
    copies = fetches(later, AHEAD * BLOCK, held, sems)
    for copy in copies:
        copy.start()
    done = 0
    for w_ref, (first, size) in zip(weights, segments):
        block = size // 2

        @pl.loop(0, 2)
        def _(c, first=first, done=done, block=block, w_ref=w_ref):
            columns = pl.ds(pl.multiple_of(first + c * block, BLOCK), block)
            out = jnp.dot(hidden_ref[...], w_ref[:, columns], preferred_element_type=jnp.float32)
            out = out.astype(jnp.bfloat16)
            columns = pl.ds(pl.multiple_of(done + c * block, BLOCK), block)
            keep_ref[:, columns] = out[:half]
            send_ref[:, columns] = out[half:]

        done += size
    for copy in copies:
        copy.wait()


def down(hidden, weights, segments, later):
    rows, depth = hidden.shape
    part = sum(size for _, size in segments)
    ahead = len(later)
    out_shape = [pltpu.VMEM((depth, w.shape[1] - AHEAD * BLOCK), jnp.bfloat16) for w in later]
    out_shape += [jax.ShapeDtypeStruct((rows // 2, part), jnp.bfloat16)] * 2
    weights = [pltpu.with_memory_space_constraint(w, pltpu.VMEM) for w in weights]
    later = [pltpu.with_memory_space_constraint(w, pltpu.HBM) for w in later]
    out = pl.pallas_call(
        functools.partial(down_kernel, ahead, segments),
        in_specs=[VMEM] * (1 + len(weights)) + [ANY] * ahead,
        out_specs=[VMEM] * (ahead + 2),
        out_shape=out_shape,
        scratch_shapes=[pltpu.SemaphoreType.DMA((max(ahead, 1), depth // FETCH_ROWS))],
        compiler_params=LIMIT if rows <= 256 else WIDE,
        cost_estimate=pl.CostEstimate(
            flops=2 * rows * depth * part,
            bytes_accessed=2 * (depth * part + rows * depth + rows * part),
            transcendentals=0,
        ),
        name="down",
    )(hidden, *weights, *later)
    return out[:ahead], out[ahead:]


def mix_kernel(group, ids_ref, logits_ref, act_ref, arrived, near, last, two, *refs):
    kept, out_ref = refs[:-1], refs[-1]
    plane = lax.axis_index("expert") // group
    first, second = choices(ids_ref[...], plane)
    lead = logits_ref[0:1, :] - logits_ref[1:2, :]
    weight = jnp.where(first, jax.nn.sigmoid(lead), 0.0)
    weight = (weight + jnp.where(second, jax.nn.sigmoid(-lead), 0.0)).T
    tokens = weight.shape[0]
    high = weight.astype(jnp.bfloat16).astype(jnp.float32)
    middle = (weight - high).astype(jnp.bfloat16).astype(jnp.float32)
    terms = jnp.concatenate([weight - high - middle, middle, high], axis=0).astype(jnp.bfloat16)
    for k, (at, part) in enumerate(spans(act_ref.shape[1], BACK)):
        columns = slice(at, at + part)
        own = kept[k][...].astype(jnp.float32) + arrived[:, columns].astype(jnp.float32)
        blocks = [own.astype(jnp.bfloat16), near[:, columns], two[:, columns]]
        rows = jnp.concatenate(blocks + [last[:, columns]], axis=0)
        sums = jnp.dot(terms, rows, preferred_element_type=jnp.float32)
        total = act_ref[:, columns].astype(jnp.float32)
        for j in range(3):
            total = total + sums[j * tokens : (j + 1) * tokens]
        out_ref[:, columns] = total.astype(jnp.bfloat16)


def mix(group, ids, logits, activations, pieces):
    return pl.pallas_call(
        functools.partial(mix_kernel, group),
        out_shape=jax.ShapeDtypeStruct(activations.shape, jnp.bfloat16),
        compiler_params=LIMIT,
        name="mix",
    )(ids, logits, activations, *pieces)


def fold_kernel(mine_ref, arrived_ref, out_ref):
    total = mine_ref[...].astype(jnp.float32) + arrived_ref[...].astype(jnp.float32)
    out_ref[...] = total.astype(jnp.bfloat16)


def fold(mine, arrived):
    return pl.pallas_call(
        fold_kernel,
        in_specs=[VMEM, VMEM],
        out_specs=VMEM,
        out_shape=jax.ShapeDtypeStruct(mine.shape, mine.dtype),
        compiler_params=LIMIT,
        cost_estimate=pl.CostEstimate(flops=0, bytes_accessed=16 * MIB, transcendentals=0),
        name="fold",
    )(mine, arrived)


def added(mine, arrived):
    total = mine.astype(jnp.float32) + arrived.astype(jnp.float32)
    return total.astype(jnp.bfloat16)


def on_device(activations, expert_ids, route_logits, norm_gain, w_gate, w_up, w_down):
    devices = lax.axis_size("expert")
    group = devices // EXPERTS
    far = group // 2
    width = activations.shape[1]
    part = width // HALVES

    def shift(x, s):
        return lax.ppermute(
            x, "expert", [(i, (i + s * group) % devices) for i in range(devices)]
        )

    def swap(x, bit):
        return lax.ppermute(x, "expert", [(i, i ^ bit) for i in range(devices)])

    def after(x, *others):
        return lax.optimization_barrier((x, *others))[0]

    others = EXPERTS - 1
    ids = expert_ids.T
    own, *sends = pack(group, ids, activations, norm_gain)
    far_own = swap(own, far)
    now = [fetch(w, 0, spans(width)[0][1], own) for w in (w_gate, w_up)]
    blocks = []
    for k in range(HALVES):
        x = sends[k * others : (k + 1) * others]
        if k:
            x = relay(after(x, *now, far_own), blocks[-1])
        arrivals = [shift(x[s - 1], s) for s in ORDER]
        blocks.append(jnp.concatenate(arrivals, axis=0))
    totals = []
    for k in range(HALVES):
        at, size = spans(width)[k]
        columns = slice(at, at + size)
        far_block = swap(blocks[k], far)
        if totals:
            far_block, totals = lax.optimization_barrier((far_block, totals))
        pieces = [own[:, columns], blocks[k], far_own[:, columns], far_block]
        bit = far // 2
        while bit:
            if k and len(pieces) == EXPERTS:
                early = swap(jnp.concatenate(pieces[:-1], axis=0), bit)
                pieces += [early, swap(far_block, bit)]
            else:
                pieces.append(swap(jnp.concatenate(pieces, axis=0), bit))
            bit //= 2
        pieces[0], pieces[2] = own, far_own
        if k < HALVES - 1:
            pieces[1] = after(pieces[1], blocks[k + 1])
        later, ahead = [w_gate, w_up], (size, width - size)
        if k == HALVES - 1:
            later, ahead = [w_down], (0, AHEAD * BLOCK)
        now, totals = gate_up(k, pieces, now, later, ahead, totals)
    hidden = totals[0]
    held = []
    early = AHEAD * BLOCK
    for k, (at, size) in enumerate(spans(width, BACK)):
        if k == 0:
            rest, (keep, send) = down(hidden, now, [(at, size)], [w_down])
        else:
            segments = [(at, early - at), (0, width - early)]
            _, (keep, send) = down(hidden, [*now, *rest], segments, [])
        bit = 1
        while bit < far:
            total = added(keep, swap(send, bit))
            keep, send = total[: total.shape[0] // 2], total[total.shape[0] // 2 :]
            bit *= 2
        held.append([total[j * CAP : (j + 1) * CAP] for j in range(2 * EXPERTS)])
    place = {s: 1 + j for j, s in enumerate(ORDER)}
    crossed = [swap(h[EXPERTS + place[2]], far) for h in held]
    two = [added(h[place[2]], x) for h, x in zip(held, crossed)]
    middle = shift(jnp.concatenate(two, axis=1), -2)
    mine = [jnp.concatenate([h[j] for h in held], axis=1) for j in range(2 * EXPERTS)]
    back = {}
    back[3] = swap(after(mine[EXPERTS + place[3]], *crossed), far)
    back[1] = swap(after(mine[EXPERTS + place[1]], back[3]), far)
    near_rows = fold(mine[place[1]], back[1])
    last_rows = fold(mine[place[3]], back[3])
    back[0] = swap(after(mine[EXPERTS], near_rows, middle), far)
    near = shift(near_rows, -1)
    last = shift(last_rows, -3)
    arrived = back[0]
    pieces = [arrived, near, last, middle, *[h[0] for h in held]]
    return mix(group, ids, route_logits.T, activations, pieces)


def solution(mesh):
    in_specs = (
        P(("parts", "expert"), None),
        P(("parts", "expert"), None),
        P(("parts", "expert"), None),
        P(),
        P("expert", None),
        P("expert", None),
        P("expert", None),
    )
    out_specs = P(("parts", "expert"), None)
    return jax.shard_map(
        on_device, mesh=mesh, in_specs=in_specs, out_specs=out_specs, check_vma=False
    )
```

```python
import functools

import jax
import jax.numpy as jnp
from jax import lax
from jax.experimental import pallas as pl
from jax.experimental.pallas import tpu as pltpu
from jax.sharding import PartitionSpec as P

EXPERTS = 4
CAP = 16
HALVES = 2
ORDER = (1, 3, 2)
FORTH = (7, 5)
BACK = (1, 1)
BLOCK = 512
AHEAD = 8
FETCH_ROWS = 144
MIB = 1 << 20
LIMIT = pltpu.CompilerParams(vmem_limit_bytes=10 * MIB)
WIDE = pltpu.CompilerParams(vmem_limit_bytes=32 * MIB)
VMEM = pl.BlockSpec(memory_space=pltpu.VMEM)
ANY = pl.BlockSpec(memory_space=pl.ANY)


def spans(width, shares=FORTH):
    unit = width // sum(shares)
    return [(sum(shares[:k]) * unit, n * unit) for k, n in enumerate(shares)]


def choices(ids, plane):
    tokens = ids.shape[1]
    line = lax.broadcasted_iota(jnp.int32, (EXPERTS * CAP, tokens), 0)
    expert = lax.rem(line // CAP + plane, EXPERTS)
    slot = (line % CAP).astype(jnp.float32)
    first = ids[0:1, :] == expert
    second = ids[1:2, :] == expert
    named = (first | second).astype(jnp.float32)
    square = (tokens, tokens)
    earlier = lax.broadcasted_iota(jnp.int32, square, 0) < lax.broadcasted_iota(
        jnp.int32, square, 1
    )
    rank = jnp.dot(named, earlier.astype(jnp.float32), preferred_element_type=jnp.float32)
    here = rank == slot
    return first & here, second & here


def pack_kernel(group, ids_ref, act_ref, gain_ref, *out_refs):
    plane = lax.axis_index("expert") // group
    values = act_ref[...].astype(jnp.float32)
    mean_sq = jnp.mean(values * values, axis=-1, keepdims=True)
    normed = (values * lax.rsqrt(mean_sq + 1e-06) * gain_ref[...]).astype(jnp.bfloat16)
    first, second = choices(ids_ref[...], plane)
    pick = (first | second).astype(jnp.float32).astype(jnp.bfloat16)
    rows = jnp.dot(pick, normed, preferred_element_type=jnp.float32).astype(jnp.bfloat16)
    out_refs[0][...] = rows[:CAP]
    for j, out_ref in enumerate(out_refs[1:]):
        k, s = j // (EXPERTS - 1), j % (EXPERTS - 1) + 1
        at, part = spans(rows.shape[1])[k]
        out_ref[...] = rows[s * CAP : (s + 1) * CAP, at : at + part]


def pack(group, ids, activations, gain):
    width = activations.shape[1]
    widths = [width] + [part for _, part in spans(width) for _ in range(EXPERTS - 1)]
    operands = [ids, activations, gain.reshape(1, width)]
    return pl.pallas_call(
        functools.partial(pack_kernel, group),
        grid=(1,),
        in_specs=[pl.BlockSpec(x.shape, lambda i: (0, 0)) for x in operands],
        out_specs=[pl.BlockSpec((CAP, n), lambda i: (0, 0)) for n in widths],
        out_shape=[jax.ShapeDtypeStruct((CAP, n), jnp.bfloat16) for n in widths],
        compiler_params=LIMIT,
        name="norm_and_pack",
    )(*[pltpu.with_memory_space_constraint(x, pltpu.HBM) for x in operands])


def fetches(weights, at, held, sems):
    copies = []
    for j, w in enumerate(weights):
        part = held[j].shape[1]
        for b in range(sems.shape[1]):
            rows = pl.ds(b * FETCH_ROWS, FETCH_ROWS)
            copies.append(
                pltpu.make_async_copy(w.at[rows, at : at + part], held[j].at[rows], sems.at[j, b])
            )
    return copies


def fetch_kernel(at, w_ref, after_ref, held_ref, sems):
    copies = fetches([w_ref], at, [held_ref], sems)
    for copy in copies:
        copy.start()
    for copy in copies:
        copy.wait()


def fetch(w, at, part, after):
    rows = w.shape[0]
    return pl.pallas_call(
        functools.partial(fetch_kernel, at),
        in_specs=[ANY, ANY],
        out_specs=VMEM,
        out_shape=pltpu.VMEM((rows, part), jnp.bfloat16),
        scratch_shapes=[pltpu.SemaphoreType.DMA((1, rows // FETCH_ROWS))],
        compiler_params=LIMIT,
        cost_estimate=pl.CostEstimate(flops=0, bytes_accessed=4 * rows * part, transcendentals=0),
        name="fetch",
    )(pltpu.with_memory_space_constraint(w, pltpu.HBM), after)


def relay_kernel(count, *refs):
    for x_ref, out_ref in zip(refs[:count], refs[count + 1 :]):
        out_ref[...] = x_ref[...]


def relay(arrays, after):
    count = len(arrays)
    return pl.pallas_call(
        functools.partial(relay_kernel, count),
        in_specs=[VMEM] * count + [ANY],
        out_specs=[VMEM] * count,
        out_shape=[jax.ShapeDtypeStruct(x.shape, x.dtype) for x in arrays],
        compiler_params=LIMIT,
        cost_estimate=pl.CostEstimate(flops=0, bytes_accessed=16 * MIB, transcendentals=0),
        name="relay",
    )(*arrays, after)


def gate_up_kernel(count, ahead, at, ahead_at, begin, end, *refs):
    pieces, refs = refs[:count], refs[count:]
    weights, later, refs = refs[:2], refs[2 : 2 + ahead], refs[2 + ahead :]
    if not begin:
        before, refs = refs[:2], refs[2:]
    held, refs = refs[:ahead], refs[ahead:]
    turned, sems, refs = *refs[-2:], refs[:-2]
    if end:
        hidden_ref, refs = refs[0], refs[1:]
    sums = refs
    part, rows = turned.shape
    copies = fetches(later, ahead_at, held, sems)
    for copy in copies:
        copy.start()

    @pl.loop(0, part // BLOCK)
    def _(c):
        parts = []
        for p in pieces:
            first = c * BLOCK + (at if p.shape[1] > part else 0)
            parts.append(p[:, pl.ds(pl.multiple_of(first, BLOCK), BLOCK)])
        turned[pl.ds(pl.multiple_of(c * BLOCK, BLOCK), BLOCK), :] = jnp.concatenate(parts, axis=0).T

    for j in range(2):
        total = jnp.dot(weights[j][...], turned[...], preferred_element_type=jnp.float32)
        sums[j][...] = total if begin else total + before[j][...]
    if end:
        hidden = (jax.nn.silu(sums[0][...]) * sums[1][...]).astype(jnp.bfloat16)
        hidden_ref[...] = hidden.T
    for copy in copies:
        copy.wait()


def gate_up(k, pieces, weights, later, ahead, totals):
    hidden, part = weights[0].shape
    begin, end = k == 0, k == HALVES - 1
    width = later[0].shape[1]
    rows = sum(p.shape[0] for p in pieces)
    total = jax.ShapeDtypeStruct((hidden, rows), jnp.float32)
    out_shape = [pltpu.VMEM((hidden, ahead[1]), jnp.bfloat16)] * len(later)
    out_specs = [VMEM] * len(later)
    scratch = []
    if end:
        out_shape.append(jax.ShapeDtypeStruct((rows, hidden), jnp.bfloat16))
        scratch += [pltpu.VMEM((hidden, rows), jnp.float32)] * 2
    else:
        out_shape += [total] * 2
    out_specs += [VMEM] * (len(out_shape) - len(later))
    scratch.append(pltpu.VMEM((part, rows), jnp.bfloat16))
    scratch.append(pltpu.SemaphoreType.DMA((len(later), hidden // FETCH_ROWS)))
    weights = [pltpu.with_memory_space_constraint(w, pltpu.VMEM) for w in weights]
    later = [pltpu.with_memory_space_constraint(w, pltpu.HBM) for w in later]
    out = pl.pallas_call(
        functools.partial(
            gate_up_kernel, len(pieces), len(later), spans(width)[k][0], ahead[0], begin, end
        ),
        in_specs=[VMEM] * (len(pieces) + 2) + [ANY] * len(later) + [VMEM] * len(totals),
        out_specs=out_specs,
        out_shape=out_shape,
        scratch_shapes=scratch,
        compiler_params=LIMIT if rows <= 256 else WIDE,
        cost_estimate=pl.CostEstimate(
            flops=4 * rows * hidden * part,
            bytes_accessed=4 * hidden * part + 8 * rows * hidden,
            transcendentals=0,
        ),
        name="gate_up",
    )(*pieces, *weights, *later, *totals)
    return out[: len(later)], out[len(later) :]


def down_kernel(ahead, segments, hidden_ref, *refs):
    weights, refs = refs[: len(segments)], refs[len(segments) :]
    later, held, refs = refs[:ahead], refs[ahead : 2 * ahead], refs[2 * ahead :]
    keep_ref, send_ref, sems = refs
    half, part = keep_ref.shape
    copies = fetches(later, AHEAD * BLOCK, held, sems)
    for copy in copies:
        copy.start()
    done = 0
    for w_ref, (first, size) in zip(weights, segments):
        block = size // 2

        @pl.loop(0, 2)
        def _(c, first=first, done=done, block=block, w_ref=w_ref):
            columns = pl.ds(pl.multiple_of(first + c * block, BLOCK), block)
            out = jnp.dot(hidden_ref[...], w_ref[:, columns], preferred_element_type=jnp.float32)
            out = out.astype(jnp.bfloat16)
            columns = pl.ds(pl.multiple_of(done + c * block, BLOCK), block)
            keep_ref[:, columns] = out[:half]
            send_ref[:, columns] = out[half:]

        done += size
    for copy in copies:
        copy.wait()


def down(hidden, weights, segments, later):
    rows, depth = hidden.shape
    part = sum(size for _, size in segments)
    ahead = len(later)
    out_shape = [pltpu.VMEM((depth, w.shape[1] - AHEAD * BLOCK), jnp.bfloat16) for w in later]
    out_shape += [jax.ShapeDtypeStruct((rows // 2, part), jnp.bfloat16)] * 2
    weights = [pltpu.with_memory_space_constraint(w, pltpu.VMEM) for w in weights]
    later = [pltpu.with_memory_space_constraint(w, pltpu.HBM) for w in later]
    out = pl.pallas_call(
        functools.partial(down_kernel, ahead, segments),
        in_specs=[VMEM] * (1 + len(weights)) + [ANY] * ahead,
        out_specs=[VMEM] * (ahead + 2),
        out_shape=out_shape,
        scratch_shapes=[pltpu.SemaphoreType.DMA((max(ahead, 1), depth // FETCH_ROWS))],
        compiler_params=LIMIT if rows <= 256 else WIDE,
        cost_estimate=pl.CostEstimate(
            flops=2 * rows * depth * part,
            bytes_accessed=2 * (depth * part + rows * depth + rows * part),
            transcendentals=0,
        ),
        name="down",
    )(hidden, *weights, *later)
    return out[:ahead], out[ahead:]


def shares_kernel(group, ids_ref, logits_ref, after_ref, out_ref):
    plane = lax.axis_index("expert") // group
    first, second = choices(ids_ref[...], plane)
    lead = logits_ref[0:1, :] - logits_ref[1:2, :]
    weight = jnp.where(first, jax.nn.sigmoid(lead), 0.0)
    weight = (weight + jnp.where(second, jax.nn.sigmoid(-lead), 0.0)).T
    high = weight.astype(jnp.bfloat16).astype(jnp.float32)
    middle = (weight - high).astype(jnp.bfloat16).astype(jnp.float32)
    terms = jnp.concatenate([weight - high - middle, middle, high], axis=0)
    out_ref[...] = terms


def shares(group, ids, logits, after):
    shape = (3 * ids.shape[1], EXPERTS * CAP)
    return pl.pallas_call(
        functools.partial(shares_kernel, group),
        in_specs=[VMEM, VMEM, ANY],
        out_specs=VMEM,
        out_shape=jax.ShapeDtypeStruct(shape, jnp.float32),
        compiler_params=LIMIT,
        name="shares",
    )(ids, logits, after)


def mix_kernel(terms_ref, act_ref, arrived, near, last, *refs):
    out_ref, kept, middle_rows = refs[-1], refs[:HALVES], refs[HALVES:-1]
    tokens = act_ref.shape[0]
    terms = terms_ref[...].astype(jnp.bfloat16)
    for k, (at, part) in enumerate(spans(act_ref.shape[1], BACK)):
        columns = slice(at, at + part)
        own = kept[k][...].astype(jnp.float32) + arrived[:, columns].astype(jnp.float32)
        blocks = [own.astype(jnp.bfloat16), near[:, columns], middle_rows[k][...]]
        rows = jnp.concatenate(blocks + [last[:, columns]], axis=0)
        sums = jnp.dot(terms, rows, preferred_element_type=jnp.float32)
        total = act_ref[:, columns].astype(jnp.float32)
        for j in range(3):
            total = total + sums[j * tokens : (j + 1) * tokens]
        out_ref[:, columns] = total.astype(jnp.bfloat16)


def mix(terms, activations, pieces):
    return pl.pallas_call(
        mix_kernel,
        out_shape=jax.ShapeDtypeStruct(activations.shape, jnp.bfloat16),
        compiler_params=LIMIT,
        name="mix",
    )(terms, activations, *pieces)


def added(mine, arrived):
    total = mine.astype(jnp.float32) + arrived.astype(jnp.float32)
    return total.astype(jnp.bfloat16)


def on_device(activations, expert_ids, route_logits, norm_gain, w_gate, w_up, w_down):
    devices = lax.axis_size("expert")
    group = devices // EXPERTS
    far = group // 2
    width = activations.shape[1]
    part = width // HALVES

    def shift(x, s):
        return lax.ppermute(
            x, "expert", [(i, (i + s * group) % devices) for i in range(devices)]
        )

    def swap(x, bit):
        return lax.ppermute(x, "expert", [(i, i ^ bit) for i in range(devices)])

    def after(x, *others):
        return lax.optimization_barrier((x, *others))[0]

    others = EXPERTS - 1
    ids = expert_ids.T
    own, *sends = pack(group, ids, activations, norm_gain)
    far_own = swap(own, far)
    now = [fetch(w, 0, spans(width)[0][1], own) for w in (w_gate, w_up)]
    blocks = []
    for k in range(HALVES):
        x = sends[k * others : (k + 1) * others]
        if k:
            x = relay(after(x, *now, far_own), blocks[-1])
        arrivals = [shift(x[s - 1], s) for s in ORDER]
        blocks.append(jnp.concatenate(arrivals, axis=0))
    totals = []
    for k in range(HALVES):
        at, size = spans(width)[k]
        columns = slice(at, at + size)
        far_block = swap(blocks[k], far)
        if totals:
            far_block, totals = lax.optimization_barrier((far_block, totals))
        pieces = [own[:, columns], blocks[k], far_own[:, columns], far_block]
        bit = far // 2
        while bit:
            if k and len(pieces) == EXPERTS:
                early = swap(jnp.concatenate(pieces[:-1], axis=0), bit)
                pieces += [early, swap(far_block, bit)]
            else:
                pieces.append(swap(jnp.concatenate(pieces, axis=0), bit))
            bit //= 2
        pieces[0], pieces[2] = own, far_own
        if k < HALVES - 1:
            pieces[1] = after(pieces[1], blocks[k + 1])
        later, ahead = [w_gate, w_up], (size, width - size)
        if k == HALVES - 1:
            later, ahead = [w_down], (0, AHEAD * BLOCK)
        now, totals = gate_up(k, pieces, now, later, ahead, totals)
    hidden = totals[0]
    held = []
    early = AHEAD * BLOCK
    for k, (at, size) in enumerate(spans(width, BACK)):
        if k == 0:
            rest, (keep, send) = down(hidden, now, [(at, size)], [w_down])
        else:
            segments = [(at, early - at), (0, width - early)]
            _, (keep, send) = down(hidden, [*now, *rest], segments, [])
        bit = 1
        while bit < far:
            total = added(keep, swap(send, bit))
            keep, send = total[: total.shape[0] // 2], total[total.shape[0] // 2 :]
            bit *= 2
        held.append([total[j * CAP : (j + 1) * CAP] for j in range(2 * EXPERTS)])
    place = {s: 1 + j for j, s in enumerate(ORDER)}
    crossed = [swap(h[EXPERTS + place[2]], far) for h in held]
    middle = [shift(added(h[place[2]], x), -2) for h, x in zip(held, crossed)]
    mine = [jnp.concatenate([h[j] for h in held], axis=1) for j in range(2 * EXPERTS)]
    back = {}
    back[1] = swap(after(mine[EXPERTS + place[1]], crossed[1]), far)
    back[3] = swap(after(mine[EXPERTS + place[3]], crossed[0]), far)
    back[0] = swap(after(mine[EXPERTS], back[1], back[3]), far)
    near = shift(after(added(mine[place[1]], back[1]), middle[1]), -1)
    last = shift(after(added(mine[place[3]], back[3]), middle[0]), -3)
    arrived = back[0]
    pieces = [arrived, near, last, *[h[0] for h in held], *middle]
    terms = shares(group, ids, route_logits.T, hidden)
    return mix(terms, activations, pieces)


def solution(mesh):
    in_specs = (
        P(("parts", "expert"), None),
        P(("parts", "expert"), None),
        P(("parts", "expert"), None),
        P(),
        P("expert", None),
        P("expert", None),
        P("expert", None),
    )
    out_specs = P(("parts", "expert"), None)
    return jax.shard_map(
        on_device, mesh=mesh, in_specs=in_specs, out_specs=out_specs, check_vma=False
    )
```

```python
import functools

import jax
import jax.numpy as jnp
from jax import lax
from jax.experimental import pallas as pl
from jax.experimental.pallas import tpu as pltpu
from jax.sharding import PartitionSpec as P

EXPERTS = 4
CAP = 16
HALVES = 2
ORDER = (1, 3, 2)
FORTH = (7, 5)
BACK = (1, 1)
BLOCK = 512
AHEAD = 8
FETCH_ROWS = 144
MIB = 1 << 20
LIMIT = pltpu.CompilerParams(vmem_limit_bytes=10 * MIB)
WIDE = pltpu.CompilerParams(vmem_limit_bytes=32 * MIB)
VMEM = pl.BlockSpec(memory_space=pltpu.VMEM)
ANY = pl.BlockSpec(memory_space=pl.ANY)


def spans(width, shares=FORTH):
    unit = width // sum(shares)
    return [(sum(shares[:k]) * unit, n * unit) for k, n in enumerate(shares)]


def choices(ids, plane):
    tokens = ids.shape[1]
    line = lax.broadcasted_iota(jnp.int32, (EXPERTS * CAP, tokens), 0)
    expert = lax.rem(line // CAP + plane, EXPERTS)
    slot = (line % CAP).astype(jnp.float32)
    first = ids[0:1, :] == expert
    second = ids[1:2, :] == expert
    named = (first | second).astype(jnp.float32)
    square = (tokens, tokens)
    earlier = lax.broadcasted_iota(jnp.int32, square, 0) < lax.broadcasted_iota(
        jnp.int32, square, 1
    )
    rank = jnp.dot(named, earlier.astype(jnp.float32), preferred_element_type=jnp.float32)
    here = rank == slot
    return first & here, second & here


def pack_kernel(group, ids_ref, act_ref, gain_ref, *out_refs):
    plane = lax.axis_index("expert") // group
    values = act_ref[...].astype(jnp.float32)
    mean_sq = jnp.mean(values * values, axis=-1, keepdims=True)
    normed = (values * lax.rsqrt(mean_sq + 1e-06) * gain_ref[...]).astype(jnp.bfloat16)
    first, second = choices(ids_ref[...], plane)
    pick = (first | second).astype(jnp.float32).astype(jnp.bfloat16)
    rows = jnp.dot(pick, normed, preferred_element_type=jnp.float32).astype(jnp.bfloat16)
    out_refs[0][...] = rows[:CAP]
    for j, out_ref in enumerate(out_refs[1:]):
        k, s = j // (EXPERTS - 1), j % (EXPERTS - 1) + 1
        at, part = spans(rows.shape[1])[k]
        out_ref[...] = rows[s * CAP : (s + 1) * CAP, at : at + part]


def pack(group, ids, activations, gain):
    width = activations.shape[1]
    widths = [width] + [part for _, part in spans(width) for _ in range(EXPERTS - 1)]
    operands = [ids, activations, gain.reshape(1, width)]
    return pl.pallas_call(
        functools.partial(pack_kernel, group),
        grid=(1,),
        in_specs=[pl.BlockSpec(x.shape, lambda i: (0, 0)) for x in operands],
        out_specs=[pl.BlockSpec((CAP, n), lambda i: (0, 0)) for n in widths],
        out_shape=[jax.ShapeDtypeStruct((CAP, n), jnp.bfloat16) for n in widths],
        compiler_params=LIMIT,
        name="norm_and_pack",
    )(*[pltpu.with_memory_space_constraint(x, pltpu.HBM) for x in operands])


def fetches(weights, at, held, sems):
    copies = []
    for j, w in enumerate(weights):
        part = held[j].shape[1]
        for b in range(sems.shape[1]):
            rows = pl.ds(b * FETCH_ROWS, FETCH_ROWS)
            copies.append(
                pltpu.make_async_copy(w.at[rows, at : at + part], held[j].at[rows], sems.at[j, b])
            )
    return copies


def fetch_kernel(at, w_ref, after_ref, held_ref, sems):
    copies = fetches([w_ref], at, [held_ref], sems)
    for copy in copies:
        copy.start()
    for copy in copies:
        copy.wait()


def fetch(w, at, part, after):
    rows = w.shape[0]
    return pl.pallas_call(
        functools.partial(fetch_kernel, at),
        in_specs=[ANY, ANY],
        out_specs=VMEM,
        out_shape=pltpu.VMEM((rows, part), jnp.bfloat16),
        scratch_shapes=[pltpu.SemaphoreType.DMA((1, rows // FETCH_ROWS))],
        compiler_params=LIMIT,
        cost_estimate=pl.CostEstimate(flops=0, bytes_accessed=4 * rows * part, transcendentals=0),
        name="fetch",
    )(pltpu.with_memory_space_constraint(w, pltpu.HBM), after)


def relay_kernel(count, *refs):
    for x_ref, out_ref in zip(refs[:count], refs[count + 1 :]):
        out_ref[...] = x_ref[...]


def relay(arrays, after):
    count = len(arrays)
    return pl.pallas_call(
        functools.partial(relay_kernel, count),
        in_specs=[VMEM] * count + [ANY],
        out_specs=[VMEM] * count,
        out_shape=[jax.ShapeDtypeStruct(x.shape, x.dtype) for x in arrays],
        compiler_params=LIMIT,
        cost_estimate=pl.CostEstimate(flops=0, bytes_accessed=16 * MIB, transcendentals=0),
        name="relay",
    )(*arrays, after)


def gate_up_kernel(count, ahead, at, ahead_at, begin, end, *refs):
    pieces, refs = refs[:count], refs[count:]
    weights, later, refs = refs[:2], refs[2 : 2 + ahead], refs[2 + ahead :]
    if not begin:
        before, refs = refs[:2], refs[2:]
    held, refs = refs[:ahead], refs[ahead:]
    turned, sems, refs = *refs[-2:], refs[:-2]
    if end:
        hidden_ref, refs = refs[0], refs[1:]
    sums = refs
    part, rows = turned.shape
    copies = fetches(later, ahead_at, held, sems)
    for copy in copies:
        copy.start()

    @pl.loop(0, part // BLOCK)
    def _(c):
        parts = []
        for p in pieces:
            first = c * BLOCK + (at if p.shape[1] > part else 0)
            parts.append(p[:, pl.ds(pl.multiple_of(first, BLOCK), BLOCK)])
        turned[pl.ds(pl.multiple_of(c * BLOCK, BLOCK), BLOCK), :] = jnp.concatenate(parts, axis=0).T

    for j in range(2):
        total = jnp.dot(weights[j][...], turned[...], preferred_element_type=jnp.float32)
        sums[j][...] = total if begin else total + before[j][...]
    if end:
        hidden = (jax.nn.silu(sums[0][...]) * sums[1][...]).astype(jnp.bfloat16)
        hidden_ref[...] = hidden.T
    for copy in copies:
        copy.wait()


def gate_up(k, pieces, weights, later, ahead, totals):
    hidden, part = weights[0].shape
    begin, end = k == 0, k == HALVES - 1
    width = later[0].shape[1]
    rows = sum(p.shape[0] for p in pieces)
    total = jax.ShapeDtypeStruct((hidden, rows), jnp.float32)
    out_shape = [pltpu.VMEM((hidden, ahead[1]), jnp.bfloat16)] * len(later)
    out_specs = [VMEM] * len(later)
    scratch = []
    if end:
        out_shape.append(jax.ShapeDtypeStruct((rows, hidden), jnp.bfloat16))
        scratch += [pltpu.VMEM((hidden, rows), jnp.float32)] * 2
    else:
        out_shape += [total] * 2
    out_specs += [VMEM] * (len(out_shape) - len(later))
    scratch.append(pltpu.VMEM((part, rows), jnp.bfloat16))
    scratch.append(pltpu.SemaphoreType.DMA((len(later), hidden // FETCH_ROWS)))
    weights = [pltpu.with_memory_space_constraint(w, pltpu.VMEM) for w in weights]
    later = [pltpu.with_memory_space_constraint(w, pltpu.HBM) for w in later]
    out = pl.pallas_call(
        functools.partial(
            gate_up_kernel, len(pieces), len(later), spans(width)[k][0], ahead[0], begin, end
        ),
        in_specs=[VMEM] * (len(pieces) + 2) + [ANY] * len(later) + [VMEM] * len(totals),
        out_specs=out_specs,
        out_shape=out_shape,
        scratch_shapes=scratch,
        compiler_params=LIMIT if rows <= 256 else WIDE,
        cost_estimate=pl.CostEstimate(
            flops=4 * rows * hidden * part,
            bytes_accessed=4 * hidden * part + 8 * rows * hidden,
            transcendentals=0,
        ),
        name="gate_up",
    )(*pieces, *weights, *later, *totals)
    return out[: len(later)], out[len(later) :]


def down_kernel(ahead, segments, hidden_ref, *refs):
    weights, refs = refs[: len(segments)], refs[len(segments) :]
    later, held, refs = refs[:ahead], refs[ahead : 2 * ahead], refs[2 * ahead :]
    keep_ref, send_ref, sems = refs
    half, part = keep_ref.shape
    copies = fetches(later, AHEAD * BLOCK, held, sems)
    for copy in copies:
        copy.start()
    done = 0
    for w_ref, (first, size) in zip(weights, segments):
        block = size if size <= 2 * BLOCK else size // 2

        @pl.loop(0, size // block)
        def _(c, first=first, done=done, block=block, w_ref=w_ref):
            columns = pl.ds(pl.multiple_of(first + c * block, BLOCK), block)
            out = jnp.dot(hidden_ref[...], w_ref[:, columns], preferred_element_type=jnp.float32)
            out = out.astype(jnp.bfloat16)
            columns = pl.ds(pl.multiple_of(done + c * block, BLOCK), block)
            keep_ref[:, columns] = out[:half]
            send_ref[:, columns] = out[half:]

        done += size
    for copy in copies:
        copy.wait()


def down(hidden, weights, segments, later):
    rows, depth = hidden.shape
    part = sum(size for _, size in segments)
    ahead = len(later)
    out_shape = [pltpu.VMEM((depth, w.shape[1] - AHEAD * BLOCK), jnp.bfloat16) for w in later]
    out_shape += [jax.ShapeDtypeStruct((rows // 2, part), jnp.bfloat16)] * 2
    weights = [pltpu.with_memory_space_constraint(w, pltpu.VMEM) for w in weights]
    later = [pltpu.with_memory_space_constraint(w, pltpu.HBM) for w in later]
    out = pl.pallas_call(
        functools.partial(down_kernel, ahead, segments),
        in_specs=[VMEM] * (1 + len(weights)) + [ANY] * ahead,
        out_specs=[VMEM] * (ahead + 2),
        out_shape=out_shape,
        scratch_shapes=[pltpu.SemaphoreType.DMA((max(ahead, 1), depth // FETCH_ROWS))],
        compiler_params=LIMIT if rows <= 256 else WIDE,
        cost_estimate=pl.CostEstimate(
            flops=2 * rows * depth * part,
            bytes_accessed=2 * (depth * part + rows * depth + rows * part),
            transcendentals=0,
        ),
        name="down",
    )(hidden, *weights, *later)
    return out[:ahead], out[ahead:]


def shares_kernel(group, ids_ref, logits_ref, after_ref, out_ref):
    plane = lax.axis_index("expert") // group
    first, second = choices(ids_ref[...], plane)
    lead = logits_ref[0:1, :] - logits_ref[1:2, :]
    weight = jnp.where(first, jax.nn.sigmoid(lead), 0.0)
    weight = (weight + jnp.where(second, jax.nn.sigmoid(-lead), 0.0)).T
    high = weight.astype(jnp.bfloat16).astype(jnp.float32)
    middle = (weight - high).astype(jnp.bfloat16).astype(jnp.float32)
    terms = jnp.concatenate([weight - high - middle, middle, high], axis=0)
    out_ref[...] = terms


def shares(group, ids, logits, after):
    shape = (3 * ids.shape[1], EXPERTS * CAP)
    return pl.pallas_call(
        functools.partial(shares_kernel, group),
        in_specs=[VMEM, VMEM, ANY],
        out_specs=VMEM,
        out_shape=jax.ShapeDtypeStruct(shape, jnp.float32),
        compiler_params=LIMIT,
        name="shares",
    )(ids, logits, after)


def mix_kernel(terms_ref, act_ref, arrived, near, last, *refs):
    out_ref, kept, middle_rows = refs[-1], refs[:HALVES], refs[HALVES:-1]
    tokens = act_ref.shape[0]
    terms = terms_ref[...].astype(jnp.bfloat16)
    for k, (at, part) in enumerate(spans(act_ref.shape[1], BACK)):
        columns = slice(at, at + part)
        own = kept[k][...].astype(jnp.float32) + arrived[:, columns].astype(jnp.float32)
        blocks = [own.astype(jnp.bfloat16), near[:, columns], middle_rows[k][...]]
        rows = jnp.concatenate(blocks + [last[:, columns]], axis=0)
        sums = jnp.dot(terms, rows, preferred_element_type=jnp.float32)
        total = act_ref[:, columns].astype(jnp.float32)
        for j in range(3):
            total = total + sums[j * tokens : (j + 1) * tokens]
        out_ref[:, columns] = total.astype(jnp.bfloat16)


def mix(terms, activations, pieces):
    return pl.pallas_call(
        mix_kernel,
        out_shape=jax.ShapeDtypeStruct(activations.shape, jnp.bfloat16),
        compiler_params=LIMIT,
        name="mix",
    )(terms, activations, *pieces)


def added(mine, arrived):
    total = mine.astype(jnp.float32) + arrived.astype(jnp.float32)
    return total.astype(jnp.bfloat16)


def on_device(activations, expert_ids, route_logits, norm_gain, w_gate, w_up, w_down):
    devices = lax.axis_size("expert")
    group = devices // EXPERTS
    far = group // 2
    width = activations.shape[1]
    part = width // HALVES

    def shift(x, s):
        return lax.ppermute(
            x, "expert", [(i, (i + s * group) % devices) for i in range(devices)]
        )

    def swap(x, bit):
        return lax.ppermute(x, "expert", [(i, i ^ bit) for i in range(devices)])

    def after(x, *others):
        return lax.optimization_barrier((x, *others))[0]

    others = EXPERTS - 1
    ids = expert_ids.T
    own, *sends = pack(group, ids, activations, norm_gain)
    size = spans(width)[0][1]
    now = [fetch(w_gate, 0, size, own)]
    fetched = after(own, *now)
    far_own = swap(fetched, far)
    now.append(fetch(w_up, 0, size, fetched))
    blocks = []
    for k in range(HALVES):
        x = sends[k * others : (k + 1) * others]
        if k:
            x = relay(after(x, *now, far_own), blocks[-1])
        arrivals = [shift(x[s - 1], s) for s in ORDER]
        blocks.append(jnp.concatenate(arrivals, axis=0))
    totals = []
    for k in range(HALVES):
        at, size = spans(width)[k]
        columns = slice(at, at + size)
        far_block = swap(blocks[k], far)
        if totals:
            far_block, totals = lax.optimization_barrier((far_block, totals))
        pieces = [own[:, columns], blocks[k], far_own[:, columns], far_block]
        bit = far // 2
        while bit:
            if k and len(pieces) == EXPERTS:
                early = swap(jnp.concatenate(pieces[:-1], axis=0), bit)
                pieces += [early, swap(far_block, bit)]
            else:
                pieces.append(swap(jnp.concatenate(pieces, axis=0), bit))
            bit //= 2
        pieces[0], pieces[2] = own, far_own
        if k < HALVES - 1:
            pieces[1] = after(pieces[1], blocks[k + 1])
        later, ahead = [w_gate, w_up], (size, width - size)
        if k == HALVES - 1:
            later, ahead = [w_down], (0, AHEAD * BLOCK)
        now, totals = gate_up(k, pieces, now, later, ahead, totals)
    hidden = totals[0]
    held = []
    early = AHEAD * BLOCK
    for k, (at, size) in enumerate(spans(width, BACK)):
        if k == 0:
            rest, (keep, send) = down(hidden, now, [(at, size)], [w_down])
        else:
            segments = [(at, early - at), (0, width - early)]
            _, (keep, send) = down(hidden, [*now, *rest], segments, [])
        bit = 1
        while bit < far:
            total = added(keep, swap(send, bit))
            keep, send = total[: total.shape[0] // 2], total[total.shape[0] // 2 :]
            bit *= 2
        held.append([total[j * CAP : (j + 1) * CAP] for j in range(2 * EXPERTS)])
    place = {s: 1 + j for j, s in enumerate(ORDER)}
    crossed = [swap(h[EXPERTS + place[2]], far) for h in held]
    middle = [shift(added(h[place[2]], x), -2) for h, x in zip(held, crossed)]
    mine = [jnp.concatenate([h[j] for h in held], axis=1) for j in range(2 * EXPERTS)]
    back = {}
    back[1] = swap(after(mine[EXPERTS + place[1]], crossed[1]), far)
    back[3] = swap(after(mine[EXPERTS + place[3]], crossed[0]), far)
    back[0] = swap(after(mine[EXPERTS], back[1], back[3]), far)
    near = shift(after(added(mine[place[1]], back[1]), middle[1]), -1)
    last = shift(after(added(mine[place[3]], back[3]), middle[0]), -3)
    arrived = back[0]
    pieces = [arrived, near, last, *[h[0] for h in held], *middle]
    terms = shares(group, ids, route_logits.T, hidden)
    return mix(terms, activations, pieces)


def solution(mesh):
    in_specs = (
        P(("parts", "expert"), None),
        P(("parts", "expert"), None),
        P(("parts", "expert"), None),
        P(),
        P("expert", None),
        P("expert", None),
        P("expert", None),
    )
    out_specs = P(("parts", "expert"), None)
    return jax.shard_map(
        on_device, mesh=mesh, in_specs=in_specs, out_specs=out_specs, check_vma=False
    )
```

```python
import functools

import jax
import jax.numpy as jnp
from jax import lax
from jax.experimental import pallas as pl
from jax.experimental.pallas import tpu as pltpu
from jax.sharding import PartitionSpec as P

EXPERTS = 4
CAP = 16
HALVES = 2
ORDER = (1, 3, 2)
FORTH = (7, 5)
BACK = (1, 1)
BLOCK = 512
AHEAD = 8
FETCH_ROWS = 144
MIB = 1 << 20
LIMIT = pltpu.CompilerParams(vmem_limit_bytes=10 * MIB)
WIDE = pltpu.CompilerParams(vmem_limit_bytes=32 * MIB)
VMEM = pl.BlockSpec(memory_space=pltpu.VMEM)
ANY = pl.BlockSpec(memory_space=pl.ANY)


def spans(width, shares=FORTH):
    unit = width // sum(shares)
    return [(sum(shares[:k]) * unit, n * unit) for k, n in enumerate(shares)]


def choices(ids, plane):
    tokens = ids.shape[1]
    line = lax.broadcasted_iota(jnp.int32, (EXPERTS * CAP, tokens), 0)
    expert = lax.rem(line // CAP + plane, EXPERTS)
    slot = (line % CAP).astype(jnp.float32)
    first = ids[0:1, :] == expert
    second = ids[1:2, :] == expert
    named = (first | second).astype(jnp.float32)
    square = (tokens, tokens)
    earlier = lax.broadcasted_iota(jnp.int32, square, 0) < lax.broadcasted_iota(
        jnp.int32, square, 1
    )
    rank = jnp.dot(named, earlier.astype(jnp.float32), preferred_element_type=jnp.float32)
    here = rank == slot
    return first & here, second & here


def pack_kernel(group, ids_ref, act_ref, gain_ref, *out_refs):
    plane = lax.axis_index("expert") // group
    values = act_ref[...].astype(jnp.float32)
    mean_sq = jnp.mean(values * values, axis=-1, keepdims=True)
    normed = (values * lax.rsqrt(mean_sq + 1e-06) * gain_ref[...]).astype(jnp.bfloat16)
    first, second = choices(ids_ref[...], plane)
    pick = (first | second).astype(jnp.float32).astype(jnp.bfloat16)
    rows = jnp.dot(pick, normed, preferred_element_type=jnp.float32).astype(jnp.bfloat16)
    out_refs[0][...] = rows[:CAP]
    for j, out_ref in enumerate(out_refs[1:]):
        k, s = j // (EXPERTS - 1), j % (EXPERTS - 1) + 1
        at, part = spans(rows.shape[1])[k]
        out_ref[...] = rows[s * CAP : (s + 1) * CAP, at : at + part]


def pack(group, ids, activations, gain):
    width = activations.shape[1]
    widths = [width] + [part for _, part in spans(width) for _ in range(EXPERTS - 1)]
    operands = [ids, activations, gain.reshape(1, width)]
    return pl.pallas_call(
        functools.partial(pack_kernel, group),
        grid=(1,),
        in_specs=[pl.BlockSpec(x.shape, lambda i: (0, 0)) for x in operands],
        out_specs=[pl.BlockSpec((CAP, n), lambda i: (0, 0)) for n in widths],
        out_shape=[jax.ShapeDtypeStruct((CAP, n), jnp.bfloat16) for n in widths],
        compiler_params=LIMIT,
        name="norm_and_pack",
    )(*[pltpu.with_memory_space_constraint(x, pltpu.HBM) for x in operands])


def fetches(weights, at, held, sems):
    copies = []
    for j, w in enumerate(weights):
        part = held[j].shape[1]
        for b in range(sems.shape[1]):
            rows = pl.ds(b * FETCH_ROWS, FETCH_ROWS)
            copies.append(
                pltpu.make_async_copy(w.at[rows, at : at + part], held[j].at[rows], sems.at[j, b])
            )
    return copies


def fetch_kernel(at, w_ref, after_ref, held_ref, sems):
    copies = fetches([w_ref], at, [held_ref], sems)
    for copy in copies:
        copy.start()
    for copy in copies:
        copy.wait()


def fetch(w, at, part, after):
    rows = w.shape[0]
    return pl.pallas_call(
        functools.partial(fetch_kernel, at),
        in_specs=[ANY, ANY],
        out_specs=VMEM,
        out_shape=pltpu.VMEM((rows, part), jnp.bfloat16),
        scratch_shapes=[pltpu.SemaphoreType.DMA((1, rows // FETCH_ROWS))],
        compiler_params=LIMIT,
        cost_estimate=pl.CostEstimate(flops=0, bytes_accessed=4 * rows * part, transcendentals=0),
        name="fetch",
    )(pltpu.with_memory_space_constraint(w, pltpu.HBM), after)


def relay_kernel(count, *refs):
    for x_ref, out_ref in zip(refs[:count], refs[count + 1 :]):
        out_ref[...] = x_ref[...]


def relay(arrays, after):
    count = len(arrays)
    return pl.pallas_call(
        functools.partial(relay_kernel, count),
        in_specs=[VMEM] * count + [ANY],
        out_specs=[VMEM] * count,
        out_shape=[jax.ShapeDtypeStruct(x.shape, x.dtype) for x in arrays],
        compiler_params=LIMIT,
        cost_estimate=pl.CostEstimate(flops=0, bytes_accessed=16 * MIB, transcendentals=0),
        name="relay",
    )(*arrays, after)


def gate_up_kernel(count, ahead, at, ahead_at, begin, end, *refs):
    pieces, refs = refs[:count], refs[count:]
    weights, later, refs = refs[:2], refs[2 : 2 + ahead], refs[2 + ahead :]
    if not begin:
        before, refs = refs[:2], refs[2:]
    held, refs = refs[:ahead], refs[ahead:]
    turned, sems, refs = *refs[-2:], refs[:-2]
    if end:
        hidden_ref, refs = refs[0], refs[1:]
    sums = refs
    part, rows = turned.shape
    copies = fetches(later, ahead_at, held, sems)
    for copy in copies:
        copy.start()

    @pl.loop(0, part // BLOCK)
    def _(c):
        parts = []
        for p in pieces:
            first = c * BLOCK + (at if p.shape[1] > part else 0)
            parts.append(p[:, pl.ds(pl.multiple_of(first, BLOCK), BLOCK)])
        turned[pl.ds(pl.multiple_of(c * BLOCK, BLOCK), BLOCK), :] = jnp.concatenate(parts, axis=0).T

    for j in range(2):
        total = jnp.dot(weights[j][...], turned[...], preferred_element_type=jnp.float32)
        sums[j][...] = total if begin else total + before[j][...]
    if end:
        hidden = (jax.nn.silu(sums[0][...]) * sums[1][...]).astype(jnp.bfloat16)
        hidden_ref[...] = hidden.T
    for copy in copies:
        copy.wait()


def gate_up(k, pieces, weights, later, ahead, totals):
    hidden, part = weights[0].shape
    begin, end = k == 0, k == HALVES - 1
    width = later[0].shape[1]
    rows = sum(p.shape[0] for p in pieces)
    total = jax.ShapeDtypeStruct((hidden, rows), jnp.float32)
    out_shape = [pltpu.VMEM((hidden, ahead[1]), jnp.bfloat16)] * len(later)
    out_specs = [VMEM] * len(later)
    scratch = []
    if end:
        out_shape.append(jax.ShapeDtypeStruct((rows, hidden), jnp.bfloat16))
        scratch += [pltpu.VMEM((hidden, rows), jnp.float32)] * 2
    else:
        out_shape += [total] * 2
    out_specs += [VMEM] * (len(out_shape) - len(later))
    scratch.append(pltpu.VMEM((part, rows), jnp.bfloat16))
    scratch.append(pltpu.SemaphoreType.DMA((len(later), hidden // FETCH_ROWS)))
    weights = [pltpu.with_memory_space_constraint(w, pltpu.VMEM) for w in weights]
    later = [pltpu.with_memory_space_constraint(w, pltpu.HBM) for w in later]
    out = pl.pallas_call(
        functools.partial(
            gate_up_kernel, len(pieces), len(later), spans(width)[k][0], ahead[0], begin, end
        ),
        in_specs=[VMEM] * (len(pieces) + 2) + [ANY] * len(later) + [VMEM] * len(totals),
        out_specs=out_specs,
        out_shape=out_shape,
        scratch_shapes=scratch,
        compiler_params=LIMIT if rows <= 256 else WIDE,
        cost_estimate=pl.CostEstimate(
            flops=4 * rows * hidden * part,
            bytes_accessed=4 * hidden * part + 8 * rows * hidden,
            transcendentals=0,
        ),
        name="gate_up",
    )(*pieces, *weights, *later, *totals)
    return out[: len(later)], out[len(later) :]


def down_kernel(ahead, segments, hidden_ref, *refs):
    weights, refs = refs[: len(segments)], refs[len(segments) :]
    later, held, refs = refs[:ahead], refs[ahead : 2 * ahead], refs[2 * ahead :]
    keep_ref, send_ref, sems = refs
    half, part = keep_ref.shape
    copies = fetches(later, AHEAD * BLOCK, held, sems)
    for copy in copies:
        copy.start()
    done = 0
    for w_ref, (first, size) in zip(weights, segments):
        block = size if size <= 2 * BLOCK else size // 2

        @pl.loop(0, size // block)
        def _(c, first=first, done=done, block=block, w_ref=w_ref):
            columns = pl.ds(pl.multiple_of(first + c * block, BLOCK), block)
            out = jnp.dot(hidden_ref[...], w_ref[:, columns], preferred_element_type=jnp.float32)
            out = out.astype(jnp.bfloat16)
            columns = pl.ds(pl.multiple_of(done + c * block, BLOCK), block)
            keep_ref[:, columns] = out[:half]
            send_ref[:, columns] = out[half:]

        done += size
    for copy in copies:
        copy.wait()


def down(hidden, weights, segments, later):
    rows, depth = hidden.shape
    part = sum(size for _, size in segments)
    ahead = len(later)
    out_shape = [pltpu.VMEM((depth, w.shape[1] - AHEAD * BLOCK), jnp.bfloat16) for w in later]
    out_shape += [jax.ShapeDtypeStruct((rows // 2, part), jnp.bfloat16)] * 2
    weights = [pltpu.with_memory_space_constraint(w, pltpu.VMEM) for w in weights]
    later = [pltpu.with_memory_space_constraint(w, pltpu.HBM) for w in later]
    out = pl.pallas_call(
        functools.partial(down_kernel, ahead, segments),
        in_specs=[VMEM] * (1 + len(weights)) + [ANY] * ahead,
        out_specs=[VMEM] * (ahead + 2),
        out_shape=out_shape,
        scratch_shapes=[pltpu.SemaphoreType.DMA((max(ahead, 1), depth // FETCH_ROWS))],
        compiler_params=LIMIT if rows <= 256 else WIDE,
        cost_estimate=pl.CostEstimate(
            flops=2 * rows * depth * part,
            bytes_accessed=2 * (depth * part + rows * depth + rows * part),
            transcendentals=0,
        ),
        name="down",
    )(hidden, *weights, *later)
    return out[:ahead], out[ahead:]


def shares_kernel(group, ids_ref, logits_ref, after_ref, out_ref):
    plane = lax.axis_index("expert") // group
    first, second = choices(ids_ref[...], plane)
    lead = logits_ref[0:1, :] - logits_ref[1:2, :]
    weight = jnp.where(first, jax.nn.sigmoid(lead), 0.0)
    weight = (weight + jnp.where(second, jax.nn.sigmoid(-lead), 0.0)).T
    high = weight.astype(jnp.bfloat16).astype(jnp.float32)
    middle = (weight - high).astype(jnp.bfloat16).astype(jnp.float32)
    terms = jnp.concatenate([weight - high - middle, middle, high], axis=0)
    out_ref[...] = terms


def shares(group, ids, logits, after):
    shape = (3 * ids.shape[1], EXPERTS * CAP)
    return pl.pallas_call(
        functools.partial(shares_kernel, group),
        in_specs=[VMEM, VMEM, ANY],
        out_specs=VMEM,
        out_shape=jax.ShapeDtypeStruct(shape, jnp.float32),
        compiler_params=LIMIT,
        name="shares",
    )(ids, logits, after)


def mix_kernel(terms_ref, act_ref, arrived, last, near, *refs):
    out_ref, kept, middle_rows = refs[-1], refs[:HALVES], refs[HALVES:-1]
    tokens = act_ref.shape[0]
    terms = terms_ref[...].astype(jnp.bfloat16)
    for k, (at, part) in enumerate(spans(act_ref.shape[1], BACK)):
        columns = slice(at, at + part)
        own = kept[k][...].astype(jnp.float32) + arrived[:, columns].astype(jnp.float32)
        blocks = [own.astype(jnp.bfloat16), near[:, columns], middle_rows[k][...]]
        rows = jnp.concatenate(blocks + [last[:, columns]], axis=0)
        sums = jnp.dot(terms, rows, preferred_element_type=jnp.float32)
        total = act_ref[:, columns].astype(jnp.float32)
        for j in range(3):
            total = total + sums[j * tokens : (j + 1) * tokens]
        out_ref[:, columns] = total.astype(jnp.bfloat16)


def mix(terms, activations, pieces):
    return pl.pallas_call(
        mix_kernel,
        out_shape=jax.ShapeDtypeStruct(activations.shape, jnp.bfloat16),
        compiler_params=LIMIT,
        name="mix",
    )(terms, activations, *pieces)


def added(mine, arrived):
    total = mine.astype(jnp.float32) + arrived.astype(jnp.float32)
    return total.astype(jnp.bfloat16)


def on_device(activations, expert_ids, route_logits, norm_gain, w_gate, w_up, w_down):
    devices = lax.axis_size("expert")
    group = devices // EXPERTS
    far = group // 2
    width = activations.shape[1]
    part = width // HALVES

    def shift(x, s):
        return lax.ppermute(
            x, "expert", [(i, (i + s * group) % devices) for i in range(devices)]
        )

    def swap(x, bit):
        return lax.ppermute(x, "expert", [(i, i ^ bit) for i in range(devices)])

    def after(x, *others):
        return lax.optimization_barrier((x, *others))[0]

    others = EXPERTS - 1
    ids = expert_ids.T
    own, *sends = pack(group, ids, activations, norm_gain)
    size = spans(width)[0][1]
    now = [fetch(w_gate, 0, size, own)]
    fetched = after(own, *now)
    far_own = swap(fetched, far)
    now.append(fetch(w_up, 0, size, fetched))
    blocks = []
    for k in range(HALVES):
        x = sends[k * others : (k + 1) * others]
        if k:
            x = relay(after(x, *now, far_own), blocks[-1])
        arrivals = [shift(x[s - 1], s) for s in ORDER]
        blocks.append(jnp.concatenate(arrivals, axis=0))
    totals = []
    for k in range(HALVES):
        at, size = spans(width)[k]
        columns = slice(at, at + size)
        far_block = swap(blocks[k], far)
        if totals:
            far_block, totals = lax.optimization_barrier((far_block, totals))
        pieces = [own[:, columns], blocks[k], far_own[:, columns], far_block]
        bit = far // 2
        while bit:
            if k and len(pieces) == EXPERTS:
                early = swap(jnp.concatenate(pieces[:-1], axis=0), bit)
                pieces += [early, swap(far_block, bit)]
            else:
                pieces.append(swap(jnp.concatenate(pieces, axis=0), bit))
            bit //= 2
        pieces[0], pieces[2] = own, far_own
        if k < HALVES - 1:
            pieces[1] = after(pieces[1], blocks[k + 1])
        later, ahead = [w_gate, w_up], (size, width - size)
        if k == HALVES - 1:
            later, ahead = [w_down], (0, AHEAD * BLOCK)
        now, totals = gate_up(k, pieces, now, later, ahead, totals)
    hidden = totals[0]
    held = []
    early = AHEAD * BLOCK
    for k, (at, size) in enumerate(spans(width, BACK)):
        if k == 0:
            rest, (keep, send) = down(hidden, now, [(at, size)], [w_down])
        else:
            segments = [(at, early - at), (0, width - early)]
            _, (keep, send) = down(hidden, [*now, *rest], segments, [])
        bit = 1
        while bit < far:
            total = added(keep, swap(send, bit))
            keep, send = total[: total.shape[0] // 2], total[total.shape[0] // 2 :]
            bit *= 2
        held.append([total[j * CAP : (j + 1) * CAP] for j in range(2 * EXPERTS)])
    place = {s: 1 + j for j, s in enumerate(ORDER)}
    crossed = [swap(h[EXPERTS + place[2]], far) for h in held]
    middle = [shift(added(h[place[2]], x), -2) for h, x in zip(held, crossed)]
    mine = [jnp.concatenate([h[j] for h in held], axis=1) for j in range(2 * EXPERTS)]
    back = {}
    back[3] = swap(after(mine[EXPERTS + place[3]], crossed[1]), far)
    back[1] = swap(after(mine[EXPERTS + place[1]], crossed[0]), far)
    back[0] = swap(after(mine[EXPERTS], back[3], back[1]), far)
    last = shift(after(added(mine[place[3]], back[3]), middle[1]), -3)
    near = shift(after(added(mine[place[1]], back[1]), middle[0]), -1)
    arrived = back[0]
    pieces = [arrived, last, near, *[h[0] for h in held], *middle]
    terms = shares(group, ids, route_logits.T, hidden)
    return mix(terms, activations, pieces)


def solution(mesh):
    in_specs = (
        P(("parts", "expert"), None),
        P(("parts", "expert"), None),
        P(("parts", "expert"), None),
        P(),
        P("expert", None),
        P("expert", None),
        P("expert", None),
    )
    out_specs = P(("parts", "expert"), None)
    return jax.shard_map(
        on_device, mesh=mesh, in_specs=in_specs, out_specs=out_specs, check_vma=False
    )
```

```python
import functools

import jax
import jax.numpy as jnp
from jax import lax
from jax.experimental import pallas as pl
from jax.experimental.pallas import tpu as pltpu
from jax.sharding import PartitionSpec as P

EXPERTS = 4
CAP = 16
HALVES = 2
ORDER = (1, 3, 2)
FORTH = (7, 5)
BACK = (1, 1)
BLOCK = 512
AHEAD = 8
FETCH_ROWS = 144
MIB = 1 << 20
LIMIT = pltpu.CompilerParams(vmem_limit_bytes=10 * MIB)
WIDE = pltpu.CompilerParams(vmem_limit_bytes=32 * MIB)
VMEM = pl.BlockSpec(memory_space=pltpu.VMEM)
ANY = pl.BlockSpec(memory_space=pl.ANY)


def spans(width, shares=FORTH):
    unit = width // sum(shares)
    return [(sum(shares[:k]) * unit, n * unit) for k, n in enumerate(shares)]


def choices(ids, plane):
    tokens = ids.shape[1]
    line = lax.broadcasted_iota(jnp.int32, (EXPERTS * CAP, tokens), 0)
    expert = lax.rem(line // CAP + plane, EXPERTS)
    slot = (line % CAP).astype(jnp.float32)
    first = ids[0:1, :] == expert
    second = ids[1:2, :] == expert
    named = (first | second).astype(jnp.float32)
    square = (tokens, tokens)
    earlier = lax.broadcasted_iota(jnp.int32, square, 0) < lax.broadcasted_iota(
        jnp.int32, square, 1
    )
    rank = jnp.dot(named, earlier.astype(jnp.float32), preferred_element_type=jnp.float32)
    here = rank == slot
    return first & here, second & here


def pack_kernel(group, ids_ref, act_ref, gain_ref, *out_refs):
    plane = lax.axis_index("expert") // group
    values = act_ref[...].astype(jnp.float32)
    mean_sq = jnp.mean(values * values, axis=-1, keepdims=True)
    normed = (values * lax.rsqrt(mean_sq + 1e-06) * gain_ref[...]).astype(jnp.bfloat16)
    first, second = choices(ids_ref[...], plane)
    pick = (first | second).astype(jnp.float32).astype(jnp.bfloat16)
    rows = jnp.dot(pick, normed, preferred_element_type=jnp.float32).astype(jnp.bfloat16)
    out_refs[0][...] = rows[:CAP]
    for j, out_ref in enumerate(out_refs[1:]):
        k, s = j // (EXPERTS - 1), j % (EXPERTS - 1) + 1
        at, part = spans(rows.shape[1])[k]
        out_ref[...] = rows[s * CAP : (s + 1) * CAP, at : at + part]


def pack(group, ids, activations, gain):
    width = activations.shape[1]
    widths = [width] + [part for _, part in spans(width) for _ in range(EXPERTS - 1)]
    operands = [ids, activations, gain.reshape(1, width)]
    return pl.pallas_call(
        functools.partial(pack_kernel, group),
        grid=(1,),
        in_specs=[pl.BlockSpec(x.shape, lambda i: (0, 0)) for x in operands],
        out_specs=[pl.BlockSpec((CAP, n), lambda i: (0, 0)) for n in widths],
        out_shape=[jax.ShapeDtypeStruct((CAP, n), jnp.bfloat16) for n in widths],
        compiler_params=LIMIT,
        name="norm_and_pack",
    )(*[pltpu.with_memory_space_constraint(x, pltpu.HBM) for x in operands])


def fetches(weights, at, held, sems):
    copies = []
    for j, w in enumerate(weights):
        part = held[j].shape[1]
        for b in range(sems.shape[1]):
            rows = pl.ds(b * FETCH_ROWS, FETCH_ROWS)
            copies.append(
                pltpu.make_async_copy(w.at[rows, at : at + part], held[j].at[rows], sems.at[j, b])
            )
    return copies


def fetch_kernel(at, w_ref, after_ref, held_ref, sems):
    copies = fetches([w_ref], at, [held_ref], sems)
    for copy in copies:
        copy.start()
    for copy in copies:
        copy.wait()


def fetch(w, at, part, after):
    rows = w.shape[0]
    return pl.pallas_call(
        functools.partial(fetch_kernel, at),
        in_specs=[ANY, ANY],
        out_specs=VMEM,
        out_shape=pltpu.VMEM((rows, part), jnp.bfloat16),
        scratch_shapes=[pltpu.SemaphoreType.DMA((1, rows // FETCH_ROWS))],
        compiler_params=LIMIT,
        cost_estimate=pl.CostEstimate(flops=0, bytes_accessed=4 * rows * part, transcendentals=0),
        name="fetch",
    )(pltpu.with_memory_space_constraint(w, pltpu.HBM), after)


def relay_kernel(count, *refs):
    for x_ref, out_ref in zip(refs[:count], refs[count + 1 :]):
        out_ref[...] = x_ref[...]


def relay(arrays, after):
    count = len(arrays)
    return pl.pallas_call(
        functools.partial(relay_kernel, count),
        in_specs=[VMEM] * count + [ANY],
        out_specs=[VMEM] * count,
        out_shape=[jax.ShapeDtypeStruct(x.shape, x.dtype) for x in arrays],
        compiler_params=LIMIT,
        cost_estimate=pl.CostEstimate(flops=0, bytes_accessed=16 * MIB, transcendentals=0),
        name="relay",
    )(*arrays, after)


def gate_up_kernel(count, ahead, at, ahead_at, begin, end, *refs):
    pieces, refs = refs[:count], refs[count:]
    weights, later, refs = refs[:2], refs[2 : 2 + ahead], refs[2 + ahead :]
    if not begin:
        before, refs = refs[:2], refs[2:]
    held, refs = refs[:ahead], refs[ahead:]
    turned, sems, refs = *refs[-2:], refs[:-2]
    if end:
        hidden_ref, refs = refs[0], refs[1:]
    sums = refs
    part, rows = turned.shape
    copies = fetches(later, ahead_at, held, sems)
    for copy in copies:
        copy.start()

    @pl.loop(0, part // BLOCK)
    def _(c):
        parts = []
        for p in pieces:
            first = c * BLOCK + (at if p.shape[1] > part else 0)
            parts.append(p[:, pl.ds(pl.multiple_of(first, BLOCK), BLOCK)])
        turned[pl.ds(pl.multiple_of(c * BLOCK, BLOCK), BLOCK), :] = jnp.concatenate(parts, axis=0).T

    units = weights[0].shape[0]
    block = 384 if end and units % 384 == 0 else units
    for first in range(0, units, block):
        here = slice(first, first + block)
        totals = []
        for j in range(2):
            total = jnp.dot(weights[j][here, :], turned[...], preferred_element_type=jnp.float32)
            totals.append(total if begin else total + before[j][here, :])
        if end:
            hidden = (jax.nn.silu(totals[0]) * totals[1]).astype(jnp.bfloat16)
            hidden_ref[:, here] = hidden.T
        else:
            sums[0][...] = totals[0]
            sums[1][...] = totals[1]
    for copy in copies:
        copy.wait()


def gate_up(k, pieces, weights, later, ahead, totals):
    hidden, part = weights[0].shape
    begin, end = k == 0, k == HALVES - 1
    width = later[0].shape[1]
    rows = sum(p.shape[0] for p in pieces)
    total = jax.ShapeDtypeStruct((hidden, rows), jnp.float32)
    out_shape = [pltpu.VMEM((hidden, ahead[1]), jnp.bfloat16)] * len(later)
    out_specs = [VMEM] * len(later)
    scratch = []
    if end:
        out_shape.append(jax.ShapeDtypeStruct((rows, hidden), jnp.bfloat16))
    else:
        out_shape += [total] * 2
    out_specs += [VMEM] * (len(out_shape) - len(later))
    scratch.append(pltpu.VMEM((part, rows), jnp.bfloat16))
    scratch.append(pltpu.SemaphoreType.DMA((len(later), hidden // FETCH_ROWS)))
    weights = [pltpu.with_memory_space_constraint(w, pltpu.VMEM) for w in weights]
    later = [pltpu.with_memory_space_constraint(w, pltpu.HBM) for w in later]
    out = pl.pallas_call(
        functools.partial(
            gate_up_kernel, len(pieces), len(later), spans(width)[k][0], ahead[0], begin, end
        ),
        in_specs=[VMEM] * (len(pieces) + 2) + [ANY] * len(later) + [VMEM] * len(totals),
        out_specs=out_specs,
        out_shape=out_shape,
        scratch_shapes=scratch,
        compiler_params=LIMIT if rows <= 256 else WIDE,
        cost_estimate=pl.CostEstimate(
            flops=4 * rows * hidden * part,
            bytes_accessed=4 * hidden * part + 8 * rows * hidden,
            transcendentals=0,
        ),
        name="gate_up",
    )(*pieces, *weights, *later, *totals)
    return out[: len(later)], out[len(later) :]


def down_kernel(ahead, segments, hidden_ref, *refs):
    weights, refs = refs[: len(segments)], refs[len(segments) :]
    later, held, refs = refs[:ahead], refs[ahead : 2 * ahead], refs[2 * ahead :]
    keep_ref, send_ref, sems = refs
    half, part = keep_ref.shape
    copies = fetches(later, AHEAD * BLOCK, held, sems)
    for copy in copies:
        copy.start()
    done = 0
    for w_ref, (first, size) in zip(weights, segments):
        block = size if size <= 2 * BLOCK else size // 2

        @pl.loop(0, size // block)
        def _(c, first=first, done=done, block=block, w_ref=w_ref):
            columns = pl.ds(pl.multiple_of(first + c * block, BLOCK), block)
            out = jnp.dot(hidden_ref[...], w_ref[:, columns], preferred_element_type=jnp.float32)
            out = out.astype(jnp.bfloat16)
            columns = pl.ds(pl.multiple_of(done + c * block, BLOCK), block)
            keep_ref[:, columns] = out[:half]
            send_ref[:, columns] = out[half:]

        done += size
    for copy in copies:
        copy.wait()


def down(hidden, weights, segments, later):
    rows, depth = hidden.shape
    part = sum(size for _, size in segments)
    ahead = len(later)
    out_shape = [pltpu.VMEM((depth, w.shape[1] - AHEAD * BLOCK), jnp.bfloat16) for w in later]
    out_shape += [jax.ShapeDtypeStruct((rows // 2, part), jnp.bfloat16)] * 2
    weights = [pltpu.with_memory_space_constraint(w, pltpu.VMEM) for w in weights]
    later = [pltpu.with_memory_space_constraint(w, pltpu.HBM) for w in later]
    out = pl.pallas_call(
        functools.partial(down_kernel, ahead, segments),
        in_specs=[VMEM] * (1 + len(weights)) + [ANY] * ahead,
        out_specs=[VMEM] * (ahead + 2),
        out_shape=out_shape,
        scratch_shapes=[pltpu.SemaphoreType.DMA((max(ahead, 1), depth // FETCH_ROWS))],
        compiler_params=LIMIT if rows <= 256 else WIDE,
        cost_estimate=pl.CostEstimate(
            flops=2 * rows * depth * part,
            bytes_accessed=2 * (depth * part + rows * depth + rows * part),
            transcendentals=0,
        ),
        name="down",
    )(hidden, *weights, *later)
    return out[:ahead], out[ahead:]


def shares_kernel(group, ids_ref, logits_ref, after_ref, out_ref):
    plane = lax.axis_index("expert") // group
    first, second = choices(ids_ref[...], plane)
    lead = logits_ref[0:1, :] - logits_ref[1:2, :]
    weight = jnp.where(first, jax.nn.sigmoid(lead), 0.0)
    weight = (weight + jnp.where(second, jax.nn.sigmoid(-lead), 0.0)).T
    high = weight.astype(jnp.bfloat16).astype(jnp.float32)
    middle = (weight - high).astype(jnp.bfloat16).astype(jnp.float32)
    terms = jnp.concatenate([weight - high - middle, middle, high], axis=0)
    out_ref[...] = terms


def shares(group, ids, logits, after):
    shape = (3 * ids.shape[1], EXPERTS * CAP)
    return pl.pallas_call(
        functools.partial(shares_kernel, group),
        in_specs=[VMEM, VMEM, ANY],
        out_specs=VMEM,
        out_shape=jax.ShapeDtypeStruct(shape, jnp.float32),
        compiler_params=LIMIT,
        name="shares",
    )(ids, logits, after)


def mix_kernel(terms_ref, act_ref, arrived, near, last, *refs):
    out_ref, kept, middle_rows = refs[-1], refs[:HALVES], refs[HALVES:-1]
    tokens = act_ref.shape[0]
    terms = terms_ref[...].astype(jnp.bfloat16)
    for k, (at, part) in enumerate(spans(act_ref.shape[1], BACK)):
        columns = slice(at, at + part)
        own = kept[k][...].astype(jnp.float32) + arrived[:, columns].astype(jnp.float32)
        blocks = [own.astype(jnp.bfloat16), near[:, columns], middle_rows[k][...]]
        rows = jnp.concatenate(blocks + [last[:, columns]], axis=0)
        sums = jnp.dot(terms, rows, preferred_element_type=jnp.float32)
        total = act_ref[:, columns].astype(jnp.float32)
        for j in range(3):
            total = total + sums[j * tokens : (j + 1) * tokens]
        out_ref[:, columns] = total.astype(jnp.bfloat16)


def mix(terms, activations, pieces):
    return pl.pallas_call(
        mix_kernel,
        out_shape=jax.ShapeDtypeStruct(activations.shape, jnp.bfloat16),
        compiler_params=LIMIT,
        name="mix",
    )(terms, activations, *pieces)


def added(mine, arrived):
    total = mine.astype(jnp.float32) + arrived.astype(jnp.float32)
    return total.astype(jnp.bfloat16)


def on_device(activations, expert_ids, route_logits, norm_gain, w_gate, w_up, w_down):
    devices = lax.axis_size("expert")
    group = devices // EXPERTS
    far = group // 2
    width = activations.shape[1]
    part = width // HALVES

    def shift(x, s):
        return lax.ppermute(
            x, "expert", [(i, (i + s * group) % devices) for i in range(devices)]
        )

    def swap(x, bit):
        return lax.ppermute(x, "expert", [(i, i ^ bit) for i in range(devices)])

    def after(x, *others):
        return lax.optimization_barrier((x, *others))[0]

    others = EXPERTS - 1
    ids = expert_ids.T
    own, *sends = pack(group, ids, activations, norm_gain)
    size = spans(width)[0][1]
    now = [fetch(w_gate, 0, size, own)]
    fetched = after(own, *now)
    far_own = swap(fetched, far)
    now.append(fetch(w_up, 0, size, fetched))
    blocks = []
    for k in range(HALVES):
        x = sends[k * others : (k + 1) * others]
        if k:
            x = relay(after(x, *now, far_own), blocks[-1])
        arrivals = [shift(x[s - 1], s) for s in ORDER]
        blocks.append(jnp.concatenate(arrivals, axis=0))
    totals = []
    for k in range(HALVES):
        at, size = spans(width)[k]
        columns = slice(at, at + size)
        far_block = swap(blocks[k], far)
        if totals:
            far_block, totals = lax.optimization_barrier((far_block, totals))
        pieces = [own[:, columns], blocks[k], far_own[:, columns], far_block]
        bit = far // 2
        while bit:
            if k and len(pieces) == EXPERTS:
                early = swap(jnp.concatenate(pieces[:-1], axis=0), bit)
                pieces += [early, swap(far_block, bit)]
            else:
                pieces.append(swap(jnp.concatenate(pieces, axis=0), bit))
            bit //= 2
        pieces[0], pieces[2] = own, far_own
        if k < HALVES - 1:
            pieces[1] = after(pieces[1], blocks[k + 1])
        later, ahead = [w_gate, w_up], (size, width - size)
        if k == HALVES - 1:
            later, ahead = [w_down], (0, AHEAD * BLOCK)
        now, totals = gate_up(k, pieces, now, later, ahead, totals)
    hidden = totals[0]
    held = []
    early = AHEAD * BLOCK
    for k, (at, size) in enumerate(spans(width, BACK)):
        if k == 0:
            rest, (keep, send) = down(hidden, now, [(at, size)], [w_down])
        else:
            segments = [(at, early - at), (0, width - early)]
            _, (keep, send) = down(hidden, [*now, *rest], segments, [])
        bit = 1
        while bit < far:
            total = added(keep, swap(send, bit))
            keep, send = total[: total.shape[0] // 2], total[total.shape[0] // 2 :]
            bit *= 2
        held.append([total[j * CAP : (j + 1) * CAP] for j in range(2 * EXPERTS)])
    place = {s: 1 + j for j, s in enumerate(ORDER)}
    crossed = [swap(h[EXPERTS + place[2]], far) for h in held]
    middle = [shift(added(h[place[2]], x), -2) for h, x in zip(held, crossed)]
    mine = [jnp.concatenate([h[j] for h in held], axis=1) for j in range(2 * EXPERTS)]
    back = {}
    back[1] = swap(after(mine[EXPERTS + place[1]], crossed[1]), far)
    back[3] = swap(after(mine[EXPERTS + place[3]], crossed[0]), far)
    back[0] = swap(after(mine[EXPERTS], back[1], back[3]), far)
    near = shift(after(added(mine[place[1]], back[1]), middle[1]), -1)
    last = shift(after(added(mine[place[3]], back[3]), middle[0]), -3)
    arrived = back[0]
    pieces = [arrived, near, last, *[h[0] for h in held], *middle]
    terms = shares(group, ids, route_logits.T, hidden)
    return mix(terms, activations, pieces)


def solution(mesh):
    in_specs = (
        P(("parts", "expert"), None),
        P(("parts", "expert"), None),
        P(("parts", "expert"), None),
        P(),
        P("expert", None),
        P("expert", None),
        P("expert", None),
    )
    out_specs = P(("parts", "expert"), None)
    return jax.shard_map(
        on_device, mesh=mesh, in_specs=in_specs, out_specs=out_specs, check_vma=False
    )
```
